256 devices in a mesh: row: 16 (over z_hi, x, core), col: 16 (over y, z_lo).
Axes of the slice: x: 4, y: 4, z: 8 (z_hi: 2, z_lo: 4; z = z_hi * 4 + z_lo), core: 2. Of those that a mesh axis runs over, the one named last changes fastest.
Arguments:
- pair: bfloat16 [576, 576, 128], P('row', 'col'), may hold values from -6 to 6
- cotangent: bfloat16 [576, 576, 128], P('row', 'col'), may hold values from -6 to 6
- gain_in: float32 [128], replicated, may hold values from 0.25 to 1.75
- bias_in: float32 [128], replicated, may hold values from -3 to 3
- w_in: bfloat16 [128, 640], replicated, may hold values from -0.5 to 0.5
- gain_out: float32 [128], replicated, may hold values from 0.25 to 1.75
- bias_out: float32 [128], replicated, may hold values from -3 to 3
- w_out: bfloat16 [128, 128], replicated, may hold values from -0.5 to 0.5
Outputs:
- update: bfloat16 [576, 576, 128], P('row', 'col')
- pair_grad: bfloat16 [576, 576, 128], P('row', 'col')
The draws below stay inside these ranges and needn't reach their ends.
All inputs are finite; a program needn't handle non-finite values.
Results may differ from the reference program's by a relative error of at most 0.023.
Values may be sent and summed in bfloat16 or wider, within the bound.
No kernel may reach another device: no remote copies, remote signals or barrier semaphores. Data moves between devices by JAX's collectives and lax.ppermute only.
A program may use at most 128 MiB of HBM per device.

```python
import jax
import jax.numpy as jnp
from jax import lax

PAIR_C = 128
INNER = 128
N = 576


def block_levels(own_key, dims, split, smallest, largest):
    level = 1.0
    for axis_at, blocks in split:
        draws = jax.random.uniform(jax.random.fold_in(jax.random.fold_in(own_key, 6), axis_at), (blocks,), jnp.float32, smallest / len(split), largest / len(split))
        level = level * jnp.repeat(jnp.exp(draws), dims[axis_at] // blocks).reshape((-1,) + (1,) * (len(dims) - 1 - axis_at))
    return level


def bell_draw(own_key, shape, width, bound, split=(), dtype=jnp.bfloat16):
    values = width * jax.random.normal(own_key, shape, jnp.float32)
    if split:
        values = values * block_levels(own_key, shape, split, -0.22, 0.18)
    return jnp.clip(values, -bound, bound).astype(dtype)


def setup_inputs(seed: int = 0) -> dict:
    splits = jax.random.split(jax.random.key(seed), 9)
    pair = bell_draw(splits[0], (N, N, PAIR_C), 1.0, 6.0, ((0, 16), (1, 16)))
    cotangent = bell_draw(splits[1], (N, N, PAIR_C), 1.0, 6.0, ((0, 16), (1, 16)))
    gain_in = jnp.clip(1.0 + 0.15 * jax.random.normal(splits[2], (PAIR_C,), jnp.float32), 0.25, 1.75)
    bias_in = bell_draw(splits[3], (PAIR_C,), 0.5, 3.0, (), jnp.float32)
    w_in = bell_draw(splits[4], (PAIR_C, 5 * INNER), PAIR_C ** -0.5, 0.5)
    gain_out = jnp.clip(1.0 + 0.15 * jax.random.normal(splits[5], (INNER,), jnp.float32), 0.25, 1.75)
    bias_out = bell_draw(splits[6], (INNER,), 0.5, 3.0, (), jnp.float32)
    w_out = bell_draw(splits[7], (INNER, PAIR_C), INNER ** -0.5, 0.5)
    return {"pair": pair, "cotangent": cotangent, "gain_in": gain_in, "bias_in": bias_in, "w_in": w_in, "gain_out": gain_out, "bias_out": bias_out, "w_out": w_out}


EPS = 1e-05

def norm_rows(values, gain, shift):
    center = values - lax.optimization_barrier(jnp.mean(values, -1, keepdims=True))
    spread = lax.optimization_barrier(jnp.mean(center * center, -1, keepdims=True))
    return center * lax.rsqrt(spread + EPS) * gain + shift

def front(pair, gain_in, bias_in, w_in):
    shape = pair.shape
    normed = norm_rows(pair.astype(jnp.float32), gain_in, bias_in).astype(jnp.bfloat16)
    proj = jnp.dot(normed.reshape(-1, shape[-1]), w_in, preferred_element_type=jnp.float32)
    inner = (w_in.shape[1] - shape[-1]) // 4
    left = jax.nn.sigmoid(proj[:, :inner]) * proj[:, inner:2 * inner]
    right = jax.nn.sigmoid(proj[:, 2 * inner:3 * inner]) * proj[:, 3 * inner:4 * inner]
    gate = jax.nn.sigmoid(proj[:, 4 * inner:])
    return (left.reshape(shape[0], shape[1], inner), right.reshape(shape[0], shape[1], inner), gate.reshape(shape[0], shape[1], shape[2]))

def back(prod, gate, gain_out, bias_out, w_out):
    shape = prod.shape
    prodn = norm_rows(prod, gain_out, bias_out).astype(jnp.bfloat16)
    mixed = jnp.dot(prodn.reshape(-1, shape[-1]), w_out, preferred_element_type=jnp.float32)
    return gate * mixed.reshape(shape[0], shape[1], w_out.shape[1])

def reference(pair, cotangent, gain_in, bias_in, w_in, gain_out, bias_out, w_out):

    def front_part(values):
        return front(values, gain_in, bias_in, w_in)
    (left_f, right_f, gate), front_vjp = jax.vjp(front_part, pair)
    left = left_f.astype(jnp.bfloat16)
    right = right_f.astype(jnp.bfloat16)
    prod = jnp.einsum('ikc,jkc->ijc', left.astype(jnp.float32), right.astype(jnp.float32))

    def back_part(values, gates):
        return back(values, gates, gain_out, bias_out, w_out)
    result, back_vjp = jax.vjp(back_part, prod, gate)
    update = result.astype(jnp.bfloat16)
    d_prod, d_gate = back_vjp(cotangent.astype(jnp.float32))
    d_prod = d_prod.astype(jnp.bfloat16).astype(jnp.float32)
    d_left = jnp.einsum('ijc,jkc->ikc', d_prod, right.astype(jnp.float32))
    d_right = jnp.einsum('ijc,ikc->jkc', d_prod, left.astype(jnp.float32))
    grad, = front_vjp((d_left, d_right, d_gate))
    return (update, grad.astype(jnp.bfloat16))
```

```python
import functools

import jax
import jax.numpy as jnp
from jax import lax
from jax.experimental import pallas as pl
from jax.experimental.pallas import tpu as pltpu
from jax.sharding import Mesh, PartitionSpec as P

EPS = 1e-05
BF = jnp.bfloat16
F32 = jnp.float32

TILE = 36
SLOT = 40
SLOTS = 3
GROUPS = 12
LANES = 128
ROWS = 16
PAIR_ROWS = 2 * GROUPS
CH = 128
NB = 8
KB = 16
KG = 6
JG = 3
NAMES = ("zh", "x", "core", "y", "zl")
WIDE = ("zh", "x", "y", "zl")


def params(mib=40):
    return pltpu.CompilerParams(vmem_limit_bytes=mib * 1024 * 1024)


def dot(a, b, ca, cb):
    return lax.dot_general(a, b, (((ca,), (cb,)), ((), ())), preferred_element_type=F32)


def used_lanes(shape):
    lane = lax.broadcasted_iota(jnp.int32, shape, len(shape) - 1)
    used = lane < TILE
    for s in range(1, SLOTS):
        used = used | ((lane >= SLOT * s) & (lane < SLOT * s + TILE))
    return used


def swap_slots(blocks):
    shape = next(b.shape for b in blocks if b is not None)
    lane = lax.broadcasted_iota(jnp.int32, shape, 1)
    out = []
    for s in range(SLOTS):
        acc = jnp.zeros(shape, F32)
        for q, b in enumerate(blocks):
            if b is None:
                continue
            shift = (SLOT * (q - s)) % LANES
            moved = pltpu.roll(b, shift, 1) if shift else b
            acc = jnp.where((lane >= SLOT * q) & (lane < SLOT * (q + 1)), moved, acc)
        out.append(acc)
    return out


def spread_tile(tile_ref, scr):
    scr[...] = jnp.zeros(scr.shape, F32)
    for r in range(GROUPS):
        for s in range(SLOTS):
            scr[r, SLOT * s : SLOT * s + TILE, :] = tile_ref[r + GROUPS * s].astype(F32)


def gather_tile(value, tile_ref, r):
    for s in range(SLOTS):
        tile_ref[r + GROUPS * s] = value[SLOT * s : SLOT * s + TILE].astype(BF)


def input_norm(x):
    center = x - jnp.mean(x, -1, keepdims=True)
    scale = lax.rsqrt(jnp.mean(center * center, -1, keepdims=True) + EPS)
    return center * scale, scale


def edges_kernel(pair_ref, gain_ref, bias_ref, w_ref, out_ref, x_scr, o_scr, wt_scr):
    spread_tile(pair_ref, x_scr)
    wt_scr[...] = w_ref[:, : 4 * CH].astype(F32).T.astype(BF)
    used = used_lanes((CH, LANES))
    for r in range(GROUPS):
        xhat, _ = input_norm(x_scr[r])
        normed = (xhat * gain_ref[...] + bias_ref[...]).astype(BF)
        proj = dot(wt_scr[...], normed, 1, 1)
        left = jax.nn.sigmoid(proj[:CH]) * proj[CH : 2 * CH]
        right = jax.nn.sigmoid(proj[2 * CH : 3 * CH]) * proj[3 * CH :]
        o_scr[pl.ds(r, CH, stride=PAIR_ROWS), :] = jnp.where(used, left, 0.0)
        o_scr[pl.ds(GROUPS + r, CH, stride=PAIR_ROWS), :] = jnp.where(used, right, 0.0)
    out_ref[...] = o_scr[...].astype(BF).reshape(CH, PAIR_ROWS, LANES)


def edges(pair, gain_in, bias_in, w_in):
    return pl.pallas_call(
        edges_kernel,
        out_shape=jax.ShapeDtypeStruct((CH, PAIR_ROWS, LANES), BF),
        scratch_shapes=[
            pltpu.VMEM((GROUPS, LANES, CH), F32),
            pltpu.VMEM((CH * PAIR_ROWS, LANES), F32),
            pltpu.VMEM((4 * CH, CH), BF),
        ],
        compiler_params=params(),
        cost_estimate=pl.CostEstimate(flops=200_000_000, bytes_accessed=1_200_000, transcendentals=400_000),
        name="edges",
    )(pair, gain_in, bias_in, w_in)


def side_kernel(
    pair_ref, cot_ref, gain_ref, bias_ref, w_ref, gain_out_ref, w_out_ref,
    gate_ref, slope_ref, dx_ref, fac_ref, xhat_ref, scale_ref,
    x_scr, c_scr, wt_scr,
):
    spread_tile(pair_ref, x_scr)
    spread_tile(cot_ref, c_scr)
    wt_scr[...] = w_ref[:, : 4 * CH].astype(F32).T.astype(BF)
    for r in range(GROUPS):
        xhat, scale = input_norm(x_scr[r])
        normed = (xhat * gain_ref[...] + bias_ref[...]).astype(BF)
        xhat_ref[r] = xhat
        scale_ref[:, r : r + 1] = scale
        proj = dot(wt_scr[...], normed, 1, 1)
        for h in range(2):
            sig = jax.nn.sigmoid(proj[2 * h * CH : (2 * h + 1) * CH])
            value = proj[(2 * h + 1) * CH : (2 * h + 2) * CH]
            fac_ref[r, 2 * h * CH : (2 * h + 1) * CH, :] = (value * sig * (1.0 - sig)).astype(BF)
            fac_ref[r, (2 * h + 1) * CH : (2 * h + 2) * CH, :] = sig.astype(BF)
        gate = jax.nn.sigmoid(dot(normed, w_ref[:, 4 * CH :], 1, 0))
        gated = c_scr[r] * gate
        gate_ref[r] = gate
        slope_ref[r] = gated * (1.0 - gate)
        dx_ref[r] = dot(w_out_ref[...], gated.astype(BF), 1, 1) * gain_out_ref[...]


def side(pair, cotangent, gain_in, bias_in, w_in, gain_out, w_out):
    square = jax.ShapeDtypeStruct((GROUPS, LANES, CH), F32)
    return pl.pallas_call(
        side_kernel,
        out_shape=[
            square,
            square,
            square,
            jax.ShapeDtypeStruct((GROUPS, 4 * CH, LANES), BF),
            square,
            jax.ShapeDtypeStruct((LANES, LANES), F32),
        ],
        scratch_shapes=[
            pltpu.VMEM((GROUPS, LANES, CH), F32),
            pltpu.VMEM((GROUPS, LANES, CH), F32),
            pltpu.VMEM((4 * CH, CH), BF),
        ],
        compiler_params=params(),
        cost_estimate=pl.CostEstimate(flops=300_000_000, bytes_accessed=6_000_000, transcendentals=600_000),
        name="side",
    )(pair, cotangent, gain_in, bias_in, w_in, gain_out, w_out)


def assemble_kernel(in_ref, left_ref, right_ref, t_scr, r_scr):
    r_scr[...] = jnp.zeros(r_scr.shape, F32)
    rows = NB * PAIR_ROWS
    for g in range(KG):
        blocks = [
            in_ref[:, SLOTS * g + q].astype(F32).reshape(rows, LANES) if SLOTS * g + q < KB else None
            for q in range(SLOTS)
        ]
        lanes = slice(LANES * g, LANES * (g + 1))
        for s, value in enumerate(swap_slots(blocks)):
            t_scr[...] = value
            for b in range(NB):
                at = PAIR_ROWS * b
                to = CH * s + ROWS * b
                left_ref[to : to + ROWS, lanes] = t_scr[at : at + ROWS].astype(BF)
                to = LANES * (b // SLOTS) + SLOT * (b % SLOTS) + GROUPS * s
                r_scr[to : to + GROUPS, lanes] = t_scr[at + GROUPS : at + PAIR_ROWS]
    right_ref[...] = r_scr[...].astype(BF)


def assemble(received):
    return pl.pallas_call(
        assemble_kernel,
        out_shape=[
            jax.ShapeDtypeStruct((SLOTS * NB * ROWS, KG * LANES), BF),
            jax.ShapeDtypeStruct((JG * LANES, KG * LANES), BF),
        ],
        scratch_shapes=[
            pltpu.VMEM((NB * PAIR_ROWS, LANES), F32),
            pltpu.VMEM((JG * LANES, KG * LANES), F32),
        ],
        compiler_params=params(),
        cost_estimate=pl.CostEstimate(flops=2_000_000, bytes_accessed=2_000_000, transcendentals=0),
        name="assemble",
    )(received.reshape(NB, KB, PAIR_ROWS, LANES))


def products_kernel(core_ref, left_ref, own_ref, other_ref, out_ref):
    core = core_ref[0]
    for t, right_ref in enumerate((own_ref, other_ref)):
        parity = core if t == 0 else 1 - core
        for g in range(JG):
            prod = dot(left_ref[...], right_ref[LANES * g : LANES * (g + 1), :], 1, 1)
            blocks = [prod[CH * s : CH * (s + 1)] for s in range(SLOTS)]
            for q, value in enumerate(swap_slots(blocks)):
                b = SLOTS * g + q
                if b < NB:
                    out_ref[:, 2 * b + parity] = value.astype(BF).reshape(NB, ROWS, LANES)


def products(core, left, own, other):
    return pl.pallas_call(
        products_kernel,
        out_shape=jax.ShapeDtypeStruct((NB, KB, ROWS, LANES), BF),
        in_specs=[pl.BlockSpec(memory_space=pltpu.SMEM)] + [pl.BlockSpec(memory_space=pltpu.VMEM)] * 3,
        compiler_params=params(),
        cost_estimate=pl.CostEstimate(flops=450_000_000, bytes_accessed=2_300_000, transcendentals=0),
        name="products",
    )(core, left, own, other).reshape(CH, ROWS, LANES)


def middle_kernel(
    prod_ref, gate_ref, slope_ref, dx_ref, gain_ref, bias_ref, w_ref,
    update_ref, out_ref, dgate_ref, p_scr, o_scr,
):
    p_scr[...] = prod_ref[...].astype(F32).reshape(CH * ROWS, LANES)
    used = used_lanes((CH, LANES))
    for r in range(GROUPS):
        prod = p_scr[pl.ds(r, CH, stride=ROWS), :]
        center = prod - jnp.mean(prod, 0, keepdims=True)
        scale = lax.rsqrt(jnp.mean(center * center, 0, keepdims=True) + EPS)
        xhat = center * scale
        prodn = (xhat * gain_ref[...] + bias_ref[...]).astype(BF)
        mixed = dot(prodn, w_ref[...], 0, 0)
        gather_tile(gate_ref[r] * mixed, update_ref, r)
        dgate_ref[r] = (slope_ref[r] * mixed).astype(BF)
        dx = dx_ref[r]
        d_prod = scale * (dx - jnp.mean(dx, 0, keepdims=True) - xhat * jnp.mean(dx * xhat, 0, keepdims=True))
        o_scr[pl.ds(r, CH, stride=ROWS), :] = jnp.where(used, d_prod, 0.0)
    for r in range(GROUPS, ROWS):
        o_scr[pl.ds(r, CH, stride=ROWS), :] = jnp.zeros((CH, LANES), F32)
    out_ref[...] = o_scr[...].astype(BF).reshape(CH, ROWS, LANES)


def middle(prod, gate, slope, dx, gain_out, bias_out, w_out):
    return pl.pallas_call(
        middle_kernel,
        out_shape=[
            jax.ShapeDtypeStruct((TILE, TILE, CH), BF),
            jax.ShapeDtypeStruct((CH, ROWS, LANES), BF),
            jax.ShapeDtypeStruct((GROUPS, LANES, CH), BF),
        ],
        scratch_shapes=[
            pltpu.VMEM((CH * ROWS, LANES), F32),
            pltpu.VMEM((CH * ROWS, LANES), F32),
        ],
        compiler_params=params(),
        cost_estimate=pl.CostEstimate(flops=50_000_000, bytes_accessed=4_000_000, transcendentals=10_000),
        name="middle",
    )(prod, gate, slope, dx, gain_out, bias_out, w_out)


def d_left_kernel(core_ref, in_ref, own_ref, other_ref, keep_ref, send_ref, out_ref):
    core = core_ref[0]
    for t, to_ref in enumerate((keep_ref, send_ref)):
        parity = core if t == 0 else 1 - core
        for g in range(JG):
            blocks = [
                in_ref[:, 2 * (SLOTS * g + q) + parity].astype(F32).reshape(CH, LANES) if SLOTS * g + q < NB else None
                for q in range(SLOTS)
            ]
            for s, value in enumerate(swap_slots(blocks)):
                to_ref[CH * s : CH * (s + 1), LANES * g : LANES * (g + 1)] = value.astype(BF)
    for g in range(KG):
        lanes = slice(LANES * g, LANES * (g + 1))
        d_left = dot(keep_ref[...], own_ref[:, lanes], 1, 0) + dot(send_ref[...], other_ref[:, lanes], 1, 0)
        for q, value in enumerate(swap_slots([d_left[CH * s : CH * (s + 1)] for s in range(SLOTS)])):
            k = SLOTS * g + q
            if k < KB:
                out_ref[:, k] = value.astype(BF).reshape(NB, ROWS, LANES)


def left_grad(core, received, own, other):
    half = jax.ShapeDtypeStruct((SLOTS * NB * ROWS, JG * LANES), BF)
    return pl.pallas_call(
        d_left_kernel,
        out_shape=[half, half, jax.ShapeDtypeStruct((NB, KB, ROWS, LANES), BF)],
        in_specs=[pl.BlockSpec(memory_space=pltpu.SMEM)] + [pl.BlockSpec(memory_space=pltpu.VMEM)] * 3,
        compiler_params=params(),
        cost_estimate=pl.CostEstimate(flops=450_000_000, bytes_accessed=2_800_000, transcendentals=0),
        name="left_grad",
    )(core, received.reshape(NB, KB, ROWS, LANES), own, other)


def d_right_kernel(keep_ref, other_ref, left_ref, left_other_ref, d_left_ref, out_ref, d_scr, o_scr):
    d_scr[: JG * LANES] = dot(keep_ref[...], left_ref[...], 0, 0) + dot(other_ref[...], left_other_ref[...], 0, 0)
    o_scr[:, :, :ROWS, :] = d_left_ref[...].astype(F32)
    for g in range(KG):
        lanes = slice(LANES * g, LANES * (g + 1))
        for b in range(NB):
            at = LANES * (b // SLOTS) + SLOT * (b % SLOTS)
            blocks = [d_scr[at + GROUPS * s : at + GROUPS * (s + 1), lanes] for s in range(SLOTS)]
            for q, value in enumerate(swap_slots(blocks)):
                k = SLOTS * g + q
                if k < KB:
                    o_scr[b, k, GROUPS:PAIR_ROWS, :] = value
    out_ref[...] = o_scr[...].astype(BF)


def right_grad(keep, other, left, left_other, d_left):
    return pl.pallas_call(
        d_right_kernel,
        out_shape=jax.ShapeDtypeStruct((NB, KB, PAIR_ROWS, LANES), BF),
        scratch_shapes=[
            pltpu.VMEM((JG * LANES, KG * LANES), F32),
            pltpu.VMEM((NB, KB, PAIR_ROWS, LANES), F32),
        ],
        compiler_params=params(),
        cost_estimate=pl.CostEstimate(flops=450_000_000, bytes_accessed=3_500_000, transcendentals=0),
        name="right_grad",
    )(keep, other, left, left_other, d_left).reshape(CH, PAIR_ROWS, LANES)


def finish_kernel(d_ref, fac_ref, dgate_ref, xhat_ref, scale_ref, gain_ref, w_ref, out_ref, d_scr, wt_scr):
    d_scr[...] = d_ref[...].astype(F32).reshape(CH * PAIR_ROWS, LANES)
    wt_scr[...] = w_ref[...].astype(F32).T.astype(BF)
    for r in range(GROUPS):
        d_left = d_scr[pl.ds(r, CH, stride=PAIR_ROWS), :]
        d_right = d_scr[pl.ds(GROUPS + r, CH, stride=PAIR_ROWS), :]
        parts = [
            (d * fac_ref[r, CH * f : CH * (f + 1), :].astype(F32)).astype(BF)
            for f, d in enumerate((d_left, d_left, d_right, d_right))
        ]
        d_proj = jnp.concatenate(parts, 0)
        d_normed = dot(d_proj, wt_scr[: 4 * CH], 0, 0) + dot(dgate_ref[r], wt_scr[4 * CH :], 1, 0)
        dx = d_normed.astype(BF).astype(F32) * gain_ref[...]
        xhat = xhat_ref[r]
        grad = scale_ref[:, r : r + 1] * (
            dx - jnp.mean(dx, -1, keepdims=True) - xhat * jnp.mean(dx * xhat, -1, keepdims=True)
        )
        gather_tile(grad, out_ref, r)


def finish(d_edges, fac, dgate, xhat, scale, gain_in, w_in):
    return pl.pallas_call(
        finish_kernel,
        out_shape=jax.ShapeDtypeStruct((TILE, TILE, CH), BF),
        scratch_shapes=[
            pltpu.VMEM((CH * PAIR_ROWS, LANES), F32),
            pltpu.VMEM((5 * CH, CH), BF),
        ],
        compiler_params=params(),
        cost_estimate=pl.CostEstimate(flops=250_000_000, bytes_accessed=4_000_000, transcendentals=0),
        name="finish",
    )(d_edges, fac, dgate, xhat, scale, gain_in, w_in)


def exchange(x):
    return lax.all_to_all(x, WIDE, 0, 0, tiled=True)


def other_core(x):
    return lax.ppermute(x, "core", [(0, 1), (1, 0)])


def shards(pair, cotangent, gain_in, bias_in, w_in, gain_out, bias_out, w_out):
    gain_row, bias_row = gain_in.reshape(1, CH), bias_in.reshape(1, CH)
    gain_col, bias_col = gain_out.reshape(CH, 1), bias_out.reshape(CH, 1)
    core = lax.axis_index("core").astype(jnp.int32).reshape(1)
    received = exchange(edges(pair, gain_row, bias_row, w_in))
    gate, slope, dx, fac, xhat, scale = side(pair, cotangent, gain_row, bias_row, w_in, gain_col, w_out)
    left, right = assemble(received)
    right_other = other_core(right)
    left_other = other_core(left)
    prod = exchange(products(core, left, right, right_other))
    update, d_prod, dgate = middle(prod, gate, slope, dx, gain_col, bias_col, w_out)
    keep, send, d_left = left_grad(core, exchange(d_prod), right, right_other)
    d_edges = exchange(right_grad(keep, other_core(send), left, left_other, d_left))
    grad = finish(d_edges, fac, dgate, xhat, scale, gain_row, w_in)
    return update, grad


def solution(mesh):
    split = Mesh(mesh.devices.reshape(2, 4, 2, 4, 4), NAMES)
    tile = P(("zh", "x", "core"), ("y", "zl"), None)
    return jax.shard_map(
        shards,
        mesh=split,
        in_specs=(tile, tile, P(), P(), P(), P(), P(), P()),
        out_specs=(tile, tile),
        check_vma=False,
    )
```

```python
import jax
import jax.numpy as jnp
from jax import lax
from jax.experimental import pallas as pl
from jax.experimental.pallas import tpu as pltpu
from jax.sharding import Mesh, PartitionSpec as P

EPS = 1e-05
BF = jnp.bfloat16
F32 = jnp.float32

TILE = 36
SLOT = 40
SLOTS = 3
GROUPS = 12
LANES = 128
ROWS = 16
PART = 4
PARTS = GROUPS // PART
PAIR_ROWS = 2 * GROUPS
CH = 128
NB = 8
KB = 16
KG = 6
JG = 3
NAMES = ("zh", "x", "core", "y", "zl")
WIDE = ("zh", "x", "y", "zl")


def params(mib=14):
    return pltpu.CompilerParams(vmem_limit_bytes=mib * 1024 * 1024)


def dot(a, b, ca, cb):
    return lax.dot_general(a, b, (((ca,), (cb,)), ((), ())), preferred_element_type=F32)


def used_lanes(shape):
    lane = lax.broadcasted_iota(jnp.int32, shape, len(shape) - 1)
    used = lane < TILE
    for s in range(1, SLOTS):
        used = used | ((lane >= SLOT * s) & (lane < SLOT * s + TILE))
    return used


def swap_slots(blocks):
    shape = next(b.shape for b in blocks if b is not None)
    lane = lax.broadcasted_iota(jnp.int32, shape, 1)
    out = []
    for s in range(SLOTS):
        acc = jnp.zeros(shape, F32)
        for q, b in enumerate(blocks):
            if b is None:
                continue
            shift = (SLOT * (q - s)) % LANES
            moved = pltpu.roll(b, shift, 1) if shift else b
            acc = jnp.where((lane >= SLOT * q) & (lane < SLOT * (q + 1)), moved, acc)
        out.append(acc)
    return out


def spread_tile(tile_ref, scr):
    for r in range(GROUPS):
        for s in range(SLOTS):
            scr[r, SLOT * s : SLOT * s + TILE, :] = tile_ref[r + GROUPS * s].astype(F32)


def gather_tile(value, tile_ref, r):
    for s in range(SLOTS):
        tile_ref[r + GROUPS * s] = value[SLOT * s : SLOT * s + TILE].astype(BF)


def normalized(x, axis):
    center = x - jnp.mean(x, axis, keepdims=True)
    scale = lax.rsqrt(jnp.mean(center * center, axis, keepdims=True) + EPS)
    return center * scale, scale


def norm_grad(d, xhat, scale, axis):
    return scale * (d - jnp.mean(d, axis, keepdims=True) - xhat * jnp.mean(d * xhat, axis, keepdims=True))


def column(row):
    return jnp.broadcast_to(row, (8, CH)).T[:, :1]


def fetch(sources, buffers, sems):
    copies = [pltpu.make_async_copy(s, b, sems.at[n]) for n, (s, b) in enumerate(zip(sources, buffers))]
    for copy in copies:
        copy.start()
    return copies


def in_hbm(n):
    return [pl.BlockSpec(memory_space=pltpu.HBM)] * n


def keep_in_hbm(*arrays):
    return [pltpu.with_memory_space_constraint(a, pltpu.HBM) for a in arrays]


def edges_kernel(
    pair_hbm, w_hbm, gain_hbm, bias_hbm, out_ref,
    pair_ref, w_ref, gain_ref, bias_ref, x_scr, o_scr, wt_scr, sems,
):
    copies = fetch(
        (pair_hbm, w_hbm, gain_hbm, bias_hbm), (pair_ref, w_ref, gain_ref, bias_ref), sems
    )
    x_scr[...] = jnp.zeros(x_scr.shape, F32)
    used = used_lanes((CH, LANES))
    copies[1].wait()
    wt_scr[...] = w_ref[:, : 4 * CH].astype(F32).T.astype(BF)
    copies[2].wait()
    copies[3].wait()
    copies[0].wait()
    spread_tile(pair_ref, x_scr)
    for r in range(GROUPS):
        xhat, _ = normalized(x_scr[r], 1)
        normed = (xhat * gain_ref[...] + bias_ref[...]).astype(BF)
        proj = dot(wt_scr[...], normed, 1, 1)
        left = jax.nn.sigmoid(proj[:CH]) * proj[CH : 2 * CH]
        right = jax.nn.sigmoid(proj[2 * CH : 3 * CH]) * proj[3 * CH :]
        o_scr[pl.ds(r, CH, stride=PAIR_ROWS), :] = jnp.where(used, left, 0.0)
        o_scr[pl.ds(GROUPS + r, CH, stride=PAIR_ROWS), :] = jnp.where(used, right, 0.0)
    out_ref[...] = o_scr[...].astype(BF).reshape(CH, PAIR_ROWS, LANES)


def edges(pair, w_in, gain_in, bias_in):
    return pl.pallas_call(
        edges_kernel,
        out_shape=jax.ShapeDtypeStruct((CH, PAIR_ROWS, LANES), BF),
        in_specs=in_hbm(4),
        scratch_shapes=[
            pltpu.VMEM((TILE, TILE, CH), BF),
            pltpu.VMEM((CH, 5 * CH), BF),
            pltpu.VMEM((1, CH), F32),
            pltpu.VMEM((1, CH), F32),
            pltpu.VMEM((GROUPS, LANES, CH), F32),
            pltpu.VMEM((CH * PAIR_ROWS, LANES), F32),
            pltpu.VMEM((4 * CH, CH), BF),
            pltpu.SemaphoreType.DMA((4,)),
        ],
        compiler_params=params(),
        cost_estimate=pl.CostEstimate(flops=200_000_000, bytes_accessed=1_200_000, transcendentals=400_000),
        name="edges",
    )(*keep_in_hbm(pair, w_in, gain_in, bias_in))


def side_kernel(
    pair_hbm, cot_hbm, w_hbm, w_out_hbm, gain_hbm, bias_hbm, gain_out_hbm, bias_out_hbm,
    gate_ref, slope_ref, dx_ref, fac_ref, xhat_ref, scale_ref, cols_ref, w_ref, w_out_t_ref,
    pair_ref, cot_ref, w_out_ref, rows_ref, x_scr, c_scr, wt_scr, sems,
):
    copies = fetch(
        (pair_hbm, cot_hbm, w_hbm, w_out_hbm, gain_hbm, bias_hbm, gain_out_hbm, bias_out_hbm),
        (pair_ref, cot_ref, w_ref, w_out_ref) + tuple(rows_ref.at[n] for n in range(4)),
        sems,
    )
    x_scr[...] = jnp.zeros(x_scr.shape, F32)
    c_scr[...] = jnp.zeros(c_scr.shape, F32)
    scale_ref[...] = jnp.zeros(scale_ref.shape, F32)
    cols_ref[...] = jnp.zeros(cols_ref.shape, F32)
    for copy in copies:
        copy.wait()
    wt_scr[...] = w_ref[...].astype(F32).T.astype(BF)
    w_out_t_ref[...] = w_out_ref[...].astype(F32).T.astype(BF)
    gain_in, bias_in, gain_out, bias_out = (column(rows_ref[n]) for n in range(4))
    cols_ref[:, 0:1] = gain_in
    cols_ref[:, 1:2] = gain_out
    cols_ref[:, 2:3] = bias_out
    spread_tile(pair_ref, x_scr)
    spread_tile(cot_ref, c_scr)
    for r in range(GROUPS):
        xhat, scale = normalized(x_scr[r].T, 0)
        normed = (xhat * gain_in + bias_in).astype(BF)
        xhat_ref[r] = xhat
        scale_ref[r : r + 1, :] = scale
        proj = dot(wt_scr[...], normed, 1, 0)
        for h in range(2):
            sig = jax.nn.sigmoid(proj[2 * h * CH : (2 * h + 1) * CH])
            value = proj[(2 * h + 1) * CH : (2 * h + 2) * CH]
            fac_ref[r, 2 * h * CH : (2 * h + 1) * CH, :] = (value * sig * (1.0 - sig)).astype(BF)
            fac_ref[r, (2 * h + 1) * CH : (2 * h + 2) * CH, :] = sig.astype(BF)
        gate = jax.nn.sigmoid(proj[4 * CH :])
        gated = c_scr[r].T * gate
        gate_ref[r] = gate
        slope_ref[r] = gated * (1.0 - gate)
        dx_ref[r] = dot(w_out_ref[...], gated.astype(BF), 1, 0) * gain_out


def side(pair, cotangent, w_in, w_out, gain_in, bias_in, gain_out, bias_out):
    square = jax.ShapeDtypeStruct((GROUPS, CH, LANES), F32)
    return pl.pallas_call(
        side_kernel,
        out_shape=[
            square,
            square,
            square,
            jax.ShapeDtypeStruct((GROUPS, 4 * CH, LANES), BF),
            square,
            jax.ShapeDtypeStruct((ROWS, LANES), F32),
            jax.ShapeDtypeStruct((CH, LANES), F32),
            jax.ShapeDtypeStruct((CH, 5 * CH), BF),
            jax.ShapeDtypeStruct((CH, CH), BF),
        ],
        in_specs=in_hbm(8),
        scratch_shapes=[
            pltpu.VMEM((TILE, TILE, CH), BF),
            pltpu.VMEM((TILE, TILE, CH), BF),
            pltpu.VMEM((CH, CH), BF),
            pltpu.VMEM((4, 1, CH), F32),
            pltpu.VMEM((GROUPS, LANES, CH), F32),
            pltpu.VMEM((GROUPS, LANES, CH), F32),
            pltpu.VMEM((5 * CH, CH), BF),
            pltpu.SemaphoreType.DMA((8,)),
        ],
        compiler_params=params(),
        cost_estimate=pl.CostEstimate(flops=300_000_000, bytes_accessed=6_000_000, transcendentals=600_000),
        name="side",
    )(*keep_in_hbm(pair, cotangent, w_in, w_out, gain_in, bias_in, gain_out, bias_out))


def assemble_kernel(in_ref, left_ref, right_ref, t_scr, r_scr):
    r_scr[...] = jnp.zeros(r_scr.shape, F32)
    rows = NB * PAIR_ROWS
    for g in range(KG):
        blocks = [
            in_ref[:, SLOTS * g + q].astype(F32).reshape(rows, LANES) if SLOTS * g + q < KB else None
            for q in range(SLOTS)
        ]
        lanes = slice(LANES * g, LANES * (g + 1))
        for s, value in enumerate(swap_slots(blocks)):
            t_scr[...] = value
            for b in range(NB):
                at = PAIR_ROWS * b
                to = CH * s + ROWS * b
                left_ref[to : to + ROWS, lanes] = t_scr[at : at + ROWS].astype(BF)
                to = LANES * (b // SLOTS) + SLOT * (b % SLOTS) + GROUPS * s
                r_scr[to : to + GROUPS, lanes] = t_scr[at + GROUPS : at + PAIR_ROWS]
    right_ref[...] = r_scr[...].astype(BF)


def assemble(received):
    return pl.pallas_call(
        assemble_kernel,
        out_shape=[
            jax.ShapeDtypeStruct((SLOTS * NB * ROWS, KG * LANES), BF),
            jax.ShapeDtypeStruct((JG * LANES, KG * LANES), BF),
        ],
        scratch_shapes=[
            pltpu.VMEM((NB * PAIR_ROWS, LANES), F32),
            pltpu.VMEM((JG * LANES, KG * LANES), F32),
        ],
        compiler_params=params(),
        cost_estimate=pl.CostEstimate(flops=2_000_000, bytes_accessed=2_000_000, transcendentals=0),
        name="assemble",
    )(received.reshape(NB, KB, PAIR_ROWS, LANES))


def products_kernel(core_ref, left_ref, own_ref, other_ref, out_ref, t_scr):
    core = core_ref[0]
    for t, right_ref in enumerate((own_ref, other_ref)):
        parity = core if t == 0 else 1 - core
        for g in range(JG):
            prod = dot(left_ref[...], right_ref[LANES * g : LANES * (g + 1), :], 1, 1)
            blocks = [prod[CH * s : CH * (s + 1)] for s in range(SLOTS)]
            for q, value in enumerate(swap_slots(blocks)):
                b = SLOTS * g + q
                if b < NB:
                    t_scr[...] = value.reshape(NB, ROWS, LANES)
                    for p in range(PARTS):
                        part = t_scr[:, PART * p : PART * (p + 1), :].astype(BF)
                        out_ref[:, 2 * b + parity, :, LANES * p : LANES * (p + 1)] = part


def products(core, left, own, other):
    return pl.pallas_call(
        products_kernel,
        out_shape=jax.ShapeDtypeStruct((NB, KB, PART, PARTS * LANES), BF),
        in_specs=[pl.BlockSpec(memory_space=pltpu.SMEM)] + [pl.BlockSpec(memory_space=pltpu.VMEM)] * 3,
        scratch_shapes=[pltpu.VMEM((NB, ROWS, LANES), F32)],
        compiler_params=params(),
        cost_estimate=pl.CostEstimate(flops=450_000_000, bytes_accessed=2_300_000, transcendentals=0),
        name="products",
    )(core, left, own, other).reshape(CH, PART, PARTS * LANES)


def middle_kernel(
    prod_ref, gate_ref, slope_ref, dx_ref, cols_ref, w_ref,
    update_ref, out_ref, dgate_ref, p_scr, o_scr,
):
    for p in range(PARTS):
        p_scr[p, :, :PART, :] = prod_ref[:, :, LANES * p : LANES * (p + 1)].astype(F32)
    prods = p_scr.reshape(PARTS * CH * 8, LANES)
    d_prods = o_scr.reshape(PARTS * CH * 8, LANES)
    used = used_lanes((CH, LANES))
    gain, bias = cols_ref[:, 1:2], cols_ref[:, 2:3]
    for r in range(GROUPS):
        xhat, scale = normalized(prods[pl.ds(r // PART * CH * 8 + r % PART, CH, stride=8), :], 0)
        prodn = (xhat * gain + bias).astype(BF)
        mixed = dot(w_ref[...], prodn, 1, 0)
        gather_tile((gate_ref[r] * mixed).T, update_ref, r)
        dgate_ref[r] = (slope_ref[r] * mixed).astype(BF)
        d_prod = norm_grad(dx_ref[r], xhat, scale, 0)
        d_prods[pl.ds(r // PART * CH * 8 + r % PART, CH, stride=8), :] = jnp.where(used, d_prod, 0.0)
    for p in range(PARTS):
        out_ref[:, :, LANES * p : LANES * (p + 1)] = o_scr[p, :, :PART, :].astype(BF)


def middle(prod, gate, slope, dx, cols, w_out_t):
    return pl.pallas_call(
        middle_kernel,
        out_shape=[
            jax.ShapeDtypeStruct((TILE, TILE, CH), BF),
            jax.ShapeDtypeStruct((CH, PART, PARTS * LANES), BF),
            jax.ShapeDtypeStruct((GROUPS, CH, LANES), BF),
        ],
        scratch_shapes=[pltpu.VMEM((PARTS, CH, 8, LANES), F32)] * 2,
        compiler_params=params(),
        cost_estimate=pl.CostEstimate(flops=50_000_000, bytes_accessed=4_000_000, transcendentals=10_000),
        name="middle",
    )(prod, gate, slope, dx, cols, w_out_t)


def d_left_kernel(core_ref, in_ref, own_ref, other_ref, keep_ref, send_ref, out_ref, t_scr):
    core = core_ref[0]
    t_scr[:, :, GROUPS:, :] = jnp.zeros((NB, KB, ROWS - GROUPS, LANES), F32)
    for p in range(PARTS):
        t_scr[:, :, PART * p : PART * (p + 1), :] = in_ref[:, :, :, LANES * p : LANES * (p + 1)].astype(F32)
    for t, to_ref in enumerate((keep_ref, send_ref)):
        parity = core if t == 0 else 1 - core
        for g in range(JG):
            blocks = [
                t_scr[:, 2 * (SLOTS * g + q) + parity].reshape(CH, LANES) if SLOTS * g + q < NB else None
                for q in range(SLOTS)
            ]
            for s, value in enumerate(swap_slots(blocks)):
                to_ref[CH * s : CH * (s + 1), LANES * g : LANES * (g + 1)] = value.astype(BF)
    for g in range(KG):
        lanes = slice(LANES * g, LANES * (g + 1))
        d_left = dot(keep_ref[...], own_ref[:, lanes], 1, 0) + dot(send_ref[...], other_ref[:, lanes], 1, 0)
        for q, value in enumerate(swap_slots([d_left[CH * s : CH * (s + 1)] for s in range(SLOTS)])):
            k = SLOTS * g + q
            if k < KB:
                out_ref[:, k] = value.astype(BF).reshape(NB, ROWS, LANES)


def left_grad(core, received, own, other):
    half = jax.ShapeDtypeStruct((SLOTS * NB * ROWS, JG * LANES), BF)
    return pl.pallas_call(
        d_left_kernel,
        out_shape=[half, half, jax.ShapeDtypeStruct((NB, KB, ROWS, LANES), BF)],
        in_specs=[pl.BlockSpec(memory_space=pltpu.SMEM)] + [pl.BlockSpec(memory_space=pltpu.VMEM)] * 3,
        scratch_shapes=[pltpu.VMEM((NB, KB, ROWS, LANES), F32)],
        compiler_params=params(),
        cost_estimate=pl.CostEstimate(flops=450_000_000, bytes_accessed=2_800_000, transcendentals=0),
        name="left_grad",
    )(core, received.reshape(NB, KB, PART, PARTS * LANES), own, other)


def d_right_kernel(keep_ref, other_ref, left_ref, left_other_ref, d_left_ref, out_ref, d_scr, o_scr):
    d_scr[: JG * LANES] = dot(keep_ref[...], left_ref[...], 0, 0) + dot(other_ref[...], left_other_ref[...], 0, 0)
    o_scr[:, :, :ROWS, :] = d_left_ref[...].astype(F32)
    for g in range(KG):
        lanes = slice(LANES * g, LANES * (g + 1))
        for b in range(NB):
            at = LANES * (b // SLOTS) + SLOT * (b % SLOTS)
            blocks = [d_scr[at + GROUPS * s : at + GROUPS * (s + 1), lanes] for s in range(SLOTS)]
            for q, value in enumerate(swap_slots(blocks)):
                k = SLOTS * g + q
                if k < KB:
                    o_scr[b, k, GROUPS:PAIR_ROWS, :] = value
    out_ref[...] = o_scr[...].astype(BF)


def right_grad(keep, other, left, left_other, d_left):
    return pl.pallas_call(
        d_right_kernel,
        out_shape=jax.ShapeDtypeStruct((NB, KB, PAIR_ROWS, LANES), BF),
        scratch_shapes=[
            pltpu.VMEM((JG * LANES, KG * LANES), F32),
            pltpu.VMEM((NB, KB, PAIR_ROWS, LANES), F32),
        ],
        compiler_params=params(),
        cost_estimate=pl.CostEstimate(flops=450_000_000, bytes_accessed=3_500_000, transcendentals=0),
        name="right_grad",
    )(keep, other, left, left_other, d_left).reshape(CH, PAIR_ROWS, LANES)


def finish_kernel(d_ref, fac_ref, dgate_ref, xhat_ref, scale_ref, cols_ref, w_ref, out_ref, d_scr):
    d_scr[...] = d_ref[...].astype(F32).reshape(CH * PAIR_ROWS, LANES)
    gain = cols_ref[:, 0:1]
    for r in range(GROUPS):
        d_left = d_scr[pl.ds(r, CH, stride=PAIR_ROWS), :]
        d_right = d_scr[pl.ds(GROUPS + r, CH, stride=PAIR_ROWS), :]
        parts = [
            (d * fac_ref[r, CH * f : CH * (f + 1), :].astype(F32)).astype(BF)
            for f, d in enumerate((d_left, d_left, d_right, d_right))
        ]
        d_proj = jnp.concatenate(parts + [dgate_ref[r]], 0)
        d_normed = dot(w_ref[...], d_proj, 1, 0).astype(BF).astype(F32)
        gather_tile(norm_grad(d_normed * gain, xhat_ref[r], scale_ref[r : r + 1, :], 0).T, out_ref, r)


def finish(d_edges, fac, dgate, xhat, scale, cols, w_in):
    return pl.pallas_call(
        finish_kernel,
        out_shape=jax.ShapeDtypeStruct((TILE, TILE, CH), BF),
        scratch_shapes=[pltpu.VMEM((CH * PAIR_ROWS, LANES), F32)],
        compiler_params=params(),
        cost_estimate=pl.CostEstimate(flops=250_000_000, bytes_accessed=4_000_000, transcendentals=0),
        name="finish",
    )(d_edges, fac, dgate, xhat, scale, cols, w_in)


def exchange(x):
    return lax.all_to_all(x, WIDE, 0, 0, tiled=True)


def other_core(x):
    return lax.ppermute(x, "core", [(0, 1), (1, 0)])


def shards(pair, cotangent, gain_in, bias_in, w_in, gain_out, bias_out, w_out):
    gain_in, bias_in = gain_in.reshape(1, CH), bias_in.reshape(1, CH)
    gain_out, bias_out = gain_out.reshape(1, CH), bias_out.reshape(1, CH)
    core = lax.axis_index("core").astype(jnp.int32).reshape(1)
    received = exchange(edges(pair, w_in, gain_in, bias_in))
    ready = side(pair, cotangent, w_in, w_out, gain_in, bias_in, gain_out, bias_out)
    received, ready = lax.optimization_barrier((received, ready))
    gate, slope, dx, fac, xhat, scale, cols, w_in, w_out_t = ready
    left, right = assemble(received)
    right_other = other_core(right)
    left_other = other_core(left)
    prod = products(core, left, right, right_other)
    prod, left_other = lax.optimization_barrier((prod, left_other))
    update, d_prod, dgate = middle(exchange(prod), gate, slope, dx, cols, w_out_t)
    keep, send, d_left = left_grad(core, exchange(d_prod), right, right_other)
    d_edges = exchange(right_grad(keep, other_core(send), left, left_other, d_left))
    grad = finish(d_edges, fac, dgate, xhat, scale, cols, w_in)
    return update, grad


def solution(mesh):
    split = Mesh(mesh.devices.reshape(2, 4, 2, 4, 4), NAMES)
    tile = P(("zh", "x", "core"), ("y", "zl"), None)
    return jax.shard_map(
        shards,
        mesh=split,
        in_specs=(tile, tile, P(), P(), P(), P(), P(), P()),
        out_specs=(tile, tile),
        check_vma=False,
    )
```

```python
import jax
import jax.numpy as jnp
from jax import lax
from jax.experimental import pallas as pl
from jax.experimental.pallas import tpu as pltpu
from jax.sharding import Mesh, PartitionSpec as P

EPS = 1e-05
BF = jnp.bfloat16
F32 = jnp.float32

TILE = 36
SLOT = 40
SLOTS = 3
GROUPS = 12
LANES = 128
ROWS = 16
PART = 4
PARTS = GROUPS // PART
CH = 128
NB = 8
KB = 16
KG = 6
JG = 3
CHUNKS = 4
NAMES = ("zh", "x", "core", "y", "zl")
WIDE = ("zh", "x", "y", "zl")


def params(mib=14):
    return pltpu.CompilerParams(vmem_limit_bytes=mib * 1024 * 1024)


def dot(a, b, ca, cb):
    return lax.dot_general(a, b, (((ca,), (cb,)), ((), ())), preferred_element_type=F32)


def used_lanes(shape):
    lane = lax.broadcasted_iota(jnp.int32, shape, len(shape) - 1)
    used = lane < TILE
    for s in range(1, SLOTS):
        used = used | ((lane >= SLOT * s) & (lane < SLOT * s + TILE))
    return used


def swap_slots(blocks):
    shape = next(b.shape for b in blocks if b is not None)
    lane = lax.broadcasted_iota(jnp.int32, shape, 1)
    out = []
    for s in range(SLOTS):
        acc = jnp.zeros(shape, F32)
        for q, b in enumerate(blocks):
            if b is None:
                continue
            shift = (SLOT * (q - s)) % LANES
            moved = pltpu.roll(b, shift, 1) if shift else b
            acc = jnp.where((lane >= SLOT * q) & (lane < SLOT * (q + 1)), moved, acc)
        out.append(acc)
    return out


def spread_tile(tile_ref, scr):
    for r in range(GROUPS):
        for s in range(SLOTS):
            scr[r, SLOT * s : SLOT * s + TILE, :] = tile_ref[r + GROUPS * s].astype(F32)


def gather_tile(value, tile_ref, r):
    for s in range(SLOTS):
        tile_ref[r + GROUPS * s] = value[SLOT * s : SLOT * s + TILE].astype(BF)


def send_tile(tile_ref, tile_hbm, r, sems):
    if r % PART < PART - 1:
        return []
    copies = []
    for s in range(SLOTS):
        rows = pl.ds(r + 1 - PART + GROUPS * s, PART)
        copies.append(pltpu.make_async_copy(tile_ref.at[rows], tile_hbm.at[rows], sems.at[r // PART * SLOTS + s]))
        copies[-1].start()
    return copies


def normalized(x, axis):
    center = x - jnp.mean(x, axis, keepdims=True)
    scale = lax.rsqrt(jnp.mean(center * center, axis, keepdims=True) + EPS)
    return center * scale, scale


def norm_grad(d, xhat, scale, axis):
    return scale * (d - jnp.mean(d, axis, keepdims=True) - xhat * jnp.mean(d * xhat, axis, keepdims=True))


def message(leading, arrays=1):
    return jax.ShapeDtypeStruct(leading + (PART, arrays * PARTS * LANES), BF)


def part_lanes(p):
    return slice(LANES * p, LANES * (p + 1))


def row_at(r):
    return pl.ds(r // PART * CH * 8 + r % PART, CH, stride=8)


def by_row(scr):
    return scr.reshape(PARTS * CH * 8, LANES)


PADDED = pltpu.VMEM((PARTS, CH, 8, LANES), F32)


def pack(out_ref, scr, array=0, rows=slice(None)):
    for p in range(PARTS):
        out_ref[rows, :, part_lanes(array * PARTS + p)] = scr[p, rows, :PART, :].astype(BF)


def unpack(in_ref, scr, array=0):
    for p in range(PARTS):
        scr[p, :, :PART, :] = in_ref[:, :, part_lanes(array * PARTS + p)].astype(F32)


def read_rows(in_ref, scr, array=0):
    scr[:, :, GROUPS:, :] = jnp.zeros((NB, KB, ROWS - GROUPS, LANES), scr.dtype)
    for p in range(PARTS):
        scr[:, :, PART * p : PART * (p + 1), :] = in_ref[:, :, :, part_lanes(array * PARTS + p)].astype(scr.dtype)


def write_rows(out_ref, at, value, scr):
    scr[...] = value.astype(scr.dtype).reshape(NB, ROWS, LANES)
    for p in range(PARTS):
        out_ref[:, at, :, part_lanes(p)] = scr[:, PART * p : PART * (p + 1), :].astype(BF)


def column(row):
    return jnp.broadcast_to(row, (8, CH)).T[:, :1]


def fetch(sources, buffers, sems):
    copies = [pltpu.make_async_copy(s, b, sems.at[n]) for n, (s, b) in enumerate(zip(sources, buffers))]
    for copy in copies:
        copy.start()
    return copies


def in_hbm(n):
    return [pl.BlockSpec(memory_space=pltpu.HBM)] * n


def keep_in_hbm(*arrays):
    return [pltpu.with_memory_space_constraint(a, pltpu.HBM) for a in arrays]


def edges_kernel(
    pair_hbm, w_hbm, gain_hbm, bias_hbm, out_hbm,
    pair_ref, w_ref, gain_ref, bias_ref, x_scr, l_scr, r_scr, wt_scr, out_ref, sems, out_sems,
):
    copies = fetch(
        (pair_hbm, w_hbm, gain_hbm, bias_hbm), (pair_ref, w_ref, gain_ref, bias_ref), sems
    )
    x_scr[...] = jnp.zeros(x_scr.shape, F32)
    used = used_lanes((CH, LANES))
    copies[1].wait()
    wt_scr[...] = w_ref[:, : 4 * CH].astype(F32).T.astype(BF)
    copies[2].wait()
    copies[3].wait()
    copies[0].wait()
    spread_tile(pair_ref, x_scr)
    for r in range(GROUPS):
        xhat, _ = normalized(x_scr[r], 1)
        normed = (xhat * gain_ref[...] + bias_ref[...]).astype(BF)
        proj = dot(wt_scr[...], normed, 1, 1)
        left = jax.nn.sigmoid(proj[:CH]) * proj[CH : 2 * CH]
        right = jax.nn.sigmoid(proj[2 * CH : 3 * CH]) * proj[3 * CH :]
        by_row(l_scr)[row_at(r), :] = jnp.where(used, left, 0.0)
        by_row(r_scr)[row_at(r), :] = jnp.where(used, right, 0.0)
    copies = []
    for n in range(CHUNKS):
        rows = slice(CH // CHUNKS * n, CH // CHUNKS * (n + 1))
        pack(out_ref, l_scr, 0, rows)
        pack(out_ref, r_scr, 1, rows)
        copies.append(pltpu.make_async_copy(out_ref.at[rows], out_hbm.at[rows], out_sems.at[n]))
        copies[-1].start()
    for copy in copies:
        copy.wait()


def edges(pair, w_in, gain_in, bias_in):
    return pl.pallas_call(
        edges_kernel,
        out_shape=message((CH,), 2),
        in_specs=in_hbm(4),
        out_specs=pl.BlockSpec(memory_space=pltpu.HBM),
        scratch_shapes=[
            pltpu.VMEM((TILE, TILE, CH), BF),
            pltpu.VMEM((CH, 5 * CH), BF),
            pltpu.VMEM((1, CH), F32),
            pltpu.VMEM((1, CH), F32),
            pltpu.VMEM((GROUPS, LANES, CH), F32),
            PADDED,
            PADDED,
            pltpu.VMEM((4 * CH, CH), BF),
            pltpu.VMEM((CH, PART, 2 * PARTS * LANES), BF),
            pltpu.SemaphoreType.DMA((4,)),
            pltpu.SemaphoreType.DMA((CHUNKS,)),
        ],
        compiler_params=params(),
        cost_estimate=pl.CostEstimate(flops=200_000_000, bytes_accessed=1_200_000, transcendentals=400_000),
        name="edges",
    )(*keep_in_hbm(pair, w_in, gain_in, bias_in))


def side_kernel(
    pair_hbm, cot_hbm, w_hbm, w_out_hbm, gain_hbm, bias_hbm, gain_out_hbm, bias_out_hbm,
    gate_ref, slope_ref, dx_ref, fac_ref, xhat_ref, scale_ref, cols_ref, w_ref, w_out_t_ref,
    pair_ref, cot_ref, w_out_ref, rows_ref, x_scr, c_scr, wt_scr, sems,
):
    copies = fetch(
        (pair_hbm, cot_hbm, w_hbm, w_out_hbm, gain_hbm, bias_hbm, gain_out_hbm, bias_out_hbm),
        (pair_ref, cot_ref, w_ref, w_out_ref) + tuple(rows_ref.at[n] for n in range(4)),
        sems,
    )
    x_scr[...] = jnp.zeros(x_scr.shape, F32)
    c_scr[...] = jnp.zeros(c_scr.shape, F32)
    scale_ref[...] = jnp.zeros(scale_ref.shape, F32)
    cols_ref[...] = jnp.zeros(cols_ref.shape, F32)
    for copy in copies:
        copy.wait()
    wt_scr[...] = w_ref[...].astype(F32).T.astype(BF)
    w_out_t_ref[...] = w_out_ref[...].astype(F32).T.astype(BF)
    gain_in, bias_in, gain_out, bias_out = (column(rows_ref[n]) for n in range(4))
    cols_ref[:, 0:1] = gain_in
    cols_ref[:, 1:2] = gain_out
    cols_ref[:, 2:3] = bias_out
    spread_tile(pair_ref, x_scr)
    spread_tile(cot_ref, c_scr)
    for r in range(GROUPS):
        xhat, scale = normalized(x_scr[r].T, 0)
        normed = (xhat * gain_in + bias_in).astype(BF)
        xhat_ref[r] = xhat
        scale_ref[r : r + 1, :] = scale
        proj = dot(wt_scr[...], normed, 1, 0)
        for h in range(2):
            sig = jax.nn.sigmoid(proj[2 * h * CH : (2 * h + 1) * CH])
            value = proj[(2 * h + 1) * CH : (2 * h + 2) * CH]
            fac_ref[r, 2 * h * CH : (2 * h + 1) * CH, :] = (value * sig * (1.0 - sig)).astype(BF)
            fac_ref[r, (2 * h + 1) * CH : (2 * h + 2) * CH, :] = sig.astype(BF)
        gate = jax.nn.sigmoid(proj[4 * CH :])
        gated = c_scr[r].T * gate
        gate_ref[r] = gate
        slope_ref[r] = gated * (1.0 - gate)
        dx_ref[r] = dot(w_out_ref[...], gated.astype(BF), 1, 0) * gain_out


def side(pair, cotangent, w_in, w_out, gain_in, bias_in, gain_out, bias_out):
    square = jax.ShapeDtypeStruct((GROUPS, CH, LANES), F32)
    return pl.pallas_call(
        side_kernel,
        out_shape=[
            square,
            square,
            square,
            jax.ShapeDtypeStruct((GROUPS, 4 * CH, LANES), BF),
            square,
            jax.ShapeDtypeStruct((ROWS, LANES), F32),
            jax.ShapeDtypeStruct((CH, LANES), F32),
            jax.ShapeDtypeStruct((CH, 5 * CH), BF),
            jax.ShapeDtypeStruct((CH, CH), BF),
        ],
        in_specs=in_hbm(8),
        scratch_shapes=[
            pltpu.VMEM((TILE, TILE, CH), BF),
            pltpu.VMEM((TILE, TILE, CH), BF),
            pltpu.VMEM((CH, CH), BF),
            pltpu.VMEM((4, 1, CH), F32),
            pltpu.VMEM((GROUPS, LANES, CH), F32),
            pltpu.VMEM((GROUPS, LANES, CH), F32),
            pltpu.VMEM((5 * CH, CH), BF),
            pltpu.SemaphoreType.DMA((8,)),
        ],
        compiler_params=params(),
        cost_estimate=pl.CostEstimate(flops=300_000_000, bytes_accessed=6_000_000, transcendentals=600_000),
        name="side",
    )(*keep_in_hbm(pair, cotangent, w_in, w_out, gain_in, bias_in, gain_out, bias_out))


def assemble_left_kernel(in_ref, left_ref, t_scr):
    read_rows(in_ref, t_scr)
    for g in range(KG):
        blocks = [
            t_scr[:, SLOTS * g + q].astype(F32).reshape(CH, LANES) if SLOTS * g + q < KB else None
            for q in range(SLOTS)
        ]
        for s, value in enumerate(swap_slots(blocks)):
            left_ref[CH * s : CH * (s + 1), part_lanes(g)] = value.astype(BF)


def assemble_left(received):
    return pl.pallas_call(
        assemble_left_kernel,
        out_shape=jax.ShapeDtypeStruct((SLOTS * NB * ROWS, KG * LANES), BF),
        scratch_shapes=[pltpu.VMEM((NB, KB, ROWS, LANES), BF)],
        compiler_params=params(),
        cost_estimate=pl.CostEstimate(flops=2_000_000, bytes_accessed=1_000_000, transcendentals=0),
        name="assemble_left",
    )(received.reshape(NB, KB, PART, 2 * PARTS * LANES))


def assemble_right_kernel(in_ref, right_ref, t_scr, v_scr, r_scr):
    read_rows(in_ref, t_scr, 1)
    r_scr[...] = jnp.zeros(r_scr.shape, F32)
    for g in range(KG):
        blocks = [
            t_scr[:, SLOTS * g + q].astype(F32).reshape(CH, LANES) if SLOTS * g + q < KB else None
            for q in range(SLOTS)
        ]
        for s, value in enumerate(swap_slots(blocks)):
            v_scr[s] = value
            for b in range(NB):
                to = LANES * (b // SLOTS) + SLOT * (b % SLOTS) + GROUPS * s
                r_scr[to : to + GROUPS, part_lanes(g)] = v_scr[s, ROWS * b : ROWS * b + GROUPS]
    right_ref[...] = r_scr[...].astype(BF)


def assemble_right(received):
    return pl.pallas_call(
        assemble_right_kernel,
        out_shape=jax.ShapeDtypeStruct((JG * LANES, KG * LANES), BF),
        scratch_shapes=[
            pltpu.VMEM((NB, KB, ROWS, LANES), BF),
            pltpu.VMEM((SLOTS, CH, LANES), F32),
            pltpu.VMEM((JG * LANES, KG * LANES), F32),
        ],
        compiler_params=params(),
        cost_estimate=pl.CostEstimate(flops=2_000_000, bytes_accessed=1_000_000, transcendentals=0),
        name="assemble_right",
    )(received.reshape(NB, KB, PART, 2 * PARTS * LANES))


def product_messages(left_ref, right_ref, out_ref, place, t_scr):
    for g in range(JG):
        prod = dot(left_ref[...], right_ref[part_lanes(g), :], 1, 1)
        blocks = [prod[CH * s : CH * (s + 1)] for s in range(SLOTS)]
        for q, value in enumerate(swap_slots(blocks)):
            b = SLOTS * g + q
            if b < NB:
                write_rows(out_ref, place(b), value, t_scr)


def products_own_kernel(left_ref, right_ref, out_ref, t_scr):
    product_messages(left_ref, right_ref, out_ref, lambda b: b, t_scr)


def products_own(left, right):
    return pl.pallas_call(
        products_own_kernel,
        out_shape=message((NB, NB)),
        scratch_shapes=[pltpu.VMEM((NB, ROWS, LANES), BF)],
        compiler_params=params(),
        cost_estimate=pl.CostEstimate(flops=230_000_000, bytes_accessed=1_400_000, transcendentals=0),
        name="products_own",
    )(left, right)


def products_kernel(core_ref, left_ref, right_ref, own_ref, out_ref, t_scr):
    core = core_ref[0]
    for b in range(NB):
        out_ref[:, 2 * b + core] = own_ref[:, b]
    product_messages(left_ref, right_ref, out_ref, lambda b: 2 * b + 1 - core, t_scr)


def products(core, left, other, own):
    return pl.pallas_call(
        products_kernel,
        out_shape=message((NB, KB)),
        in_specs=[pl.BlockSpec(memory_space=pltpu.SMEM)] + [pl.BlockSpec(memory_space=pltpu.VMEM)] * 3,
        scratch_shapes=[pltpu.VMEM((NB, ROWS, LANES), BF)],
        compiler_params=params(),
        cost_estimate=pl.CostEstimate(flops=230_000_000, bytes_accessed=1_600_000, transcendentals=0),
        name="products",
    )(core, left, other, own).reshape(CH, PART, PARTS * LANES)


def middle_kernel(
    prod_ref, gate_ref, slope_ref, dx_ref, cols_ref, w_ref,
    update_hbm, out_ref, dgate_ref, p_scr, o_scr, update_ref, sems,
):
    copies = []
    unpack(prod_ref, p_scr)
    used = used_lanes((CH, LANES))
    gain, bias = cols_ref[:, 1:2], cols_ref[:, 2:3]
    for r in range(GROUPS):
        xhat, scale = normalized(by_row(p_scr)[row_at(r), :], 0)
        prodn = (xhat * gain + bias).astype(BF)
        mixed = dot(w_ref[...], prodn, 1, 0)
        gather_tile((gate_ref[r] * mixed).T, update_ref, r)
        copies += send_tile(update_ref, update_hbm, r, sems)
        dgate_ref[r] = (slope_ref[r] * mixed).astype(BF)
        d_prod = norm_grad(dx_ref[r], xhat, scale, 0)
        by_row(o_scr)[row_at(r), :] = jnp.where(used, d_prod, 0.0)
    pack(out_ref, o_scr)
    for copy in copies:
        copy.wait()


def middle(prod, gate, slope, dx, cols, w_out_t):
    return pl.pallas_call(
        middle_kernel,
        out_shape=[
            jax.ShapeDtypeStruct((TILE, TILE, CH), BF),
            message((CH,)),
            jax.ShapeDtypeStruct((GROUPS, CH, LANES), BF),
        ],
        out_specs=[pl.BlockSpec(memory_space=pltpu.HBM)] + [pl.BlockSpec(memory_space=pltpu.VMEM)] * 2,
        scratch_shapes=[
            PADDED,
            PADDED,
            pltpu.VMEM((TILE, TILE, CH), BF),
            pltpu.SemaphoreType.DMA((TILE // PART,)),
        ],
        compiler_params=params(),
        cost_estimate=pl.CostEstimate(flops=50_000_000, bytes_accessed=4_000_000, transcendentals=10_000),
        name="middle",
    )(prod, gate, slope, dx, cols, w_out_t)


def regroup_kernel(core_ref, in_ref, keep_ref, send_ref, t_scr):
    core = core_ref[0]
    read_rows(in_ref, t_scr)
    for t, to_ref in enumerate((send_ref, keep_ref)):
        parity = 1 - core if t == 0 else core
        for g in range(JG):
            blocks = [
                t_scr[:, 2 * (SLOTS * g + q) + parity].astype(F32).reshape(CH, LANES) if SLOTS * g + q < NB else None
                for q in range(SLOTS)
            ]
            for s, value in enumerate(swap_slots(blocks)):
                to_ref[CH * s : CH * (s + 1), part_lanes(g)] = value.astype(BF)


def regroup(core, received):
    half = jax.ShapeDtypeStruct((SLOTS * NB * ROWS, JG * LANES), BF)
    return pl.pallas_call(
        regroup_kernel,
        out_shape=[half, half],
        in_specs=[pl.BlockSpec(memory_space=pltpu.SMEM), pl.BlockSpec(memory_space=pltpu.VMEM)],
        scratch_shapes=[pltpu.VMEM((NB, KB, ROWS, LANES), BF)],
        compiler_params=params(),
        cost_estimate=pl.CostEstimate(flops=2_000_000, bytes_accessed=1_000_000, transcendentals=0),
        name="regroup",
    )(core, received.reshape(NB, KB, PART, PARTS * LANES))


def left_grad_kernel(keep_ref, send_ref, own_ref, other_ref, left_hbm, out_ref, left_ref, t_scr, sem):
    copy = pltpu.make_async_copy(left_hbm, left_ref, sem)
    copy.start()
    for g in range(KG):
        lanes = part_lanes(g)
        d_left = dot(keep_ref[...], own_ref[:, lanes], 1, 0) + dot(send_ref[...], other_ref[:, lanes], 1, 0)
        for q, value in enumerate(swap_slots([d_left[CH * s : CH * (s + 1)] for s in range(SLOTS)])):
            if SLOTS * g + q < KB:
                write_rows(out_ref, SLOTS * g + q, value, t_scr)
    copy.wait()


def left_grad(keep, send, own, other, left_other):
    return pl.pallas_call(
        left_grad_kernel,
        out_shape=[message((NB, KB)), jax.ShapeDtypeStruct((SLOTS * NB * ROWS, KG * LANES), BF)],
        in_specs=[pl.BlockSpec(memory_space=pltpu.VMEM)] * 4 + in_hbm(1),
        scratch_shapes=[pltpu.VMEM((NB, ROWS, LANES), BF), pltpu.SemaphoreType.DMA],
        compiler_params=params(),
        cost_estimate=pl.CostEstimate(flops=450_000_000, bytes_accessed=2_200_000, transcendentals=0),
        name="left_grad",
    )(keep, send, own, other, *keep_in_hbm(left_other))


def right_grad_kernel(keep_ref, other_ref, left_ref, left_other_ref, d_left_ref, out_ref, d_scr, o_scr):
    out_ref[:, :, :, : PARTS * LANES] = d_left_ref[...]
    d_scr[...] = dot(keep_ref[...], left_ref[...], 0, 0) + dot(other_ref[...], left_other_ref[...], 0, 0)
    for g in range(KG):
        for b in range(NB):
            at = LANES * (b // SLOTS) + SLOT * (b % SLOTS)
            blocks = [d_scr[at + GROUPS * s : at + GROUPS * s + ROWS, part_lanes(g)] for s in range(SLOTS)]
            for q, value in enumerate(swap_slots(blocks)):
                if SLOTS * g + q < KB:
                    o_scr[b, SLOTS * g + q] = value.astype(o_scr.dtype)
    for p in range(PARTS):
        out_ref[:, :, :, part_lanes(PARTS + p)] = o_scr[:, :, PART * p : PART * (p + 1), :].astype(BF)


def right_grad(keep, other, left, left_other, d_left):
    return pl.pallas_call(
        right_grad_kernel,
        out_shape=message((NB, KB), 2),
        scratch_shapes=[
            pltpu.VMEM((JG * LANES, KG * LANES), F32),
            pltpu.VMEM((NB, KB, ROWS, LANES), BF),
        ],
        compiler_params=params(),
        cost_estimate=pl.CostEstimate(flops=450_000_000, bytes_accessed=2_500_000, transcendentals=0),
        name="right_grad",
    )(keep, other, left, left_other, d_left).reshape(CH, PART, 2 * PARTS * LANES)


def finish_kernel(
    d_ref, fac_ref, dgate_ref, xhat_ref, scale_ref, cols_ref, w_ref, out_hbm, l_scr, r_scr, out_ref, sems
):
    copies = []
    unpack(d_ref, l_scr, 0)
    unpack(d_ref, r_scr, 1)
    gain = cols_ref[:, 0:1]
    for r in range(GROUPS):
        d_left = by_row(l_scr)[row_at(r), :]
        d_right = by_row(r_scr)[row_at(r), :]
        parts = [
            (d * fac_ref[r, CH * f : CH * (f + 1), :].astype(F32)).astype(BF)
            for f, d in enumerate((d_left, d_left, d_right, d_right))
        ]
        d_proj = jnp.concatenate(parts + [dgate_ref[r]], 0)
        d_normed = dot(w_ref[...], d_proj, 1, 0).astype(BF).astype(F32)
        gather_tile(norm_grad(d_normed * gain, xhat_ref[r], scale_ref[r : r + 1, :], 0).T, out_ref, r)
        copies += send_tile(out_ref, out_hbm, r, sems)
    for copy in copies:
        copy.wait()


def finish(d_edges, fac, dgate, xhat, scale, cols, w_in):
    return pl.pallas_call(
        finish_kernel,
        out_shape=jax.ShapeDtypeStruct((TILE, TILE, CH), BF),
        out_specs=pl.BlockSpec(memory_space=pltpu.HBM),
        scratch_shapes=[
            PADDED,
            PADDED,
            pltpu.VMEM((TILE, TILE, CH), BF),
            pltpu.SemaphoreType.DMA((TILE // PART,)),
        ],
        compiler_params=params(),
        cost_estimate=pl.CostEstimate(flops=250_000_000, bytes_accessed=4_000_000, transcendentals=0),
        name="finish",
    )(d_edges, fac, dgate, xhat, scale, cols, w_in)


def exchange(x):
    return lax.all_to_all(x, WIDE, 0, 0, tiled=True)


def other_core(x):
    return lax.ppermute(x, "core", [(0, 1), (1, 0)])


def shards(pair, cotangent, gain_in, bias_in, w_in, gain_out, bias_out, w_out):
    gain_in, bias_in = gain_in.reshape(1, CH), bias_in.reshape(1, CH)
    gain_out, bias_out = gain_out.reshape(1, CH), bias_out.reshape(1, CH)
    core = lax.axis_index("core").astype(jnp.int32).reshape(1)
    received = exchange(edges(pair, w_in, gain_in, bias_in))
    ready = side(pair, cotangent, w_in, w_out, gain_in, bias_in, gain_out, bias_out)
    received, ready = lax.optimization_barrier((received, ready))
    gate, slope, dx, fac, xhat, scale, cols, w_in, w_out_t = ready
    right = assemble_right(received)
    right_other = other_core(right)
    left = assemble_left(received)
    left_other = other_core(left)
    prod = products(core, left, right_other, products_own(left, right))
    prod, left_other = lax.optimization_barrier((prod, left_other))
    update, d_prod, dgate = middle(exchange(prod), gate, slope, dx, cols, w_out_t)
    keep, send = regroup(core, exchange(d_prod))
    sent = other_core(send)
    d_left, left_other = left_grad(keep, send, right, right_other, left_other)
    d_edges = exchange(right_grad(keep, sent, left, left_other, d_left))
    grad = finish(d_edges, fac, dgate, xhat, scale, cols, w_in)
    return update, grad


def solution(mesh):
    split = Mesh(mesh.devices.reshape(2, 4, 2, 4, 4), NAMES)
    tile = P(("zh", "x", "core"), ("y", "zl"), None)
    return jax.shard_map(
        shards,
        mesh=split,
        in_specs=(tile, tile, P(), P(), P(), P(), P(), P()),
        out_specs=(tile, tile),
        check_vma=False,
    )
```

```python
import jax
import jax.numpy as jnp
from jax import lax
from jax.experimental import pallas as pl
from jax.experimental.pallas import tpu as pltpu
from jax.sharding import Mesh, PartitionSpec as P

EPS = 1e-05
BF = jnp.bfloat16
F32 = jnp.float32

TILE = 36
SLOT = 40
SLOTS = 3
GROUPS = 12
LANES = 128
ROWS = 16
PART = 4
PARTS = GROUPS // PART
CH = 128
NB = 8
KB = 16
KG = 6
JG = 3
CHUNKS = 4
NAMES = ("zh", "x", "core", "y", "zl")
WIDE = ("zh", "x", "y", "zl")


def params(mib=14):
    return pltpu.CompilerParams(vmem_limit_bytes=mib * 1024 * 1024)


def dot(a, b, ca, cb):
    return lax.dot_general(a, b, (((ca,), (cb,)), ((), ())), preferred_element_type=F32)


def used_lanes(shape):
    lane = lax.broadcasted_iota(jnp.int32, shape, len(shape) - 1)
    used = lane < TILE
    for s in range(1, SLOTS):
        used = used | ((lane >= SLOT * s) & (lane < SLOT * s + TILE))
    return used


def swap_slots(blocks):
    shape = next(b.shape for b in blocks if b is not None)
    lane = lax.broadcasted_iota(jnp.int32, shape, 1)
    out = []
    for s in range(SLOTS):
        acc = jnp.zeros(shape, F32)
        for q, b in enumerate(blocks):
            if b is None:
                continue
            shift = (SLOT * (q - s)) % LANES
            moved = pltpu.roll(b, shift, 1) if shift else b
            acc = jnp.where((lane >= SLOT * q) & (lane < SLOT * (q + 1)), moved, acc)
        out.append(acc)
    return out


def spread_tile(tile_ref, scr):
    for r in range(GROUPS):
        for s in range(SLOTS):
            scr[r, SLOT * s : SLOT * s + TILE, :] = tile_ref[r + GROUPS * s].astype(F32)


def gather_tile(value, tile_ref, r):
    for s in range(SLOTS):
        tile_ref[r + GROUPS * s] = value[SLOT * s : SLOT * s + TILE].astype(BF)


def send_tile(tile_ref, tile_hbm, r, sems):
    if r % PART < PART - 1:
        return []
    copies = []
    for s in range(SLOTS):
        rows = pl.ds(r + 1 - PART + GROUPS * s, PART)
        copies.append(pltpu.make_async_copy(tile_ref.at[rows], tile_hbm.at[rows], sems.at[r // PART * SLOTS + s]))
        copies[-1].start()
    return copies


def normalized(x, axis):
    center = x - jnp.mean(x, axis, keepdims=True)
    scale = lax.rsqrt(jnp.mean(center * center, axis, keepdims=True) + EPS)
    return center * scale, scale


def norm_grad(d, xhat, scale, axis):
    return scale * (d - jnp.mean(d, axis, keepdims=True) - xhat * jnp.mean(d * xhat, axis, keepdims=True))


def message(leading, arrays=1):
    return jax.ShapeDtypeStruct(leading + (PART, arrays * PARTS * LANES), BF)


def part_lanes(p):
    return slice(LANES * p, LANES * (p + 1))


def row_at(r):
    return pl.ds(r // PART * CH * 8 + r % PART, CH, stride=8)


def by_row(scr):
    return scr.reshape(PARTS * CH * 8, LANES)


PADDED = pltpu.VMEM((PARTS, CH, 8, LANES), F32)


def pack(out_ref, scr, array=0, rows=slice(None)):
    for p in range(PARTS):
        out_ref[rows, :, part_lanes(array * PARTS + p)] = scr[p, rows, :PART, :].astype(BF)


def unpack(in_ref, scr, array=0):
    for p in range(PARTS):
        scr[p, :, :PART, :] = in_ref[:, :, part_lanes(array * PARTS + p)].astype(F32)


def read_rows(in_ref, scr, array=0):
    scr[:, :, GROUPS:, :] = jnp.zeros((NB, KB, ROWS - GROUPS, LANES), scr.dtype)
    for p in range(PARTS):
        scr[:, :, PART * p : PART * (p + 1), :] = in_ref[:, :, :, part_lanes(array * PARTS + p)].astype(scr.dtype)


def write_rows(out_ref, at, value, scr):
    scr[...] = value.astype(scr.dtype).reshape(NB, ROWS, LANES)
    for p in range(PARTS):
        out_ref[:, at, :, part_lanes(p)] = scr[:, PART * p : PART * (p + 1), :].astype(BF)


def column(row):
    return jnp.broadcast_to(row, (8, CH)).T[:, :1]


def fetch(sources, buffers, sems):
    copies = [pltpu.make_async_copy(s, b, sems.at[n]) for n, (s, b) in enumerate(zip(sources, buffers))]
    for copy in copies:
        copy.start()
    return copies


def in_hbm(n):
    return [pl.BlockSpec(memory_space=pltpu.HBM)] * n


def keep_in_hbm(*arrays):
    return [pltpu.with_memory_space_constraint(a, pltpu.HBM) for a in arrays]


def edges_kernel(
    pair_hbm, w_hbm, gain_hbm, bias_hbm, out_hbm,
    pair_ref, w_ref, gain_ref, bias_ref, x_scr, l_scr, r_scr, wt_scr, out_ref, sems, out_sems,
):
    copies = fetch(
        (pair_hbm, w_hbm, gain_hbm, bias_hbm), (pair_ref, w_ref, gain_ref, bias_ref), sems
    )
    x_scr[...] = jnp.zeros(x_scr.shape, F32)
    used = used_lanes((CH, LANES))
    copies[1].wait()
    wt_scr[...] = w_ref[:, : 4 * CH].astype(F32).T.astype(BF)
    copies[2].wait()
    copies[3].wait()
    copies[0].wait()
    spread_tile(pair_ref, x_scr)
    for r in range(0, GROUPS, 2):
        xhat, _ = normalized(x_scr[r : r + 2].reshape(2 * LANES, CH), 1)
        normed = (xhat * gain_ref[...] + bias_ref[...]).astype(BF)
        proj = dot(wt_scr[...], normed, 1, 1)
        left = jax.nn.sigmoid(proj[:CH]) * proj[CH : 2 * CH]
        right = jax.nn.sigmoid(proj[2 * CH : 3 * CH]) * proj[3 * CH :]
        for n in (r, r + 1):
            by_row(l_scr)[row_at(n), :] = jnp.where(used, left[:, part_lanes(n - r)], 0.0)
            by_row(r_scr)[row_at(n), :] = jnp.where(used, right[:, part_lanes(n - r)], 0.0)
    copies = []
    for n in range(CHUNKS):
        rows = slice(CH // CHUNKS * n, CH // CHUNKS * (n + 1))
        pack(out_ref, l_scr, 0, rows)
        pack(out_ref, r_scr, 1, rows)
        copies.append(pltpu.make_async_copy(out_ref.at[rows], out_hbm.at[rows], out_sems.at[n]))
        copies[-1].start()
    for copy in copies:
        copy.wait()


def edges(pair, w_in, gain_in, bias_in):
    return pl.pallas_call(
        edges_kernel,
        out_shape=message((CH,), 2),
        in_specs=in_hbm(4),
        out_specs=pl.BlockSpec(memory_space=pltpu.HBM),
        scratch_shapes=[
            pltpu.VMEM((TILE, TILE, CH), BF),
            pltpu.VMEM((CH, 5 * CH), BF),
            pltpu.VMEM((1, CH), F32),
            pltpu.VMEM((1, CH), F32),
            pltpu.VMEM((GROUPS, LANES, CH), F32),
            PADDED,
            PADDED,
            pltpu.VMEM((4 * CH, CH), BF),
            pltpu.VMEM((CH, PART, 2 * PARTS * LANES), BF),
            pltpu.SemaphoreType.DMA((4,)),
            pltpu.SemaphoreType.DMA((CHUNKS,)),
        ],
        compiler_params=params(),
        cost_estimate=pl.CostEstimate(flops=200_000_000, bytes_accessed=1_200_000, transcendentals=400_000),
        name="edges",
    )(*keep_in_hbm(pair, w_in, gain_in, bias_in))


def side_kernel(
    pair_hbm, cot_hbm, w_hbm, w_out_hbm, gain_hbm, bias_hbm, gain_out_hbm, bias_out_hbm,
    gate_ref, slope_ref, dx_ref, fac_ref, xhat_ref, scale_ref, cols_ref, w_ref, w_out_t_ref,
    pair_ref, cot_ref, w_out_ref, rows_ref, x_scr, c_scr, wt_scr, sems,
):
    copies = fetch(
        (pair_hbm, cot_hbm, w_hbm, w_out_hbm, gain_hbm, bias_hbm, gain_out_hbm, bias_out_hbm),
        (pair_ref, cot_ref, w_ref, w_out_ref) + tuple(rows_ref.at[n] for n in range(4)),
        sems,
    )
    x_scr[...] = jnp.zeros(x_scr.shape, F32)
    c_scr[...] = jnp.zeros(c_scr.shape, F32)
    scale_ref[...] = jnp.zeros(scale_ref.shape, F32)
    cols_ref[...] = jnp.zeros(cols_ref.shape, F32)
    for copy in copies:
        copy.wait()
    wt_scr[...] = w_ref[...].astype(F32).T.astype(BF)
    w_out_t_ref[...] = w_out_ref[...].astype(F32).T.astype(BF)
    gain_in, bias_in, gain_out, bias_out = (column(rows_ref[n]) for n in range(4))
    cols_ref[:, 0:1] = gain_in
    cols_ref[:, 1:2] = gain_out
    cols_ref[:, 2:3] = bias_out
    spread_tile(pair_ref, x_scr)
    spread_tile(cot_ref, c_scr)
    for r in range(GROUPS):
        xhat, scale = normalized(x_scr[r].T, 0)
        normed = (xhat * gain_in + bias_in).astype(BF)
        xhat_ref[r] = xhat
        scale_ref[r : r + 1, :] = scale
        proj = dot(wt_scr[...], normed, 1, 0)
        for h in range(2):
            sig = jax.nn.sigmoid(proj[2 * h * CH : (2 * h + 1) * CH])
            value = proj[(2 * h + 1) * CH : (2 * h + 2) * CH]
            fac_ref[r, 2 * h * CH : (2 * h + 1) * CH, :] = (value * sig * (1.0 - sig)).astype(BF)
            fac_ref[r, (2 * h + 1) * CH : (2 * h + 2) * CH, :] = sig.astype(BF)
        gate = jax.nn.sigmoid(proj[4 * CH :])
        gated = c_scr[r].T * gate
        gate_ref[r] = gate
        slope_ref[r] = gated * (1.0 - gate)
        dx_ref[r] = dot(w_out_ref[...], gated.astype(BF), 1, 0) * gain_out


def side(pair, cotangent, w_in, w_out, gain_in, bias_in, gain_out, bias_out):
    square = jax.ShapeDtypeStruct((GROUPS, CH, LANES), F32)
    return pl.pallas_call(
        side_kernel,
        out_shape=[
            square,
            square,
            square,
            jax.ShapeDtypeStruct((GROUPS, 4 * CH, LANES), BF),
            square,
            jax.ShapeDtypeStruct((ROWS, LANES), F32),
            jax.ShapeDtypeStruct((CH, LANES), F32),
            jax.ShapeDtypeStruct((CH, 5 * CH), BF),
            jax.ShapeDtypeStruct((CH, CH), BF),
        ],
        in_specs=in_hbm(8),
        scratch_shapes=[
            pltpu.VMEM((TILE, TILE, CH), BF),
            pltpu.VMEM((TILE, TILE, CH), BF),
            pltpu.VMEM((CH, CH), BF),
            pltpu.VMEM((4, 1, CH), F32),
            pltpu.VMEM((GROUPS, LANES, CH), F32),
            pltpu.VMEM((GROUPS, LANES, CH), F32),
            pltpu.VMEM((5 * CH, CH), BF),
            pltpu.SemaphoreType.DMA((8,)),
        ],
        compiler_params=params(),
        cost_estimate=pl.CostEstimate(flops=300_000_000, bytes_accessed=6_000_000, transcendentals=600_000),
        name="side",
    )(*keep_in_hbm(pair, cotangent, w_in, w_out, gain_in, bias_in, gain_out, bias_out))


def assemble_left_kernel(in_ref, left_ref, t_scr):
    read_rows(in_ref, t_scr)
    for g in range(KG):
        blocks = [
            t_scr[:, SLOTS * g + q].astype(F32).reshape(CH, LANES) if SLOTS * g + q < KB else None
            for q in range(SLOTS)
        ]
        for s, value in enumerate(swap_slots(blocks)):
            left_ref[CH * s : CH * (s + 1), part_lanes(g)] = value.astype(BF)


def assemble_left(received):
    return pl.pallas_call(
        assemble_left_kernel,
        out_shape=jax.ShapeDtypeStruct((SLOTS * NB * ROWS, KG * LANES), BF),
        scratch_shapes=[pltpu.VMEM((NB, KB, ROWS, LANES), BF)],
        compiler_params=params(),
        cost_estimate=pl.CostEstimate(flops=2_000_000, bytes_accessed=1_000_000, transcendentals=0),
        name="assemble_left",
    )(received.reshape(NB, KB, PART, 2 * PARTS * LANES))


def assemble_right_kernel(in_ref, right_ref, t_scr, v_scr, r_scr):
    read_rows(in_ref, t_scr, 1)
    r_scr[...] = jnp.zeros(r_scr.shape, F32)
    for g in range(KG):
        blocks = [
            t_scr[:, SLOTS * g + q].astype(F32).reshape(CH, LANES) if SLOTS * g + q < KB else None
            for q in range(SLOTS)
        ]
        for s, value in enumerate(swap_slots(blocks)):
            v_scr[s] = value
            for b in range(NB):
                to = LANES * (b // SLOTS) + SLOT * (b % SLOTS) + GROUPS * s
                r_scr[to : to + GROUPS, part_lanes(g)] = v_scr[s, ROWS * b : ROWS * b + GROUPS]
    right_ref[...] = r_scr[...].astype(BF)


def assemble_right(received):
    return pl.pallas_call(
        assemble_right_kernel,
        out_shape=jax.ShapeDtypeStruct((JG * LANES, KG * LANES), BF),
        scratch_shapes=[
            pltpu.VMEM((NB, KB, ROWS, LANES), BF),
            pltpu.VMEM((SLOTS, CH, LANES), F32),
            pltpu.VMEM((JG * LANES, KG * LANES), F32),
        ],
        compiler_params=params(),
        cost_estimate=pl.CostEstimate(flops=2_000_000, bytes_accessed=1_000_000, transcendentals=0),
        name="assemble_right",
    )(received.reshape(NB, KB, PART, 2 * PARTS * LANES))


def product_messages(left_ref, right_ref, out_ref, place, t_scr):
    prod = dot(left_ref[...], right_ref[...], 1, 1)
    for g in range(JG):
        blocks = [prod[CH * s : CH * (s + 1), part_lanes(g)] for s in range(SLOTS)]
        for q, value in enumerate(swap_slots(blocks)):
            b = SLOTS * g + q
            if b < NB:
                write_rows(out_ref, place(b), value, t_scr)


def products_own_kernel(left_ref, right_ref, out_ref, t_scr):
    product_messages(left_ref, right_ref, out_ref, lambda b: b, t_scr)


def products_own(left, right):
    return pl.pallas_call(
        products_own_kernel,
        out_shape=message((NB, NB)),
        scratch_shapes=[pltpu.VMEM((NB, ROWS, LANES), BF)],
        compiler_params=params(),
        cost_estimate=pl.CostEstimate(flops=230_000_000, bytes_accessed=1_400_000, transcendentals=0),
        name="products_own",
    )(left, right)


def products_kernel(core_ref, left_ref, right_ref, own_ref, out_ref, t_scr):
    core = core_ref[0]
    for b in range(NB):
        out_ref[:, 2 * b + core] = own_ref[:, b]
    product_messages(left_ref, right_ref, out_ref, lambda b: 2 * b + 1 - core, t_scr)


def products(core, left, other, own):
    return pl.pallas_call(
        products_kernel,
        out_shape=message((NB, KB)),
        in_specs=[pl.BlockSpec(memory_space=pltpu.SMEM)] + [pl.BlockSpec(memory_space=pltpu.VMEM)] * 3,
        scratch_shapes=[pltpu.VMEM((NB, ROWS, LANES), BF)],
        compiler_params=params(),
        cost_estimate=pl.CostEstimate(flops=230_000_000, bytes_accessed=1_600_000, transcendentals=0),
        name="products",
    )(core, left, other, own).reshape(CH, PART, PARTS * LANES)


def middle_kernel(
    prod_ref, gate_ref, slope_ref, dx_ref, cols_ref, w_ref,
    update_ref, out_ref, dgate_ref, p_scr, o_scr,
):
    unpack(prod_ref, p_scr)
    used = used_lanes((CH, LANES))
    gain, bias = cols_ref[:, 1:2], cols_ref[:, 2:3]
    for r in range(GROUPS):
        xhat, scale = normalized(by_row(p_scr)[row_at(r), :], 0)
        prodn = (xhat * gain + bias).astype(BF)
        mixed = dot(w_ref[...], prodn, 1, 0)
        gather_tile((gate_ref[r] * mixed).T, update_ref, r)
        dgate_ref[r] = (slope_ref[r] * mixed).astype(BF)
        d_prod = norm_grad(dx_ref[r], xhat, scale, 0)
        by_row(o_scr)[row_at(r), :] = jnp.where(used, d_prod, 0.0)
    pack(out_ref, o_scr)


def middle(prod, gate, slope, dx, cols, w_out_t):
    return pl.pallas_call(
        middle_kernel,
        out_shape=[
            pltpu.VMEM((TILE, TILE, CH), BF),
            message((CH,)),
            jax.ShapeDtypeStruct((GROUPS, CH, LANES), BF),
        ],
        scratch_shapes=[PADDED, PADDED],
        compiler_params=params(),
        cost_estimate=pl.CostEstimate(flops=50_000_000, bytes_accessed=4_000_000, transcendentals=10_000),
        name="middle",
    )(prod, gate, slope, dx, cols, w_out_t)


def regroup_kernel(core_ref, in_ref, keep_ref, send_ref, t_scr):
    core = core_ref[0]
    read_rows(in_ref, t_scr)
    for t, to_ref in enumerate((send_ref, keep_ref)):
        parity = 1 - core if t == 0 else core
        for g in range(JG):
            blocks = [
                t_scr[:, 2 * (SLOTS * g + q) + parity].astype(F32).reshape(CH, LANES) if SLOTS * g + q < NB else None
                for q in range(SLOTS)
            ]
            for s, value in enumerate(swap_slots(blocks)):
                to_ref[CH * s : CH * (s + 1), part_lanes(g)] = value.astype(BF)


def regroup(core, received):
    half = jax.ShapeDtypeStruct((SLOTS * NB * ROWS, JG * LANES), BF)
    return pl.pallas_call(
        regroup_kernel,
        out_shape=[half, half],
        in_specs=[pl.BlockSpec(memory_space=pltpu.SMEM), pl.BlockSpec(memory_space=pltpu.VMEM)],
        scratch_shapes=[pltpu.VMEM((NB, KB, ROWS, LANES), BF)],
        compiler_params=params(),
        cost_estimate=pl.CostEstimate(flops=2_000_000, bytes_accessed=1_000_000, transcendentals=0),
        name="regroup",
    )(core, received.reshape(NB, KB, PART, PARTS * LANES))


def left_grad_kernel(keep_ref, send_ref, own_ref, other_ref, left_hbm, out_ref, left_ref, t_scr, sems):
    rows = [pl.ds(CH * s, CH) for s in range(SLOTS)]
    copies = fetch([left_hbm.at[at] for at in rows], [left_ref.at[at] for at in rows], sems)
    for g in range(KG):
        lanes = part_lanes(g)
        d_left = dot(keep_ref[...], own_ref[:, lanes], 1, 0) + dot(send_ref[...], other_ref[:, lanes], 1, 0)
        for q, value in enumerate(swap_slots([d_left[CH * s : CH * (s + 1)] for s in range(SLOTS)])):
            if SLOTS * g + q < KB:
                write_rows(out_ref, SLOTS * g + q, value, t_scr)
    for copy in copies:
        copy.wait()


def left_grad(keep, send, own, other, left_other):
    return pl.pallas_call(
        left_grad_kernel,
        out_shape=[message((NB, KB)), jax.ShapeDtypeStruct((SLOTS * NB * ROWS, KG * LANES), BF)],
        in_specs=[pl.BlockSpec(memory_space=pltpu.VMEM)] * 4 + in_hbm(1),
        scratch_shapes=[pltpu.VMEM((NB, ROWS, LANES), BF), pltpu.SemaphoreType.DMA((SLOTS,))],
        compiler_params=params(),
        cost_estimate=pl.CostEstimate(flops=450_000_000, bytes_accessed=2_200_000, transcendentals=0),
        name="left_grad",
    )(keep, send, own, other, *keep_in_hbm(left_other))


def right_grad_kernel(
    keep_ref, other_ref, left_ref, left_other_ref, d_left_ref, update_ref, out_ref, update_hbm, d_scr, o_scr, sem
):
    copy = pltpu.make_async_copy(update_ref, update_hbm, sem)
    copy.start()
    out_ref[:, :, :, : PARTS * LANES] = d_left_ref[...]
    d_scr[...] = dot(keep_ref[...], left_ref[...], 0, 0) + dot(other_ref[...], left_other_ref[...], 0, 0)
    for g in range(KG):
        for b in range(NB):
            at = LANES * (b // SLOTS) + SLOT * (b % SLOTS)
            blocks = [d_scr[at + GROUPS * s : at + GROUPS * s + ROWS, part_lanes(g)] for s in range(SLOTS)]
            for q, value in enumerate(swap_slots(blocks)):
                if SLOTS * g + q < KB:
                    o_scr[b, SLOTS * g + q] = value.astype(o_scr.dtype)
    for p in range(PARTS):
        out_ref[:, :, :, part_lanes(PARTS + p)] = o_scr[:, :, PART * p : PART * (p + 1), :].astype(BF)
    copy.wait()


def right_grad(keep, other, left, left_other, d_left, update):
    out, update = pl.pallas_call(
        right_grad_kernel,
        out_shape=[message((NB, KB), 2), jax.ShapeDtypeStruct((TILE, TILE, CH), BF)],
        out_specs=[pl.BlockSpec(memory_space=pltpu.VMEM), pl.BlockSpec(memory_space=pltpu.HBM)],
        scratch_shapes=[
            pltpu.VMEM((JG * LANES, KG * LANES), F32),
            pltpu.VMEM((NB, KB, ROWS, LANES), BF),
            pltpu.SemaphoreType.DMA,
        ],
        compiler_params=params(),
        cost_estimate=pl.CostEstimate(flops=450_000_000, bytes_accessed=2_500_000, transcendentals=0),
        name="right_grad",
    )(keep, other, left, left_other, d_left, pltpu.with_memory_space_constraint(update, pltpu.VMEM))
    return out.reshape(CH, PART, 2 * PARTS * LANES), update


def finish_kernel(
    d_ref, fac_ref, dgate_ref, xhat_ref, scale_ref, cols_ref, w_ref, out_hbm, l_scr, r_scr, out_ref, sems
):
    copies = []
    unpack(d_ref, l_scr, 0)
    unpack(d_ref, r_scr, 1)
    gain = cols_ref[:, 0:1]
    for r in range(GROUPS):
        d_left = by_row(l_scr)[row_at(r), :]
        d_right = by_row(r_scr)[row_at(r), :]
        parts = [
            (d * fac_ref[r, CH * f : CH * (f + 1), :].astype(F32)).astype(BF)
            for f, d in enumerate((d_left, d_left, d_right, d_right))
        ]
        d_proj = jnp.concatenate(parts + [dgate_ref[r]], 0)
        d_normed = dot(w_ref[...], d_proj, 1, 0).astype(BF).astype(F32)
        gather_tile(norm_grad(d_normed * gain, xhat_ref[r], scale_ref[r : r + 1, :], 0).T, out_ref, r)
        copies += send_tile(out_ref, out_hbm, r, sems)
    for copy in copies:
        copy.wait()


def finish(d_edges, fac, dgate, xhat, scale, cols, w_in):
    return pl.pallas_call(
        finish_kernel,
        out_shape=jax.ShapeDtypeStruct((TILE, TILE, CH), BF),
        out_specs=pl.BlockSpec(memory_space=pltpu.HBM),
        scratch_shapes=[
            PADDED,
            PADDED,
            pltpu.VMEM((TILE, TILE, CH), BF),
            pltpu.SemaphoreType.DMA((TILE // PART,)),
        ],
        compiler_params=params(),
        cost_estimate=pl.CostEstimate(flops=250_000_000, bytes_accessed=4_000_000, transcendentals=0),
        name="finish",
    )(d_edges, fac, dgate, xhat, scale, cols, w_in)


def exchange(x):
    return lax.all_to_all(x, WIDE, 0, 0, tiled=True)


def other_core(x):
    return lax.ppermute(x, "core", [(0, 1), (1, 0)])


def shards(pair, cotangent, gain_in, bias_in, w_in, gain_out, bias_out, w_out):
    gain_in, bias_in = gain_in.reshape(1, CH), bias_in.reshape(1, CH)
    gain_out, bias_out = gain_out.reshape(1, CH), bias_out.reshape(1, CH)
    core = lax.axis_index("core").astype(jnp.int32).reshape(1)
    received = exchange(edges(pair, w_in, gain_in, bias_in))
    ready = side(pair, cotangent, w_in, w_out, gain_in, bias_in, gain_out, bias_out)
    received, ready = lax.optimization_barrier((received, ready))
    gate, slope, dx, fac, xhat, scale, cols, w_in, w_out_t = ready
    right = assemble_right(received)
    right_other = other_core(right)
    left = assemble_left(received)
    left_other = other_core(left)
    prod = products(core, left, right_other, products_own(left, right))
    prod, left_other = lax.optimization_barrier((prod, left_other))
    update, d_prod, dgate = middle(exchange(prod), gate, slope, dx, cols, w_out_t)
    keep, send = regroup(core, exchange(d_prod))
    sent = other_core(send)
    d_left, left_other = left_grad(keep, send, right, right_other, left_other)
    d_edges, update = right_grad(keep, sent, left, left_other, d_left, update)
    d_edges = exchange(d_edges)
    grad = finish(d_edges, fac, dgate, xhat, scale, cols, w_in)
    return update, grad


def solution(mesh):
    split = Mesh(mesh.devices.reshape(2, 4, 2, 4, 4), NAMES)
    tile = P(("zh", "x", "core"), ("y", "zl"), None)
    return jax.shard_map(
        shards,
        mesh=split,
        in_specs=(tile, tile, P(), P(), P(), P(), P(), P()),
        out_specs=(tile, tile),
        check_vma=False,
    )
```

```python
import jax
import jax.numpy as jnp
from jax import lax
from jax.experimental import pallas as pl
from jax.experimental.pallas import tpu as pltpu
from jax.sharding import Mesh, PartitionSpec as P

EPS = 1e-05
BF = jnp.bfloat16
F32 = jnp.float32

TILE = 36
SLOT = 40
SLOTS = 3
GROUPS = 12
LANES = 128
ROWS = 16
PART = 4
PARTS = GROUPS // PART
CH = 128
NB = 8
KB = 16
KG = 6
JG = 3
CHUNKS = 4
NAMES = ("zh", "x", "core", "y", "zl")
WIDE = ("zh", "zl", "x", "y")
BLOCKS = (2, 4, 4, 4)


def params(mib=14):
    return pltpu.CompilerParams(vmem_limit_bytes=mib * 1024 * 1024)


def dot(a, b, ca, cb):
    return lax.dot_general(a, b, (((ca,), (cb,)), ((), ())), preferred_element_type=F32)


def used_lanes(shape):
    lane = lax.broadcasted_iota(jnp.int32, shape, len(shape) - 1)
    used = lane < TILE
    for s in range(1, SLOTS):
        used = used | ((lane >= SLOT * s) & (lane < SLOT * s + TILE))
    return used


def swap_slots(blocks):
    shape = next(b.shape for b in blocks if b is not None)
    lane = lax.broadcasted_iota(jnp.int32, shape, 1)
    out = []
    for s in range(SLOTS):
        acc = jnp.zeros(shape, F32)
        for q, b in enumerate(blocks):
            if b is None:
                continue
            shift = (SLOT * (q - s)) % LANES
            moved = pltpu.roll(b, shift, 1) if shift else b
            acc = jnp.where((lane >= SLOT * q) & (lane < SLOT * (q + 1)), moved, acc)
        out.append(acc)
    return out


def spread_tile(tile_ref, scr):
    for r in range(GROUPS):
        for s in range(SLOTS):
            scr[r, SLOT * s : SLOT * s + TILE, :] = tile_ref[r + GROUPS * s].astype(F32)


def gather_tile(value, tile_ref, r):
    for s in range(SLOTS):
        tile_ref[r + GROUPS * s] = value[SLOT * s : SLOT * s + TILE].astype(BF)


def send_tile(tile_ref, tile_hbm, r, sems):
    if r % PART < PART - 1:
        return []
    copies = []
    for s in range(SLOTS):
        rows = pl.ds(r + 1 - PART + GROUPS * s, PART)
        copies.append(pltpu.make_async_copy(tile_ref.at[rows], tile_hbm.at[rows], sems.at[r // PART * SLOTS + s]))
        copies[-1].start()
    return copies


def normalized(x, axis):
    center = x - jnp.mean(x, axis, keepdims=True)
    scale = lax.rsqrt(jnp.mean(center * center, axis, keepdims=True) + EPS)
    return center * scale, scale


def norm_grad(d, xhat, scale, axis):
    return scale * (d - jnp.mean(d, axis, keepdims=True) - xhat * jnp.mean(d * xhat, axis, keepdims=True))


def message(leading, arrays=1):
    return jax.ShapeDtypeStruct(leading + (PART, arrays * PARTS * LANES), BF)


def part_lanes(p):
    return slice(LANES * p, LANES * (p + 1))


def row_at(r):
    return pl.ds(r // PART * CH * 8 + r % PART, CH, stride=8)


def by_row(scr):
    return scr.reshape(PARTS * CH * 8, LANES)


PADDED = pltpu.VMEM((PARTS, CH, 8, LANES), F32)


def pack(out_ref, scr, array=0, rows=slice(None)):
    for p in range(PARTS):
        out_ref[rows, :, part_lanes(array * PARTS + p)] = scr[p, rows, :PART, :].astype(BF)


def unpack(in_ref, scr, array=0):
    for p in range(PARTS):
        scr[p, :, :PART, :] = in_ref[:, :, part_lanes(array * PARTS + p)].astype(F32)


def read_rows(in_ref, scr, array=0):
    scr[:, :, :, :, GROUPS:, :] = jnp.zeros(BLOCKS + (ROWS - GROUPS, LANES), scr.dtype)
    for p in range(PARTS):
        part = in_ref[:, :, :, :, :, part_lanes(array * PARTS + p)]
        scr[:, :, :, :, PART * p : PART * (p + 1), :] = part.astype(scr.dtype)


def write_rows(out_ref, at, value, scr):
    scr[...] = value.astype(scr.dtype).reshape(NB, ROWS, LANES)
    for p in range(PARTS):
        part = scr[:, PART * p : PART * (p + 1), :].astype(BF)
        if isinstance(at, tuple):
            out_ref[(*at, slice(None), part_lanes(p))] = by_block(part)
        else:
            out_ref[:, at, :, part_lanes(p)] = part


def column_block(k, parity=0):
    return (slice(None), k % 4 + parity, slice(None), k // 4)


def by_block(value):
    return value.reshape(BLOCKS[0], BLOCKS[2], *value.shape[1:])


def column(row):
    return jnp.broadcast_to(row, (8, CH)).T[:, :1]


def fetch(sources, buffers, sems):
    copies = [pltpu.make_async_copy(s, b, sems.at[n]) for n, (s, b) in enumerate(zip(sources, buffers))]
    for copy in copies:
        copy.start()
    return copies


def in_hbm(n):
    return [pl.BlockSpec(memory_space=pltpu.HBM)] * n


def keep_in_hbm(*arrays):
    return [pltpu.with_memory_space_constraint(a, pltpu.HBM) for a in arrays]


def edges_kernel(
    pair_hbm, w_hbm, gain_hbm, bias_hbm, out_hbm,
    pair_ref, w_ref, gain_ref, bias_ref, x_scr, l_scr, r_scr, wt_scr, out_ref, sems, out_sems,
):
    copies = fetch(
        (pair_hbm, w_hbm, gain_hbm, bias_hbm), (pair_ref, w_ref, gain_ref, bias_ref), sems
    )
    x_scr[...] = jnp.zeros(x_scr.shape, F32)
    used = used_lanes((CH, LANES))
    copies[1].wait()
    wt_scr[...] = w_ref[:, : 4 * CH].astype(F32).T.astype(BF)
    copies[2].wait()
    copies[3].wait()
    copies[0].wait()
    spread_tile(pair_ref, x_scr)
    for r in range(0, GROUPS, 2):
        xhat, _ = normalized(x_scr[r : r + 2].reshape(2 * LANES, CH), 1)
        normed = (xhat * gain_ref[...] + bias_ref[...]).astype(BF)
        proj = dot(wt_scr[...], normed, 1, 1)
        left = jax.nn.sigmoid(proj[:CH]) * proj[CH : 2 * CH]
        right = jax.nn.sigmoid(proj[2 * CH : 3 * CH]) * proj[3 * CH :]
        for n in (r, r + 1):
            by_row(l_scr)[row_at(n), :] = jnp.where(used, left[:, part_lanes(n - r)], 0.0)
            by_row(r_scr)[row_at(n), :] = jnp.where(used, right[:, part_lanes(n - r)], 0.0)
    copies = []
    for n in range(CHUNKS):
        rows = slice(CH // CHUNKS * n, CH // CHUNKS * (n + 1))
        pack(out_ref, l_scr, 0, rows)
        pack(out_ref, r_scr, 1, rows)
        copies.append(pltpu.make_async_copy(out_ref.at[rows], out_hbm.at[rows], out_sems.at[n]))
        copies[-1].start()
    for copy in copies:
        copy.wait()


def edges(pair, w_in, gain_in, bias_in):
    return pl.pallas_call(
        edges_kernel,
        out_shape=message((CH,), 2),
        in_specs=in_hbm(4),
        out_specs=pl.BlockSpec(memory_space=pltpu.HBM),
        scratch_shapes=[
            pltpu.VMEM((TILE, TILE, CH), BF),
            pltpu.VMEM((CH, 5 * CH), BF),
            pltpu.VMEM((1, CH), F32),
            pltpu.VMEM((1, CH), F32),
            pltpu.VMEM((GROUPS, LANES, CH), F32),
            PADDED,
            PADDED,
            pltpu.VMEM((4 * CH, CH), BF),
            pltpu.VMEM((CH, PART, 2 * PARTS * LANES), BF),
            pltpu.SemaphoreType.DMA((4,)),
            pltpu.SemaphoreType.DMA((CHUNKS,)),
        ],
        compiler_params=params(),
        cost_estimate=pl.CostEstimate(flops=200_000_000, bytes_accessed=1_200_000, transcendentals=400_000),
        name="edges",
    )(*keep_in_hbm(pair, w_in, gain_in, bias_in))


def side_kernel(
    pair_hbm, cot_hbm, w_hbm, w_out_hbm, gain_hbm, bias_hbm, gain_out_hbm, bias_out_hbm,
    gate_ref, slope_ref, dx_ref, fac_ref, xhat_ref, scale_ref, cols_ref, w_ref, w_out_t_ref,
    pair_ref, cot_ref, w_out_ref, rows_ref, x_scr, c_scr, wt_scr, sems,
):
    copies = fetch(
        (pair_hbm, cot_hbm, w_hbm, w_out_hbm, gain_hbm, bias_hbm, gain_out_hbm, bias_out_hbm),
        (pair_ref, cot_ref, w_ref, w_out_ref) + tuple(rows_ref.at[n] for n in range(4)),
        sems,
    )
    x_scr[...] = jnp.zeros(x_scr.shape, F32)
    c_scr[...] = jnp.zeros(c_scr.shape, F32)
    scale_ref[...] = jnp.zeros(scale_ref.shape, F32)
    cols_ref[...] = jnp.zeros(cols_ref.shape, F32)
    for copy in copies:
        copy.wait()
    wt_scr[...] = w_ref[...].astype(F32).T.astype(BF)
    w_out_t_ref[...] = w_out_ref[...].astype(F32).T.astype(BF)
    gain_in, bias_in, gain_out, bias_out = (column(rows_ref[n]) for n in range(4))
    cols_ref[:, 0:1] = gain_in
    cols_ref[:, 1:2] = gain_out
    cols_ref[:, 2:3] = bias_out
    spread_tile(pair_ref, x_scr)
    spread_tile(cot_ref, c_scr)
    for r in range(GROUPS):
        xhat, scale = normalized(x_scr[r].T, 0)
        normed = (xhat * gain_in + bias_in).astype(BF)
        xhat_ref[r] = xhat
        scale_ref[r : r + 1, :] = scale
        proj = dot(wt_scr[...], normed, 1, 0)
        for h in range(2):
            sig = jax.nn.sigmoid(proj[2 * h * CH : (2 * h + 1) * CH])
            value = proj[(2 * h + 1) * CH : (2 * h + 2) * CH]
            fac_ref[r, 2 * h * CH : (2 * h + 1) * CH, :] = (value * sig * (1.0 - sig)).astype(BF)
            fac_ref[r, (2 * h + 1) * CH : (2 * h + 2) * CH, :] = sig.astype(BF)
        gate = jax.nn.sigmoid(proj[4 * CH :])
        gated = c_scr[r].T * gate
        gate_ref[r] = gate
        slope_ref[r] = gated * (1.0 - gate)
        dx_ref[r] = dot(w_out_ref[...], gated.astype(BF), 1, 0) * gain_out


def side(pair, cotangent, w_in, w_out, gain_in, bias_in, gain_out, bias_out):
    square = jax.ShapeDtypeStruct((GROUPS, CH, LANES), F32)
    return pl.pallas_call(
        side_kernel,
        out_shape=[
            square,
            square,
            square,
            jax.ShapeDtypeStruct((GROUPS, 4 * CH, LANES), BF),
            square,
            jax.ShapeDtypeStruct((ROWS, LANES), F32),
            jax.ShapeDtypeStruct((CH, LANES), F32),
            jax.ShapeDtypeStruct((CH, 5 * CH), BF),
            jax.ShapeDtypeStruct((CH, CH), BF),
        ],
        in_specs=in_hbm(8),
        scratch_shapes=[
            pltpu.VMEM((TILE, TILE, CH), BF),
            pltpu.VMEM((TILE, TILE, CH), BF),
            pltpu.VMEM((CH, CH), BF),
            pltpu.VMEM((4, 1, CH), F32),
            pltpu.VMEM((GROUPS, LANES, CH), F32),
            pltpu.VMEM((GROUPS, LANES, CH), F32),
            pltpu.VMEM((5 * CH, CH), BF),
            pltpu.SemaphoreType.DMA((8,)),
        ],
        compiler_params=params(),
        cost_estimate=pl.CostEstimate(flops=300_000_000, bytes_accessed=6_000_000, transcendentals=600_000),
        name="side",
    )(*keep_in_hbm(pair, cotangent, w_in, w_out, gain_in, bias_in, gain_out, bias_out))


def assemble_left_kernel(in_ref, left_ref, t_scr):
    read_rows(in_ref, t_scr)
    for g in range(KG):
        blocks = [
            t_scr[column_block(SLOTS * g + q)].astype(F32).reshape(CH, LANES) if SLOTS * g + q < KB else None
            for q in range(SLOTS)
        ]
        for s, value in enumerate(swap_slots(blocks)):
            left_ref[CH * s : CH * (s + 1), part_lanes(g)] = value.astype(BF)


def assemble_left(received):
    return pl.pallas_call(
        assemble_left_kernel,
        out_shape=jax.ShapeDtypeStruct((SLOTS * NB * ROWS, KG * LANES), BF),
        scratch_shapes=[pltpu.VMEM(BLOCKS + (ROWS, LANES), BF)],
        compiler_params=params(),
        cost_estimate=pl.CostEstimate(flops=2_000_000, bytes_accessed=1_000_000, transcendentals=0),
        name="assemble_left",
    )(received.reshape(BLOCKS + (PART, 2 * PARTS * LANES)))


def assemble_right_kernel(in_ref, right_ref, t_scr, v_scr, r_scr):
    read_rows(in_ref, t_scr, 1)
    r_scr[...] = jnp.zeros(r_scr.shape, F32)
    for g in range(KG):
        blocks = [
            t_scr[column_block(SLOTS * g + q)].astype(F32).reshape(CH, LANES) if SLOTS * g + q < KB else None
            for q in range(SLOTS)
        ]
        for s, value in enumerate(swap_slots(blocks)):
            v_scr[s] = value
            for b in range(NB):
                to = LANES * (b // SLOTS) + SLOT * (b % SLOTS) + GROUPS * s
                r_scr[to : to + GROUPS, part_lanes(g)] = v_scr[s, ROWS * b : ROWS * b + GROUPS]
    right_ref[...] = r_scr[...].astype(BF)


def assemble_right(received):
    return pl.pallas_call(
        assemble_right_kernel,
        out_shape=jax.ShapeDtypeStruct((JG * LANES, KG * LANES), BF),
        scratch_shapes=[
            pltpu.VMEM(BLOCKS + (ROWS, LANES), BF),
            pltpu.VMEM((SLOTS, CH, LANES), F32),
            pltpu.VMEM((JG * LANES, KG * LANES), F32),
        ],
        compiler_params=params(),
        cost_estimate=pl.CostEstimate(flops=2_000_000, bytes_accessed=1_000_000, transcendentals=0),
        name="assemble_right",
    )(received.reshape(BLOCKS + (PART, 2 * PARTS * LANES)))


def product_messages(left_ref, right_ref, out_ref, place, t_scr):
    prod = dot(left_ref[...], right_ref[...], 1, 1)
    for g in range(JG):
        blocks = [prod[CH * s : CH * (s + 1), part_lanes(g)] for s in range(SLOTS)]
        for q, value in enumerate(swap_slots(blocks)):
            b = SLOTS * g + q
            if b < NB:
                write_rows(out_ref, place(b), value, t_scr)


def products_own_kernel(left_ref, right_ref, out_ref, t_scr):
    product_messages(left_ref, right_ref, out_ref, lambda b: b, t_scr)


def products_own(left, right):
    return pl.pallas_call(
        products_own_kernel,
        out_shape=message((NB, NB)),
        scratch_shapes=[pltpu.VMEM((NB, ROWS, LANES), BF)],
        compiler_params=params(),
        cost_estimate=pl.CostEstimate(flops=230_000_000, bytes_accessed=1_400_000, transcendentals=0),
        name="products_own",
    )(left, right)


def products_kernel(core_ref, left_ref, right_ref, own_ref, out_ref, t_scr):
    core = core_ref[0]
    for b in range(NB):
        out_ref[column_block(2 * b, core)] = by_block(own_ref[:, b])
    product_messages(left_ref, right_ref, out_ref, lambda b: column_block(2 * b, 1 - core), t_scr)


def products(core, left, other, own):
    return pl.pallas_call(
        products_kernel,
        out_shape=message(BLOCKS),
        in_specs=[pl.BlockSpec(memory_space=pltpu.SMEM)] + [pl.BlockSpec(memory_space=pltpu.VMEM)] * 3,
        scratch_shapes=[pltpu.VMEM((NB, ROWS, LANES), BF)],
        compiler_params=params(),
        cost_estimate=pl.CostEstimate(flops=230_000_000, bytes_accessed=1_600_000, transcendentals=0),
        name="products",
    )(core, left, other, own).reshape(CH, PART, PARTS * LANES)


def middle_kernel(
    prod_ref, gate_ref, slope_ref, dx_ref, cols_ref, w_ref,
    update_ref, out_ref, dgate_ref, p_scr, o_scr,
):
    unpack(prod_ref, p_scr)
    used = used_lanes((CH, LANES))
    gain, bias = cols_ref[:, 1:2], cols_ref[:, 2:3]
    for r in range(GROUPS):
        xhat, scale = normalized(by_row(p_scr)[row_at(r), :], 0)
        prodn = (xhat * gain + bias).astype(BF)
        mixed = dot(w_ref[...], prodn, 1, 0)
        gather_tile((gate_ref[r] * mixed).T, update_ref, r)
        dgate_ref[r] = (slope_ref[r] * mixed).astype(BF)
        d_prod = norm_grad(dx_ref[r], xhat, scale, 0)
        by_row(o_scr)[row_at(r), :] = jnp.where(used, d_prod, 0.0)
    pack(out_ref, o_scr)


def middle(prod, gate, slope, dx, cols, w_out_t):
    return pl.pallas_call(
        middle_kernel,
        out_shape=[
            pltpu.VMEM((TILE, TILE, CH), BF),
            message((CH,)),
            jax.ShapeDtypeStruct((GROUPS, CH, LANES), BF),
        ],
        scratch_shapes=[PADDED, PADDED],
        compiler_params=params(),
        cost_estimate=pl.CostEstimate(flops=50_000_000, bytes_accessed=4_000_000, transcendentals=10_000),
        name="middle",
    )(prod, gate, slope, dx, cols, w_out_t)


def regroup_kernel(core_ref, in_ref, keep_ref, send_ref, t_scr):
    core = core_ref[0]
    read_rows(in_ref, t_scr)
    for t, to_ref in enumerate((send_ref, keep_ref)):
        parity = 1 - core if t == 0 else core
        for g in range(JG):
            blocks = [
                t_scr[column_block(2 * (SLOTS * g + q), parity)].astype(F32).reshape(CH, LANES)
                if SLOTS * g + q < NB
                else None
                for q in range(SLOTS)
            ]
            for s, value in enumerate(swap_slots(blocks)):
                to_ref[CH * s : CH * (s + 1), part_lanes(g)] = value.astype(BF)


def regroup(core, received):
    half = jax.ShapeDtypeStruct((SLOTS * NB * ROWS, JG * LANES), BF)
    return pl.pallas_call(
        regroup_kernel,
        out_shape=[half, half],
        in_specs=[pl.BlockSpec(memory_space=pltpu.SMEM), pl.BlockSpec(memory_space=pltpu.VMEM)],
        scratch_shapes=[pltpu.VMEM(BLOCKS + (ROWS, LANES), BF)],
        compiler_params=params(),
        cost_estimate=pl.CostEstimate(flops=2_000_000, bytes_accessed=1_000_000, transcendentals=0),
        name="regroup",
    )(core, received.reshape(BLOCKS + (PART, PARTS * LANES)))


def left_grad_kernel(keep_ref, send_ref, own_ref, other_ref, left_hbm, out_ref, left_ref, t_scr, sems):
    rows = [pl.ds(CH * s, CH) for s in range(SLOTS)]
    copies = fetch([left_hbm.at[at] for at in rows], [left_ref.at[at] for at in rows], sems)
    for g in range(KG):
        lanes = part_lanes(g)
        d_left = dot(keep_ref[...], own_ref[:, lanes], 1, 0) + dot(send_ref[...], other_ref[:, lanes], 1, 0)
        for q, value in enumerate(swap_slots([d_left[CH * s : CH * (s + 1)] for s in range(SLOTS)])):
            if SLOTS * g + q < KB:
                write_rows(out_ref, column_block(SLOTS * g + q), value, t_scr)
    for copy in copies:
        copy.wait()


def left_grad(keep, send, own, other, left_other):
    return pl.pallas_call(
        left_grad_kernel,
        out_shape=[message(BLOCKS), jax.ShapeDtypeStruct((SLOTS * NB * ROWS, KG * LANES), BF)],
        in_specs=[pl.BlockSpec(memory_space=pltpu.VMEM)] * 4 + in_hbm(1),
        scratch_shapes=[pltpu.VMEM((NB, ROWS, LANES), BF), pltpu.SemaphoreType.DMA((SLOTS,))],
        compiler_params=params(),
        cost_estimate=pl.CostEstimate(flops=450_000_000, bytes_accessed=2_200_000, transcendentals=0),
        name="left_grad",
    )(keep, send, own, other, *keep_in_hbm(left_other))


def right_grad_kernel(
    keep_ref, other_ref, left_ref, left_other_ref, d_left_ref, update_ref, out_ref, update_hbm, d_scr, o_scr, sem
):
    copy = pltpu.make_async_copy(update_ref, update_hbm, sem)
    copy.start()
    out_ref[:, :, :, :, :, : PARTS * LANES] = d_left_ref[...]
    d_scr[...] = dot(keep_ref[...], left_ref[...], 0, 0) + dot(other_ref[...], left_other_ref[...], 0, 0)
    for g in range(KG):
        for b in range(NB):
            at = LANES * (b // SLOTS) + SLOT * (b % SLOTS)
            blocks = [d_scr[at + GROUPS * s : at + GROUPS * s + ROWS, part_lanes(g)] for s in range(SLOTS)]
            for q, value in enumerate(swap_slots(blocks)):
                if SLOTS * g + q < KB:
                    k = SLOTS * g + q
                    o_scr[b // 4, k % 4, b % 4, k // 4] = value.astype(o_scr.dtype)
    for p in range(PARTS):
        out_ref[:, :, :, :, :, part_lanes(PARTS + p)] = o_scr[:, :, :, :, PART * p : PART * (p + 1), :].astype(BF)
    copy.wait()


def right_grad(keep, other, left, left_other, d_left, update):
    out, update = pl.pallas_call(
        right_grad_kernel,
        out_shape=[message(BLOCKS, 2), jax.ShapeDtypeStruct((TILE, TILE, CH), BF)],
        out_specs=[pl.BlockSpec(memory_space=pltpu.VMEM), pl.BlockSpec(memory_space=pltpu.HBM)],
        scratch_shapes=[
            pltpu.VMEM((JG * LANES, KG * LANES), F32),
            pltpu.VMEM(BLOCKS + (ROWS, LANES), BF),
            pltpu.SemaphoreType.DMA,
        ],
        compiler_params=params(),
        cost_estimate=pl.CostEstimate(flops=450_000_000, bytes_accessed=2_500_000, transcendentals=0),
        name="right_grad",
    )(keep, other, left, left_other, d_left, pltpu.with_memory_space_constraint(update, pltpu.VMEM))
    return out.reshape(CH, PART, 2 * PARTS * LANES), update


def finish_kernel(
    d_ref, fac_ref, dgate_ref, xhat_ref, scale_ref, cols_ref, w_ref, out_hbm, l_scr, r_scr, out_ref, sems
):
    copies = []
    unpack(d_ref, l_scr, 0)
    unpack(d_ref, r_scr, 1)
    gain = cols_ref[:, 0:1]
    for r in range(GROUPS):
        d_left = by_row(l_scr)[row_at(r), :]
        d_right = by_row(r_scr)[row_at(r), :]
        parts = [
            (d * fac_ref[r, CH * f : CH * (f + 1), :].astype(F32)).astype(BF)
            for f, d in enumerate((d_left, d_left, d_right, d_right))
        ]
        d_proj = jnp.concatenate(parts + [dgate_ref[r]], 0)
        d_normed = dot(w_ref[...], d_proj, 1, 0).astype(BF).astype(F32)
        gather_tile(norm_grad(d_normed * gain, xhat_ref[r], scale_ref[r : r + 1, :], 0).T, out_ref, r)
        copies += send_tile(out_ref, out_hbm, r, sems)
    for copy in copies:
        copy.wait()


def finish(d_edges, fac, dgate, xhat, scale, cols, w_in):
    return pl.pallas_call(
        finish_kernel,
        out_shape=jax.ShapeDtypeStruct((TILE, TILE, CH), BF),
        out_specs=pl.BlockSpec(memory_space=pltpu.HBM),
        scratch_shapes=[
            PADDED,
            PADDED,
            pltpu.VMEM((TILE, TILE, CH), BF),
            pltpu.SemaphoreType.DMA((TILE // PART,)),
        ],
        compiler_params=params(),
        cost_estimate=pl.CostEstimate(flops=250_000_000, bytes_accessed=4_000_000, transcendentals=0),
        name="finish",
    )(d_edges, fac, dgate, xhat, scale, cols, w_in)


def exchange(x):
    return lax.all_to_all(x, WIDE, 0, 0, tiled=True)


def other_core(x):
    return lax.ppermute(x, "core", [(0, 1), (1, 0)])


def shards(pair, cotangent, gain_in, bias_in, w_in, gain_out, bias_out, w_out):
    gain_in, bias_in = gain_in.reshape(1, CH), bias_in.reshape(1, CH)
    gain_out, bias_out = gain_out.reshape(1, CH), bias_out.reshape(1, CH)
    core = lax.axis_index("core").astype(jnp.int32).reshape(1)
    received = exchange(edges(pair, w_in, gain_in, bias_in))
    ready = side(pair, cotangent, w_in, w_out, gain_in, bias_in, gain_out, bias_out)
    received, ready = lax.optimization_barrier((received, ready))
    gate, slope, dx, fac, xhat, scale, cols, w_in, w_out_t = ready
    right = assemble_right(received)
    right_other = other_core(right)
    left = assemble_left(received)
    left_other = other_core(left)
    prod = products(core, left, right_other, products_own(left, right))
    prod, left_other = lax.optimization_barrier((prod, left_other))
    update, d_prod, dgate = middle(exchange(prod), gate, slope, dx, cols, w_out_t)
    keep, send = regroup(core, exchange(d_prod))
    sent = other_core(send)
    d_left, left_other = left_grad(keep, send, right, right_other, left_other)
    d_edges, update = right_grad(keep, sent, left, left_other, d_left, update)
    d_edges = exchange(d_edges)
    grad = finish(d_edges, fac, dgate, xhat, scale, cols, w_in)
    return update, grad


def solution(mesh):
    split = Mesh(mesh.devices.reshape(2, 4, 2, 4, 4), NAMES)
    tile = P(("zh", "x", "core"), ("y", "zl"), None)
    return jax.shard_map(
        shards,
        mesh=split,
        in_specs=(tile, tile, P(), P(), P(), P(), P(), P()),
        out_specs=(tile, tile),
        check_vma=False,
    )
```

```python
import jax
import jax.numpy as jnp
from jax import lax
from jax.experimental import pallas as pl
from jax.experimental.pallas import tpu as pltpu
from jax.sharding import Mesh, PartitionSpec as P

EPS = 1e-05
BF = jnp.bfloat16
F32 = jnp.float32

TILE = 36
SLOT = 40
SLOTS = 3
GROUPS = 12
LANES = 128
ROWS = 16
PART = 4
PARTS = GROUPS // PART
CH = 128
NB = 8
KB = 16
KG = 6
JG = 3
CHUNKS = 4
EARLY = 256
NAMES = ("zh", "x", "core", "y", "zl")
WIDE = ("zh", "zl", "x", "y")
BLOCKS = (2, 4, 4, 4)


def params(mib=14):
    return pltpu.CompilerParams(vmem_limit_bytes=mib * 1024 * 1024)


def dot(a, b, ca, cb):
    return lax.dot_general(a, b, (((ca,), (cb,)), ((), ())), preferred_element_type=F32)


def used_lanes(shape):
    lane = lax.broadcasted_iota(jnp.int32, shape, len(shape) - 1)
    used = lane < TILE
    for s in range(1, SLOTS):
        used = used | ((lane >= SLOT * s) & (lane < SLOT * s + TILE))
    return used


def swap_slots(blocks):
    shape = next(b.shape for b in blocks if b is not None)
    lane = lax.broadcasted_iota(jnp.int32, shape, 1)
    out = []
    for s in range(SLOTS):
        acc = jnp.zeros(shape, F32)
        for q, b in enumerate(blocks):
            if b is None:
                continue
            shift = (SLOT * (q - s)) % LANES
            moved = pltpu.roll(b, shift, 1) if shift else b
            acc = jnp.where((lane >= SLOT * q) & (lane < SLOT * (q + 1)), moved, acc)
        out.append(acc)
    return out


def spread_tile(tile_ref, scr):
    for r in range(GROUPS):
        for s in range(SLOTS):
            scr[r, SLOT * s : SLOT * s + TILE, :] = tile_ref[r + GROUPS * s].astype(F32)


def gather_tile(value, tile_ref, r):
    for s in range(SLOTS):
        tile_ref[r + GROUPS * s] = value[SLOT * s : SLOT * s + TILE].astype(BF)


def send_tile(tile_ref, tile_hbm, r, sems):
    if r % PART < PART - 1:
        return []
    copies = []
    for s in range(SLOTS):
        rows = pl.ds(r + 1 - PART + GROUPS * s, PART)
        copies.append(pltpu.make_async_copy(tile_ref.at[rows], tile_hbm.at[rows], sems.at[r // PART * SLOTS + s]))
        copies[-1].start()
    return copies


def normalized(x, axis):
    center = x - jnp.mean(x, axis, keepdims=True)
    scale = lax.rsqrt(jnp.mean(center * center, axis, keepdims=True) + EPS)
    return center * scale, scale


def norm_grad(d, xhat, scale, axis):
    return scale * (d - jnp.mean(d, axis, keepdims=True) - xhat * jnp.mean(d * xhat, axis, keepdims=True))


def message(leading, arrays=1):
    return jax.ShapeDtypeStruct(leading + (PART, arrays * PARTS * LANES), BF)


def part_lanes(p):
    return slice(LANES * p, LANES * (p + 1))


def row_at(r):
    return pl.ds(r // PART * CH * 8 + r % PART, CH, stride=8)


def by_row(scr):
    return scr.reshape(PARTS * CH * 8, LANES)


PADDED = pltpu.VMEM((PARTS, CH, 8, LANES), F32)


def pack(out_ref, scr, array=0, rows=slice(None)):
    for p in range(PARTS):
        out_ref[rows, :, part_lanes(array * PARTS + p)] = scr[p, rows, :PART, :].astype(BF)


def unpack(in_ref, scr, array=0):
    for p in range(PARTS):
        scr[p, :, :PART, :] = in_ref[:, :, part_lanes(array * PARTS + p)].astype(F32)


def read_rows(in_ref, scr, array=0):
    scr[:, :, :, :, GROUPS:, :] = jnp.zeros(BLOCKS + (ROWS - GROUPS, LANES), scr.dtype)
    for p in range(PARTS):
        part = in_ref[:, :, :, :, :, part_lanes(array * PARTS + p)]
        scr[:, :, :, :, PART * p : PART * (p + 1), :] = part.astype(scr.dtype)


def write_rows(out_ref, at, value, scr):
    scr[...] = value.astype(scr.dtype).reshape(NB, ROWS, LANES)
    for p in range(PARTS):
        part = scr[:, PART * p : PART * (p + 1), :].astype(BF)
        if isinstance(at, tuple):
            out_ref[(*at, slice(None), part_lanes(p))] = by_block(part)
        else:
            out_ref[:, at, :, part_lanes(p)] = part


def column_block(k, parity=0):
    return (slice(None), k % 4 + parity, slice(None), k // 4)


def by_block(value):
    return value.reshape(BLOCKS[0], BLOCKS[2], *value.shape[1:])


def column(row):
    return jnp.broadcast_to(row, (8, CH)).T[:, :1]


def fetch(sources, buffers, sems):
    copies = [pltpu.make_async_copy(s, b, sems.at[n]) for n, (s, b) in enumerate(zip(sources, buffers))]
    for copy in copies:
        copy.start()
    return copies


def in_hbm(n):
    return [pl.BlockSpec(memory_space=pltpu.HBM)] * n


def keep_in_hbm(*arrays):
    return [pltpu.with_memory_space_constraint(a, pltpu.HBM) for a in arrays]


def edges_kernel(
    pair_hbm, w_hbm, gain_hbm, bias_hbm, out_hbm,
    pair_ref, w_ref, gain_ref, bias_ref, x_scr, l_scr, r_scr, wt_scr, out_ref, sems, out_sems,
):
    copies = fetch(
        (pair_hbm, w_hbm, gain_hbm, bias_hbm), (pair_ref, w_ref, gain_ref, bias_ref), sems
    )
    x_scr[...] = jnp.zeros(x_scr.shape, F32)
    used = used_lanes((CH, LANES))
    copies[1].wait()
    wt_scr[...] = w_ref[:, : 4 * CH].astype(F32).T.astype(BF)
    copies[2].wait()
    copies[3].wait()
    copies[0].wait()
    spread_tile(pair_ref, x_scr)
    for r in range(0, GROUPS, 2):
        xhat, _ = normalized(x_scr[r : r + 2].reshape(2 * LANES, CH), 1)
        normed = (xhat * gain_ref[...] + bias_ref[...]).astype(BF)
        proj = dot(wt_scr[...], normed, 1, 1)
        left = jax.nn.sigmoid(proj[:CH]) * proj[CH : 2 * CH]
        right = jax.nn.sigmoid(proj[2 * CH : 3 * CH]) * proj[3 * CH :]
        for n in (r, r + 1):
            by_row(l_scr)[row_at(n), :] = jnp.where(used, left[:, part_lanes(n - r)], 0.0)
            by_row(r_scr)[row_at(n), :] = jnp.where(used, right[:, part_lanes(n - r)], 0.0)
    copies = []
    for n in range(CHUNKS):
        rows = slice(CH // CHUNKS * n, CH // CHUNKS * (n + 1))
        pack(out_ref, l_scr, 0, rows)
        pack(out_ref, r_scr, 1, rows)
        copies.append(pltpu.make_async_copy(out_ref.at[rows], out_hbm.at[rows], out_sems.at[n]))
        copies[-1].start()
    for copy in copies:
        copy.wait()


def edges(pair, w_in, gain_in, bias_in):
    return pl.pallas_call(
        edges_kernel,
        out_shape=message((CH,), 2),
        in_specs=in_hbm(4),
        out_specs=pl.BlockSpec(memory_space=pltpu.HBM),
        scratch_shapes=[
            pltpu.VMEM((TILE, TILE, CH), BF),
            pltpu.VMEM((CH, 5 * CH), BF),
            pltpu.VMEM((1, CH), F32),
            pltpu.VMEM((1, CH), F32),
            pltpu.VMEM((GROUPS, LANES, CH), F32),
            PADDED,
            PADDED,
            pltpu.VMEM((4 * CH, CH), BF),
            pltpu.VMEM((CH, PART, 2 * PARTS * LANES), BF),
            pltpu.SemaphoreType.DMA((4,)),
            pltpu.SemaphoreType.DMA((CHUNKS,)),
        ],
        compiler_params=params(),
        cost_estimate=pl.CostEstimate(flops=200_000_000, bytes_accessed=1_200_000, transcendentals=400_000),
        name="edges",
    )(*keep_in_hbm(pair, w_in, gain_in, bias_in))


def side_kernel(
    pair_hbm, cot_hbm, w_hbm, w_out_hbm, gain_hbm, bias_hbm, gain_out_hbm, bias_out_hbm,
    gate_ref, slope_ref, dx_ref, fac_ref, xhat_ref, scale_ref, cols_ref, w_ref, w_out_t_ref,
    pair_ref, cot_ref, w_out_ref, rows_ref, x_scr, c_scr, wt_scr, sems,
):
    copies = fetch(
        (pair_hbm, cot_hbm, w_hbm, w_out_hbm, gain_hbm, bias_hbm, gain_out_hbm, bias_out_hbm),
        (pair_ref, cot_ref, w_ref, w_out_ref) + tuple(rows_ref.at[n] for n in range(4)),
        sems,
    )
    x_scr[...] = jnp.zeros(x_scr.shape, F32)
    c_scr[...] = jnp.zeros(c_scr.shape, F32)
    scale_ref[...] = jnp.zeros(scale_ref.shape, F32)
    cols_ref[...] = jnp.zeros(cols_ref.shape, F32)
    for copy in copies:
        copy.wait()
    wt_scr[...] = w_ref[...].astype(F32).T.astype(BF)
    w_out_t_ref[...] = w_out_ref[...].astype(F32).T.astype(BF)
    gain_in, bias_in, gain_out, bias_out = (column(rows_ref[n]) for n in range(4))
    cols_ref[:, 0:1] = gain_in
    cols_ref[:, 1:2] = gain_out
    cols_ref[:, 2:3] = bias_out
    spread_tile(pair_ref, x_scr)
    spread_tile(cot_ref, c_scr)
    for r in range(GROUPS):
        xhat, scale = normalized(x_scr[r].T, 0)
        normed = (xhat * gain_in + bias_in).astype(BF)
        xhat_ref[r] = xhat
        scale_ref[r : r + 1, :] = scale
        proj = dot(wt_scr[...], normed, 1, 0)
        for h in range(2):
            sig = jax.nn.sigmoid(proj[2 * h * CH : (2 * h + 1) * CH])
            value = proj[(2 * h + 1) * CH : (2 * h + 2) * CH]
            fac_ref[r, 2 * h * CH : (2 * h + 1) * CH, :] = (value * sig * (1.0 - sig)).astype(BF)
            fac_ref[r, (2 * h + 1) * CH : (2 * h + 2) * CH, :] = sig.astype(BF)
        gate = jax.nn.sigmoid(proj[4 * CH :])
        gated = c_scr[r].T * gate
        gate_ref[r] = gate
        slope_ref[r] = gated * (1.0 - gate)
        dx_ref[r] = dot(w_out_ref[...], gated.astype(BF), 1, 0) * gain_out


def side(pair, cotangent, w_in, w_out, gain_in, bias_in, gain_out, bias_out):
    square = jax.ShapeDtypeStruct((GROUPS, CH, LANES), F32)
    return pl.pallas_call(
        side_kernel,
        out_shape=[
            square,
            square,
            square,
            jax.ShapeDtypeStruct((GROUPS, 4 * CH, LANES), BF),
            square,
            jax.ShapeDtypeStruct((ROWS, LANES), F32),
            jax.ShapeDtypeStruct((CH, LANES), F32),
            jax.ShapeDtypeStruct((CH, 5 * CH), BF),
            jax.ShapeDtypeStruct((CH, CH), BF),
        ],
        in_specs=in_hbm(8),
        scratch_shapes=[
            pltpu.VMEM((TILE, TILE, CH), BF),
            pltpu.VMEM((TILE, TILE, CH), BF),
            pltpu.VMEM((CH, CH), BF),
            pltpu.VMEM((4, 1, CH), F32),
            pltpu.VMEM((GROUPS, LANES, CH), F32),
            pltpu.VMEM((GROUPS, LANES, CH), F32),
            pltpu.VMEM((5 * CH, CH), BF),
            pltpu.SemaphoreType.DMA((8,)),
        ],
        compiler_params=params(),
        cost_estimate=pl.CostEstimate(flops=300_000_000, bytes_accessed=6_000_000, transcendentals=600_000),
        name="side",
    )(*keep_in_hbm(pair, cotangent, w_in, w_out, gain_in, bias_in, gain_out, bias_out))


def assemble_left_kernel(in_ref, left_ref, t_scr):
    read_rows(in_ref, t_scr)
    for g in range(KG):
        blocks = [
            t_scr[column_block(SLOTS * g + q)].astype(F32).reshape(CH, LANES) if SLOTS * g + q < KB else None
            for q in range(SLOTS)
        ]
        for s, value in enumerate(swap_slots(blocks)):
            left_ref[CH * s : CH * (s + 1), part_lanes(g)] = value.astype(BF)


def assemble_left(received):
    return pl.pallas_call(
        assemble_left_kernel,
        out_shape=jax.ShapeDtypeStruct((SLOTS * NB * ROWS, KG * LANES), BF),
        scratch_shapes=[pltpu.VMEM(BLOCKS + (ROWS, LANES), BF)],
        compiler_params=params(),
        cost_estimate=pl.CostEstimate(flops=2_000_000, bytes_accessed=1_000_000, transcendentals=0),
        name="assemble_left",
    )(received.reshape(BLOCKS + (PART, 2 * PARTS * LANES)))


def assemble_right_kernel(in_ref, right_ref, t_scr, v_scr, r_scr):
    read_rows(in_ref, t_scr, 1)
    r_scr[...] = jnp.zeros(r_scr.shape, F32)
    for g in range(KG):
        blocks = [
            t_scr[column_block(SLOTS * g + q)].astype(F32).reshape(CH, LANES) if SLOTS * g + q < KB else None
            for q in range(SLOTS)
        ]
        for s, value in enumerate(swap_slots(blocks)):
            v_scr[s] = value
            for b in range(NB):
                to = LANES * (b // SLOTS) + SLOT * (b % SLOTS) + GROUPS * s
                r_scr[to : to + GROUPS, part_lanes(g)] = v_scr[s, ROWS * b : ROWS * b + GROUPS]
    right_ref[...] = r_scr[...].astype(BF)


def assemble_right(received):
    return pl.pallas_call(
        assemble_right_kernel,
        out_shape=jax.ShapeDtypeStruct((JG * LANES, KG * LANES), BF),
        scratch_shapes=[
            pltpu.VMEM(BLOCKS + (ROWS, LANES), BF),
            pltpu.VMEM((SLOTS, CH, LANES), F32),
            pltpu.VMEM((JG * LANES, KG * LANES), F32),
        ],
        compiler_params=params(),
        cost_estimate=pl.CostEstimate(flops=2_000_000, bytes_accessed=1_000_000, transcendentals=0),
        name="assemble_right",
    )(received.reshape(BLOCKS + (PART, 2 * PARTS * LANES)))


def product_messages(left_ref, right_ref, out_ref, place, t_scr):
    prod = dot(left_ref[...], right_ref[...], 1, 1)
    for g in range(JG):
        blocks = [prod[CH * s : CH * (s + 1), part_lanes(g)] for s in range(SLOTS)]
        for q, value in enumerate(swap_slots(blocks)):
            b = SLOTS * g + q
            if b < NB:
                write_rows(out_ref, place(b), value, t_scr)


def products_own_kernel(left_ref, right_ref, out_ref, t_scr):
    product_messages(left_ref, right_ref, out_ref, lambda b: b, t_scr)


def products_own(left, right):
    return pl.pallas_call(
        products_own_kernel,
        out_shape=message((NB, NB)),
        scratch_shapes=[pltpu.VMEM((NB, ROWS, LANES), BF)],
        compiler_params=params(),
        cost_estimate=pl.CostEstimate(flops=230_000_000, bytes_accessed=1_400_000, transcendentals=0),
        name="products_own",
    )(left, right)


def products_kernel(core_ref, left_ref, right_ref, own_ref, out_ref, t_scr):
    core = core_ref[0]
    for b in range(NB):
        out_ref[column_block(2 * b, core)] = by_block(own_ref[:, b])
    product_messages(left_ref, right_ref, out_ref, lambda b: column_block(2 * b, 1 - core), t_scr)


def products(core, left, other, own):
    return pl.pallas_call(
        products_kernel,
        out_shape=message(BLOCKS),
        in_specs=[pl.BlockSpec(memory_space=pltpu.SMEM)] + [pl.BlockSpec(memory_space=pltpu.VMEM)] * 3,
        scratch_shapes=[pltpu.VMEM((NB, ROWS, LANES), BF)],
        compiler_params=params(),
        cost_estimate=pl.CostEstimate(flops=230_000_000, bytes_accessed=1_600_000, transcendentals=0),
        name="products",
    )(core, left, other, own).reshape(CH, PART, PARTS * LANES)


def middle_kernel(
    prod_ref, gate_ref, slope_ref, dx_ref, cols_ref, w_ref,
    update_ref, out_ref, dgate_ref, p_scr, o_scr,
):
    unpack(prod_ref, p_scr)
    used = used_lanes((CH, LANES))
    gain, bias = cols_ref[:, 1:2], cols_ref[:, 2:3]
    for r in range(GROUPS):
        xhat, scale = normalized(by_row(p_scr)[row_at(r), :], 0)
        prodn = (xhat * gain + bias).astype(BF)
        mixed = dot(w_ref[...], prodn, 1, 0)
        gather_tile((gate_ref[r] * mixed).T, update_ref, r)
        dgate_ref[r] = (slope_ref[r] * mixed).astype(BF)
        d_prod = norm_grad(dx_ref[r], xhat, scale, 0)
        by_row(o_scr)[row_at(r), :] = jnp.where(used, d_prod, 0.0)
    pack(out_ref, o_scr)


def middle(prod, gate, slope, dx, cols, w_out_t):
    return pl.pallas_call(
        middle_kernel,
        out_shape=[
            pltpu.VMEM((TILE, TILE, CH), BF),
            message((CH,)),
            jax.ShapeDtypeStruct((GROUPS, CH, LANES), BF),
        ],
        scratch_shapes=[PADDED, PADDED],
        compiler_params=params(),
        cost_estimate=pl.CostEstimate(flops=50_000_000, bytes_accessed=4_000_000, transcendentals=10_000),
        name="middle",
    )(prod, gate, slope, dx, cols, w_out_t)


def regroup_kernel(core_ref, in_ref, keep_ref, send_ref, t_scr):
    core = core_ref[0]
    read_rows(in_ref, t_scr)
    for t, to_ref in enumerate((send_ref, keep_ref)):
        parity = 1 - core if t == 0 else core
        for g in range(JG):
            blocks = [
                t_scr[column_block(2 * (SLOTS * g + q), parity)].astype(F32).reshape(CH, LANES)
                if SLOTS * g + q < NB
                else None
                for q in range(SLOTS)
            ]
            for s, value in enumerate(swap_slots(blocks)):
                to_ref[CH * s : CH * (s + 1), part_lanes(g)] = value.astype(BF)


def regroup(core, received):
    half = jax.ShapeDtypeStruct((SLOTS * NB * ROWS, JG * LANES), BF)
    return pl.pallas_call(
        regroup_kernel,
        out_shape=[half, half],
        in_specs=[pl.BlockSpec(memory_space=pltpu.SMEM), pl.BlockSpec(memory_space=pltpu.VMEM)],
        scratch_shapes=[pltpu.VMEM(BLOCKS + (ROWS, LANES), BF)],
        compiler_params=params(),
        cost_estimate=pl.CostEstimate(flops=2_000_000, bytes_accessed=1_000_000, transcendentals=0),
        name="regroup",
    )(core, received.reshape(BLOCKS + (PART, PARTS * LANES)))


def left_grad_kernel(keep_ref, send_ref, own_ref, other_ref, left_hbm, out_ref, left_ref, t_scr, sems):
    rows = [pl.ds(CH * s, CH) for s in range(EARLY // CH)]
    copies = fetch([left_hbm.at[at] for at in rows], [left_ref.at[at] for at in rows], sems)
    for g in range(KG):
        lanes = part_lanes(g)
        d_left = dot(keep_ref[...], own_ref[:, lanes], 1, 0) + dot(send_ref[...], other_ref[:, lanes], 1, 0)
        for q, value in enumerate(swap_slots([d_left[CH * s : CH * (s + 1)] for s in range(SLOTS)])):
            if SLOTS * g + q < KB:
                write_rows(out_ref, column_block(SLOTS * g + q), value, t_scr)
    for copy in copies:
        copy.wait()


def left_grad(keep, send, own, other, left_other):
    return pl.pallas_call(
        left_grad_kernel,
        out_shape=[message(BLOCKS), jax.ShapeDtypeStruct((EARLY, KG * LANES), BF)],
        in_specs=[pl.BlockSpec(memory_space=pltpu.VMEM)] * 4 + in_hbm(1),
        scratch_shapes=[pltpu.VMEM((NB, ROWS, LANES), BF), pltpu.SemaphoreType.DMA((EARLY // CH,))],
        compiler_params=params(),
        cost_estimate=pl.CostEstimate(flops=450_000_000, bytes_accessed=2_200_000, transcendentals=0),
        name="left_grad",
    )(keep, send, own, other, *keep_in_hbm(left_other))


def right_grad_kernel(
    keep_ref, other_ref, left_ref, early_ref, left_hbm, d_left_ref, update_ref, out_ref, update_hbm,
    late_ref, d_scr, o_scr, sem, late_sem,
):
    late = pltpu.make_async_copy(left_hbm.at[pl.ds(EARLY, SLOTS * CH - EARLY)], late_ref, late_sem)
    late.start()
    copy = pltpu.make_async_copy(update_ref, update_hbm, sem)
    copy.start()
    out_ref[:, :, :, :, :, : PARTS * LANES] = d_left_ref[...]
    d_scr[...] = dot(keep_ref[...], left_ref[...], 0, 0) + dot(other_ref[:EARLY, :], early_ref[...], 0, 0)
    late.wait()
    d_scr[...] += dot(other_ref[EARLY:, :], late_ref[...], 0, 0)
    for g in range(KG):
        for b in range(NB):
            at = LANES * (b // SLOTS) + SLOT * (b % SLOTS)
            blocks = [d_scr[at + GROUPS * s : at + GROUPS * s + ROWS, part_lanes(g)] for s in range(SLOTS)]
            for q, value in enumerate(swap_slots(blocks)):
                if SLOTS * g + q < KB:
                    k = SLOTS * g + q
                    o_scr[b // 4, k % 4, b % 4, k // 4] = value.astype(o_scr.dtype)
    for p in range(PARTS):
        out_ref[:, :, :, :, :, part_lanes(PARTS + p)] = o_scr[:, :, :, :, PART * p : PART * (p + 1), :].astype(BF)
    copy.wait()


def right_grad(keep, other, left, early, left_other, d_left, update):
    out, update = pl.pallas_call(
        right_grad_kernel,
        out_shape=[message(BLOCKS, 2), jax.ShapeDtypeStruct((TILE, TILE, CH), BF)],
        out_specs=[pl.BlockSpec(memory_space=pltpu.VMEM), pl.BlockSpec(memory_space=pltpu.HBM)],
        in_specs=[pl.BlockSpec(memory_space=pltpu.VMEM)] * 4
        + in_hbm(1)
        + [pl.BlockSpec(memory_space=pltpu.VMEM)] * 2,
        scratch_shapes=[
            pltpu.VMEM((SLOTS * CH - EARLY, KG * LANES), BF),
            pltpu.VMEM((JG * LANES, KG * LANES), F32),
            pltpu.VMEM(BLOCKS + (ROWS, LANES), BF),
            pltpu.SemaphoreType.DMA,
            pltpu.SemaphoreType.DMA,
        ],
        compiler_params=params(),
        cost_estimate=pl.CostEstimate(flops=450_000_000, bytes_accessed=2_500_000, transcendentals=0),
        name="right_grad",
    )(keep, other, left, early, *keep_in_hbm(left_other), d_left, pltpu.with_memory_space_constraint(update, pltpu.VMEM))
    return out.reshape(CH, PART, 2 * PARTS * LANES), update


def finish_kernel(
    d_ref, fac_ref, dgate_ref, xhat_ref, scale_ref, cols_ref, w_ref, out_hbm, l_scr, r_scr, out_ref, sems
):
    copies = []
    unpack(d_ref, l_scr, 0)
    unpack(d_ref, r_scr, 1)
    gain = cols_ref[:, 0:1]
    for r in range(GROUPS):
        d_left = by_row(l_scr)[row_at(r), :]
        d_right = by_row(r_scr)[row_at(r), :]
        parts = [
            (d * fac_ref[r, CH * f : CH * (f + 1), :].astype(F32)).astype(BF)
            for f, d in enumerate((d_left, d_left, d_right, d_right))
        ]
        d_proj = jnp.concatenate(parts + [dgate_ref[r]], 0)
        d_normed = dot(w_ref[...], d_proj, 1, 0).astype(BF).astype(F32)
        gather_tile(norm_grad(d_normed * gain, xhat_ref[r], scale_ref[r : r + 1, :], 0).T, out_ref, r)
        copies += send_tile(out_ref, out_hbm, r, sems)
    for copy in copies:
        copy.wait()


def finish(d_edges, fac, dgate, xhat, scale, cols, w_in):
    return pl.pallas_call(
        finish_kernel,
        out_shape=jax.ShapeDtypeStruct((TILE, TILE, CH), BF),
        out_specs=pl.BlockSpec(memory_space=pltpu.HBM),
        scratch_shapes=[
            PADDED,
            PADDED,
            pltpu.VMEM((TILE, TILE, CH), BF),
            pltpu.SemaphoreType.DMA((TILE // PART,)),
        ],
        compiler_params=params(),
        cost_estimate=pl.CostEstimate(flops=250_000_000, bytes_accessed=4_000_000, transcendentals=0),
        name="finish",
    )(d_edges, fac, dgate, xhat, scale, cols, w_in)


def exchange(x):
    return lax.all_to_all(x, WIDE, 0, 0, tiled=True)


def other_core(x):
    return lax.ppermute(x, "core", [(0, 1), (1, 0)])


def shards(pair, cotangent, gain_in, bias_in, w_in, gain_out, bias_out, w_out):
    gain_in, bias_in = gain_in.reshape(1, CH), bias_in.reshape(1, CH)
    gain_out, bias_out = gain_out.reshape(1, CH), bias_out.reshape(1, CH)
    core = lax.axis_index("core").astype(jnp.int32).reshape(1)
    received = exchange(edges(pair, w_in, gain_in, bias_in))
    ready = side(pair, cotangent, w_in, w_out, gain_in, bias_in, gain_out, bias_out)
    received, ready = lax.optimization_barrier((received, ready))
    gate, slope, dx, fac, xhat, scale, cols, w_in, w_out_t = ready
    right = assemble_right(received)
    right_other = other_core(right)
    left = assemble_left(received)
    left_other = other_core(left)
    prod = products(core, left, right_other, products_own(left, right))
    prod, left_other = lax.optimization_barrier((prod, left_other))
    update, d_prod, dgate = middle(exchange(prod), gate, slope, dx, cols, w_out_t)
    keep, send = regroup(core, exchange(d_prod))
    sent = other_core(send)
    d_left, early = left_grad(keep, send, right, right_other, left_other)
    d_edges, update = right_grad(keep, sent, left, early, left_other, d_left, update)
    d_edges = exchange(d_edges)
    grad = finish(d_edges, fac, dgate, xhat, scale, cols, w_in)
    return update, grad


def solution(mesh):
    split = Mesh(mesh.devices.reshape(2, 4, 2, 4, 4), NAMES)
    tile = P(("zh", "x", "core"), ("y", "zl"), None)
    return jax.shard_map(
        shards,
        mesh=split,
        in_specs=(tile, tile, P(), P(), P(), P(), P(), P()),
        out_specs=(tile, tile),
        check_vma=False,
    )
```

```python
import jax
import jax.numpy as jnp
from jax import lax
from jax.experimental import pallas as pl
from jax.experimental.pallas import tpu as pltpu
from jax.sharding import Mesh, PartitionSpec as P

EPS = 1e-05
BF = jnp.bfloat16
F32 = jnp.float32

TILE = 36
SLOT = 40
SLOTS = 3
GROUPS = 12
LANES = 128
ROWS = 16
PART = 4
PARTS = GROUPS // PART
CH = 128
NB = 8
KB = 16
KG = 6
JG = 3
CHUNKS = 4
NAMES = ("zh", "x", "core", "y", "zl")
WIDE = ("zh", "zl", "x", "y")
BLOCKS = (2, 4, 4, 4)


def params(mib=14):
    return pltpu.CompilerParams(vmem_limit_bytes=mib * 1024 * 1024)


def dot(a, b, ca, cb):
    return lax.dot_general(a, b, (((ca,), (cb,)), ((), ())), preferred_element_type=F32)


def used_lanes(shape):
    lane = lax.broadcasted_iota(jnp.int32, shape, len(shape) - 1)
    used = lane < TILE
    for s in range(1, SLOTS):
        used = used | ((lane >= SLOT * s) & (lane < SLOT * s + TILE))
    return used


def swap_slots(blocks):
    shape = next(b.shape for b in blocks if b is not None)
    lane = lax.broadcasted_iota(jnp.int32, shape, 1)
    out = []
    for s in range(SLOTS):
        acc = jnp.zeros(shape, F32)
        for q, b in enumerate(blocks):
            if b is None:
                continue
            shift = (SLOT * (q - s)) % LANES
            moved = pltpu.roll(b, shift, 1) if shift else b
            acc = jnp.where((lane >= SLOT * q) & (lane < SLOT * (q + 1)), moved, acc)
        out.append(acc)
    return out


def spread_tile(tile_ref, scr):
    for r in range(GROUPS):
        for s in range(SLOTS):
            scr[r, SLOT * s : SLOT * s + TILE, :] = tile_ref[r + GROUPS * s].astype(F32)


def gather_tile(value, tile_ref, r):
    for s in range(SLOTS):
        tile_ref[r + GROUPS * s] = value[SLOT * s : SLOT * s + TILE].astype(BF)


def send_tile(tile_ref, tile_hbm, r, sems):
    if r % PART < PART - 1:
        return []
    copies = []
    for s in range(SLOTS):
        rows = pl.ds(r + 1 - PART + GROUPS * s, PART)
        copies.append(pltpu.make_async_copy(tile_ref.at[rows], tile_hbm.at[rows], sems.at[r // PART * SLOTS + s]))
        copies[-1].start()
    return copies


def normalized(x, axis):
    center = x - jnp.mean(x, axis, keepdims=True)
    scale = lax.rsqrt(jnp.mean(center * center, axis, keepdims=True) + EPS)
    return center * scale, scale


def norm_grad(d, xhat, scale, axis):
    return scale * (d - jnp.mean(d, axis, keepdims=True) - xhat * jnp.mean(d * xhat, axis, keepdims=True))


def message(leading, arrays=1):
    return jax.ShapeDtypeStruct(leading + (PART, arrays * PARTS * LANES), BF)


def part_lanes(p):
    return slice(LANES * p, LANES * (p + 1))


def row_at(r):
    return pl.ds(r // PART * CH * 8 + r % PART, CH, stride=8)


def by_row(scr):
    return scr.reshape(PARTS * CH * 8, LANES)


PADDED = pltpu.VMEM((PARTS, CH, 8, LANES), F32)


def pack(out_ref, scr, array=0, rows=slice(None)):
    for p in range(PARTS):
        out_ref[rows, :, part_lanes(array * PARTS + p)] = scr[p, rows, :PART, :].astype(BF)


def unpack(in_ref, scr, array=0):
    for p in range(PARTS):
        scr[p, :, :PART, :] = in_ref[:, :, part_lanes(array * PARTS + p)].astype(F32)


def read_rows(in_ref, scr, array=0):
    scr[:, :, :, :, GROUPS:, :] = jnp.zeros(BLOCKS + (ROWS - GROUPS, LANES), scr.dtype)
    for p in range(PARTS):
        part = in_ref[:, :, :, :, :, part_lanes(array * PARTS + p)]
        scr[:, :, :, :, PART * p : PART * (p + 1), :] = part.astype(scr.dtype)


def write_rows(out_ref, at, value, scr):
    scr[...] = value.astype(scr.dtype).reshape(NB, ROWS, LANES)
    for p in range(PARTS):
        part = scr[:, PART * p : PART * (p + 1), :].astype(BF)
        if isinstance(at, tuple):
            out_ref[(*at, slice(None), part_lanes(p))] = by_block(part)
        else:
            out_ref[:, at, :, part_lanes(p)] = part


def column_block(k, parity=0):
    return (slice(None), k % 4 + parity, slice(None), k // 4)


def by_block(value):
    return value.reshape(BLOCKS[0], BLOCKS[2], *value.shape[1:])


def column(row):
    return jnp.broadcast_to(row, (8, CH)).T[:, :1]


def fetch(sources, buffers, sems):
    copies = [pltpu.make_async_copy(s, b, sems.at[n]) for n, (s, b) in enumerate(zip(sources, buffers))]
    for copy in copies:
        copy.start()
    return copies


def in_hbm(n):
    return [pl.BlockSpec(memory_space=pltpu.HBM)] * n


def keep_in_hbm(*arrays):
    return [pltpu.with_memory_space_constraint(a, pltpu.HBM) for a in arrays]


def edges_kernel(
    pair_hbm, w_hbm, gain_hbm, bias_hbm, out_hbm,
    pair_ref, w_ref, gain_ref, bias_ref, x_scr, l_scr, r_scr, wt_scr, out_ref, sems, out_sems,
):
    copies = fetch(
        (pair_hbm, w_hbm, gain_hbm, bias_hbm), (pair_ref, w_ref, gain_ref, bias_ref), sems
    )
    x_scr[...] = jnp.zeros(x_scr.shape, F32)
    used = used_lanes((CH, LANES))
    copies[1].wait()
    wt_scr[...] = w_ref[:, : 4 * CH].astype(F32).T.astype(BF)
    copies[2].wait()
    copies[3].wait()
    copies[0].wait()
    spread_tile(pair_ref, x_scr)
    for r in range(0, GROUPS, 2):
        xhat, _ = normalized(x_scr[r : r + 2].reshape(2 * LANES, CH), 1)
        normed = (xhat * gain_ref[...] + bias_ref[...]).astype(BF)
        proj = dot(wt_scr[...], normed, 1, 1)
        left = jax.nn.sigmoid(proj[:CH]) * proj[CH : 2 * CH]
        right = jax.nn.sigmoid(proj[2 * CH : 3 * CH]) * proj[3 * CH :]
        for n in (r, r + 1):
            by_row(l_scr)[row_at(n), :] = jnp.where(used, left[:, part_lanes(n - r)], 0.0)
            by_row(r_scr)[row_at(n), :] = jnp.where(used, right[:, part_lanes(n - r)], 0.0)
    copies = []
    for n in range(CHUNKS):
        rows = slice(CH // CHUNKS * n, CH // CHUNKS * (n + 1))
        pack(out_ref, l_scr, 0, rows)
        pack(out_ref, r_scr, 1, rows)
        copies.append(pltpu.make_async_copy(out_ref.at[rows], out_hbm.at[rows], out_sems.at[n]))
        copies[-1].start()
    for copy in copies:
        copy.wait()


def edges(pair, w_in, gain_in, bias_in):
    return pl.pallas_call(
        edges_kernel,
        out_shape=message((CH,), 2),
        in_specs=in_hbm(4),
        out_specs=pl.BlockSpec(memory_space=pltpu.HBM),
        scratch_shapes=[
            pltpu.VMEM((TILE, TILE, CH), BF),
            pltpu.VMEM((CH, 5 * CH), BF),
            pltpu.VMEM((1, CH), F32),
            pltpu.VMEM((1, CH), F32),
            pltpu.VMEM((GROUPS, LANES, CH), F32),
            PADDED,
            PADDED,
            pltpu.VMEM((4 * CH, CH), BF),
            pltpu.VMEM((CH, PART, 2 * PARTS * LANES), BF),
            pltpu.SemaphoreType.DMA((4,)),
            pltpu.SemaphoreType.DMA((CHUNKS,)),
        ],
        compiler_params=params(),
        cost_estimate=pl.CostEstimate(flops=200_000_000, bytes_accessed=1_200_000, transcendentals=400_000),
        name="edges",
    )(*keep_in_hbm(pair, w_in, gain_in, bias_in))


def side_kernel(
    pair_hbm, cot_hbm, w_hbm, w_out_hbm, gain_hbm, bias_hbm, gain_out_hbm, bias_out_hbm,
    gate_ref, slope_ref, dx_ref, fac_ref, xhat_ref, scale_ref, cols_ref, w_ref, w_out_t_ref,
    pair_ref, cot_ref, w_out_ref, rows_ref, x_scr, c_scr, wt_scr, sems,
):
    copies = fetch(
        (pair_hbm, cot_hbm, w_hbm, w_out_hbm, gain_hbm, bias_hbm, gain_out_hbm, bias_out_hbm),
        (pair_ref, cot_ref, w_ref, w_out_ref) + tuple(rows_ref.at[n] for n in range(4)),
        sems,
    )
    x_scr[...] = jnp.zeros(x_scr.shape, F32)
    c_scr[...] = jnp.zeros(c_scr.shape, F32)
    scale_ref[...] = jnp.zeros(scale_ref.shape, F32)
    cols_ref[...] = jnp.zeros(cols_ref.shape, F32)
    for copy in copies:
        copy.wait()
    wt_scr[...] = w_ref[...].astype(F32).T.astype(BF)
    w_out_t_ref[...] = w_out_ref[...].astype(F32).T.astype(BF)
    gain_in, bias_in, gain_out, bias_out = (column(rows_ref[n]) for n in range(4))
    cols_ref[:, 0:1] = gain_in
    cols_ref[:, 1:2] = gain_out
    cols_ref[:, 2:3] = bias_out
    spread_tile(pair_ref, x_scr)
    spread_tile(cot_ref, c_scr)
    for r in range(GROUPS):
        xhat, scale = normalized(x_scr[r].T, 0)
        normed = (xhat * gain_in + bias_in).astype(BF)
        xhat_ref[r] = xhat
        scale_ref[r : r + 1, :] = scale
        proj = dot(wt_scr[...], normed, 1, 0)
        for h in range(2):
            sig = jax.nn.sigmoid(proj[2 * h * CH : (2 * h + 1) * CH])
            value = proj[(2 * h + 1) * CH : (2 * h + 2) * CH]
            fac_ref[r, 2 * h * CH : (2 * h + 1) * CH, :] = (value * sig * (1.0 - sig)).astype(BF)
            fac_ref[r, (2 * h + 1) * CH : (2 * h + 2) * CH, :] = sig.astype(BF)
        gate = jax.nn.sigmoid(proj[4 * CH :])
        gated = c_scr[r].T * gate
        gate_ref[r] = gate
        slope_ref[r] = gated * (1.0 - gate)
        dx_ref[r] = dot(w_out_ref[...], gated.astype(BF), 1, 0) * gain_out


def side(pair, cotangent, w_in, w_out, gain_in, bias_in, gain_out, bias_out):
    square = jax.ShapeDtypeStruct((GROUPS, CH, LANES), F32)
    return pl.pallas_call(
        side_kernel,
        out_shape=[
            square,
            square,
            square,
            jax.ShapeDtypeStruct((GROUPS, 4 * CH, LANES), BF),
            square,
            jax.ShapeDtypeStruct((ROWS, LANES), F32),
            jax.ShapeDtypeStruct((CH, LANES), F32),
            jax.ShapeDtypeStruct((CH, 5 * CH), BF),
            jax.ShapeDtypeStruct((CH, CH), BF),
        ],
        in_specs=in_hbm(8),
        scratch_shapes=[
            pltpu.VMEM((TILE, TILE, CH), BF),
            pltpu.VMEM((TILE, TILE, CH), BF),
            pltpu.VMEM((CH, CH), BF),
            pltpu.VMEM((4, 1, CH), F32),
            pltpu.VMEM((GROUPS, LANES, CH), F32),
            pltpu.VMEM((GROUPS, LANES, CH), F32),
            pltpu.VMEM((5 * CH, CH), BF),
            pltpu.SemaphoreType.DMA((8,)),
        ],
        compiler_params=params(),
        cost_estimate=pl.CostEstimate(flops=300_000_000, bytes_accessed=6_000_000, transcendentals=600_000),
        name="side",
    )(*keep_in_hbm(pair, cotangent, w_in, w_out, gain_in, bias_in, gain_out, bias_out))


def assemble_left_kernel(in_ref, left_ref, t_scr):
    read_rows(in_ref, t_scr)
    for g in range(KG):
        blocks = [
            t_scr[column_block(SLOTS * g + q)].astype(F32).reshape(CH, LANES) if SLOTS * g + q < KB else None
            for q in range(SLOTS)
        ]
        for s, value in enumerate(swap_slots(blocks)):
            left_ref[CH * s : CH * (s + 1), part_lanes(g)] = value.astype(BF)


def assemble_left(received):
    return pl.pallas_call(
        assemble_left_kernel,
        out_shape=jax.ShapeDtypeStruct((SLOTS * NB * ROWS, KG * LANES), BF),
        scratch_shapes=[pltpu.VMEM(BLOCKS + (ROWS, LANES), BF)],
        compiler_params=params(),
        cost_estimate=pl.CostEstimate(flops=2_000_000, bytes_accessed=1_000_000, transcendentals=0),
        name="assemble_left",
    )(received.reshape(BLOCKS + (PART, 2 * PARTS * LANES)))


def assemble_right_kernel(in_ref, right_ref, t_scr, v_scr, r_scr):
    read_rows(in_ref, t_scr, 1)
    r_scr[...] = jnp.zeros(r_scr.shape, F32)
    for g in range(KG):
        blocks = [
            t_scr[column_block(SLOTS * g + q)].astype(F32).reshape(CH, LANES) if SLOTS * g + q < KB else None
            for q in range(SLOTS)
        ]
        for s, value in enumerate(swap_slots(blocks)):
            v_scr[s] = value
            for b in range(NB):
                to = LANES * (b // SLOTS) + SLOT * (b % SLOTS) + GROUPS * s
                r_scr[to : to + GROUPS, part_lanes(g)] = v_scr[s, ROWS * b : ROWS * b + GROUPS]
    right_ref[...] = r_scr[...].astype(BF)


def assemble_right(received):
    return pl.pallas_call(
        assemble_right_kernel,
        out_shape=jax.ShapeDtypeStruct((JG * LANES, KG * LANES), BF),
        scratch_shapes=[
            pltpu.VMEM(BLOCKS + (ROWS, LANES), BF),
            pltpu.VMEM((SLOTS, CH, LANES), F32),
            pltpu.VMEM((JG * LANES, KG * LANES), F32),
        ],
        compiler_params=params(),
        cost_estimate=pl.CostEstimate(flops=2_000_000, bytes_accessed=1_000_000, transcendentals=0),
        name="assemble_right",
    )(received.reshape(BLOCKS + (PART, 2 * PARTS * LANES)))


def product_messages(left_ref, right_ref, out_ref, place, t_scr):
    prod = dot(left_ref[...], right_ref[...], 1, 1)
    for g in range(JG):
        blocks = [prod[CH * s : CH * (s + 1), part_lanes(g)] for s in range(SLOTS)]
        for q, value in enumerate(swap_slots(blocks)):
            b = SLOTS * g + q
            if b < NB:
                write_rows(out_ref, place(b), value, t_scr)


def products_own_kernel(left_ref, right_ref, out_ref, t_scr):
    product_messages(left_ref, right_ref, out_ref, lambda b: b, t_scr)


def products_own(left, right):
    return pl.pallas_call(
        products_own_kernel,
        out_shape=message((NB, NB)),
        scratch_shapes=[pltpu.VMEM((NB, ROWS, LANES), BF)],
        compiler_params=params(),
        cost_estimate=pl.CostEstimate(flops=230_000_000, bytes_accessed=1_400_000, transcendentals=0),
        name="products_own",
    )(left, right)


def products_kernel(core_ref, left_ref, right_ref, own_ref, out_ref, t_scr):
    core = core_ref[0]
    for b in range(NB):
        out_ref[column_block(2 * b, core)] = by_block(own_ref[:, b])
    product_messages(left_ref, right_ref, out_ref, lambda b: column_block(2 * b, 1 - core), t_scr)


def products(core, left, other, own):
    return pl.pallas_call(
        products_kernel,
        out_shape=message(BLOCKS),
        in_specs=[pl.BlockSpec(memory_space=pltpu.SMEM)] + [pl.BlockSpec(memory_space=pltpu.VMEM)] * 3,
        scratch_shapes=[pltpu.VMEM((NB, ROWS, LANES), BF)],
        compiler_params=params(),
        cost_estimate=pl.CostEstimate(flops=230_000_000, bytes_accessed=1_600_000, transcendentals=0),
        name="products",
    )(core, left, other, own).reshape(CH, PART, PARTS * LANES)


def middle_kernel(
    prod_ref, gate_ref, slope_ref, dx_ref, cols_ref, w_ref,
    update_ref, out_ref, dgate_ref, p_scr, o_scr,
):
    unpack(prod_ref, p_scr)
    used = used_lanes((CH, LANES))
    gain, bias = cols_ref[:, 1:2], cols_ref[:, 2:3]
    for r in range(GROUPS):
        xhat, scale = normalized(by_row(p_scr)[row_at(r), :], 0)
        prodn = (xhat * gain + bias).astype(BF)
        mixed = dot(w_ref[...], prodn, 1, 0)
        gather_tile((gate_ref[r] * mixed).T, update_ref, r)
        dgate_ref[r] = (slope_ref[r] * mixed).astype(BF)
        d_prod = norm_grad(dx_ref[r], xhat, scale, 0)
        by_row(o_scr)[row_at(r), :] = jnp.where(used, d_prod, 0.0)
    pack(out_ref, o_scr)


def middle(prod, gate, slope, dx, cols, w_out_t):
    return pl.pallas_call(
        middle_kernel,
        out_shape=[
            pltpu.VMEM((TILE, TILE, CH), BF),
            message((CH,)),
            jax.ShapeDtypeStruct((GROUPS, CH, LANES), BF),
        ],
        scratch_shapes=[PADDED, PADDED],
        compiler_params=params(),
        cost_estimate=pl.CostEstimate(flops=50_000_000, bytes_accessed=4_000_000, transcendentals=10_000),
        name="middle",
    )(prod, gate, slope, dx, cols, w_out_t)


def regroup_kernel(core_ref, in_ref, keep_ref, send_ref, t_scr):
    core = core_ref[0]
    read_rows(in_ref, t_scr)
    for t, to_ref in enumerate((send_ref, keep_ref)):
        parity = 1 - core if t == 0 else core
        for g in range(JG):
            blocks = [
                t_scr[column_block(2 * (SLOTS * g + q), parity)].astype(F32).reshape(CH, LANES)
                if SLOTS * g + q < NB
                else None
                for q in range(SLOTS)
            ]
            for s, value in enumerate(swap_slots(blocks)):
                to_ref[CH * s : CH * (s + 1), part_lanes(g)] = value.astype(BF)


def regroup(core, received):
    half = jax.ShapeDtypeStruct((SLOTS * NB * ROWS, JG * LANES), BF)
    return pl.pallas_call(
        regroup_kernel,
        out_shape=[half, half],
        in_specs=[pl.BlockSpec(memory_space=pltpu.SMEM), pl.BlockSpec(memory_space=pltpu.VMEM)],
        scratch_shapes=[pltpu.VMEM(BLOCKS + (ROWS, LANES), BF)],
        compiler_params=params(),
        cost_estimate=pl.CostEstimate(flops=2_000_000, bytes_accessed=1_000_000, transcendentals=0),
        name="regroup",
    )(core, received.reshape(BLOCKS + (PART, PARTS * LANES)))


def left_grad_kernel(
    keep_ref, send_ref, own_ref, other_ref, left_own_ref, left_hbm, out_ref, left_ref, part_ref, t_scr, sems
):
    rows = [pl.ds(CH * s, CH) for s in range(SLOTS)]
    copies = fetch([left_hbm.at[at] for at in rows], [left_ref.at[at] for at in rows], sems)
    for g in range(KG):
        lanes = part_lanes(g)
        d_left = dot(keep_ref[...], own_ref[:, lanes], 1, 0) + dot(send_ref[...], other_ref[:, lanes], 1, 0)
        for q, value in enumerate(swap_slots([d_left[CH * s : CH * (s + 1)] for s in range(SLOTS)])):
            if SLOTS * g + q < KB:
                write_rows(out_ref, column_block(SLOTS * g + q), value, t_scr)
    part_ref[...] = dot(keep_ref[...], left_own_ref[...], 0, 0)
    for copy in copies:
        copy.wait()


def left_grad(keep, send, own, other, left, left_other):
    return pl.pallas_call(
        left_grad_kernel,
        out_shape=[message(BLOCKS), jax.ShapeDtypeStruct((SLOTS * NB * ROWS, KG * LANES), BF),
            jax.ShapeDtypeStruct((JG * LANES, KG * LANES), F32),
        ],
        in_specs=[pl.BlockSpec(memory_space=pltpu.VMEM)] * 5 + in_hbm(1),
        scratch_shapes=[pltpu.VMEM((NB, ROWS, LANES), BF), pltpu.SemaphoreType.DMA((SLOTS,))],
        compiler_params=params(),
        cost_estimate=pl.CostEstimate(flops=450_000_000, bytes_accessed=2_200_000, transcendentals=0),
        name="left_grad",
    )(keep, send, own, other, left, *keep_in_hbm(left_other))


def right_grad_kernel(
    part_ref, other_ref, left_other_ref, d_left_ref, update_ref, out_ref, update_hbm, d_scr, o_scr, sem
):
    copy = pltpu.make_async_copy(update_ref, update_hbm, sem)
    copy.start()
    out_ref[:, :, :, :, :, : PARTS * LANES] = d_left_ref[...]
    d_scr[...] = part_ref[...] + dot(other_ref[...], left_other_ref[...], 0, 0)
    for g in range(KG):
        for b in range(NB):
            at = LANES * (b // SLOTS) + SLOT * (b % SLOTS)
            blocks = [d_scr[at + GROUPS * s : at + GROUPS * s + ROWS, part_lanes(g)] for s in range(SLOTS)]
            for q, value in enumerate(swap_slots(blocks)):
                if SLOTS * g + q < KB:
                    k = SLOTS * g + q
                    o_scr[b // 4, k % 4, b % 4, k // 4] = value.astype(o_scr.dtype)
    for p in range(PARTS):
        out_ref[:, :, :, :, :, part_lanes(PARTS + p)] = o_scr[:, :, :, :, PART * p : PART * (p + 1), :].astype(BF)
    copy.wait()


def right_grad(part, other, left_other, d_left, update):
    out, update = pl.pallas_call(
        right_grad_kernel,
        out_shape=[message(BLOCKS, 2), jax.ShapeDtypeStruct((TILE, TILE, CH), BF)],
        out_specs=[pl.BlockSpec(memory_space=pltpu.VMEM), pl.BlockSpec(memory_space=pltpu.HBM)],
        scratch_shapes=[
            pltpu.VMEM((JG * LANES, KG * LANES), F32),
            pltpu.VMEM(BLOCKS + (ROWS, LANES), BF),
            pltpu.SemaphoreType.DMA,
        ],
        compiler_params=params(),
        cost_estimate=pl.CostEstimate(flops=450_000_000, bytes_accessed=2_500_000, transcendentals=0),
        name="right_grad",
    )(part, other, left_other, d_left, pltpu.with_memory_space_constraint(update, pltpu.VMEM))
    return out.reshape(CH, PART, 2 * PARTS * LANES), update


def finish_kernel(
    d_ref, fac_ref, dgate_ref, xhat_ref, scale_ref, cols_ref, w_ref, out_hbm, l_scr, r_scr, out_ref, sems
):
    copies = []
    unpack(d_ref, l_scr, 0)
    unpack(d_ref, r_scr, 1)
    gain = cols_ref[:, 0:1]
    for r in range(GROUPS):
        d_left = by_row(l_scr)[row_at(r), :]
        d_right = by_row(r_scr)[row_at(r), :]
        parts = [
            (d * fac_ref[r, CH * f : CH * (f + 1), :].astype(F32)).astype(BF)
            for f, d in enumerate((d_left, d_left, d_right, d_right))
        ]
        d_proj = jnp.concatenate(parts + [dgate_ref[r]], 0)
        d_normed = dot(w_ref[...], d_proj, 1, 0).astype(BF).astype(F32)
        gather_tile(norm_grad(d_normed * gain, xhat_ref[r], scale_ref[r : r + 1, :], 0).T, out_ref, r)
        copies += send_tile(out_ref, out_hbm, r, sems)
    for copy in copies:
        copy.wait()


def finish(d_edges, fac, dgate, xhat, scale, cols, w_in):
    return pl.pallas_call(
        finish_kernel,
        out_shape=jax.ShapeDtypeStruct((TILE, TILE, CH), BF),
        out_specs=pl.BlockSpec(memory_space=pltpu.HBM),
        scratch_shapes=[
            PADDED,
            PADDED,
            pltpu.VMEM((TILE, TILE, CH), BF),
            pltpu.SemaphoreType.DMA((TILE // PART,)),
        ],
        compiler_params=params(),
        cost_estimate=pl.CostEstimate(flops=250_000_000, bytes_accessed=4_000_000, transcendentals=0),
        name="finish",
    )(d_edges, fac, dgate, xhat, scale, cols, w_in)


def exchange(x):
    return lax.all_to_all(x, WIDE, 0, 0, tiled=True)


def other_core(x):
    return lax.ppermute(x, "core", [(0, 1), (1, 0)])


def shards(pair, cotangent, gain_in, bias_in, w_in, gain_out, bias_out, w_out):
    gain_in, bias_in = gain_in.reshape(1, CH), bias_in.reshape(1, CH)
    gain_out, bias_out = gain_out.reshape(1, CH), bias_out.reshape(1, CH)
    core = lax.axis_index("core").astype(jnp.int32).reshape(1)
    received = exchange(edges(pair, w_in, gain_in, bias_in))
    ready = side(pair, cotangent, w_in, w_out, gain_in, bias_in, gain_out, bias_out)
    received, ready = lax.optimization_barrier((received, ready))
    gate, slope, dx, fac, xhat, scale, cols, w_in, w_out_t = ready
    right = assemble_right(received)
    right_other = other_core(right)
    left = assemble_left(received)
    left_other = other_core(left)
    prod = products(core, left, right_other, products_own(left, right))
    prod, left_other = lax.optimization_barrier((prod, left_other))
    update, d_prod, dgate = middle(exchange(prod), gate, slope, dx, cols, w_out_t)
    keep, send = regroup(core, exchange(d_prod))
    sent = other_core(send)
    d_left, left_other, part = left_grad(keep, send, right, right_other, left, left_other)
    d_edges, update = right_grad(part, sent, left_other, d_left, update)
    d_edges = exchange(d_edges)
    grad = finish(d_edges, fac, dgate, xhat, scale, cols, w_in)
    return update, grad


def solution(mesh):
    split = Mesh(mesh.devices.reshape(2, 4, 2, 4, 4), NAMES)
    tile = P(("zh", "x", "core"), ("y", "zl"), None)
    return jax.shard_map(
        shards,
        mesh=split,
        in_specs=(tile, tile, P(), P(), P(), P(), P(), P()),
        out_specs=(tile, tile),
        check_vma=False,
    )
```

```python
import jax
import jax.numpy as jnp
from jax import lax
from jax.experimental import pallas as pl
from jax.experimental.pallas import tpu as pltpu
from jax.sharding import Mesh, PartitionSpec as P

EPS = 1e-05
BF = jnp.bfloat16
F32 = jnp.float32

TILE = 36
SLOT = 40
SLOTS = 3
GROUPS = 12
LANES = 128
ROWS = 16
PART = 4
PARTS = GROUPS // PART
CH = 128
NB = 8
KB = 16
KG = 6
JG = 3
CHUNKS = 4
NAMES = ("zh", "x", "core", "y", "zl")
WIDE = ("zh", "zl", "x", "y")
BLOCKS = (2, 4, 4, 4)


def params(mib=14):
    return pltpu.CompilerParams(vmem_limit_bytes=mib * 1024 * 1024)


def dot(a, b, ca, cb):
    return lax.dot_general(a, b, (((ca,), (cb,)), ((), ())), preferred_element_type=F32)


def used_lanes(shape):
    lane = lax.broadcasted_iota(jnp.int32, shape, len(shape) - 1)
    used = lane < TILE
    for s in range(1, SLOTS):
        used = used | ((lane >= SLOT * s) & (lane < SLOT * s + TILE))
    return used


def swap_slots(blocks):
    shape = next(b.shape for b in blocks if b is not None)
    lane = lax.broadcasted_iota(jnp.int32, shape, 1)
    out = []
    for s in range(SLOTS):
        acc = jnp.zeros(shape, F32)
        for q, b in enumerate(blocks):
            if b is None:
                continue
            shift = (SLOT * (q - s)) % LANES
            moved = pltpu.roll(b, shift, 1) if shift else b
            acc = jnp.where((lane >= SLOT * q) & (lane < SLOT * (q + 1)), moved, acc)
        out.append(acc)
    return out


def spread_tile(tile_ref, scr):
    for r in range(GROUPS):
        for s in range(SLOTS):
            scr[r, SLOT * s : SLOT * s + TILE, :] = tile_ref[r + GROUPS * s].astype(F32)


def gather_tile(value, tile_ref, r):
    for s in range(SLOTS):
        tile_ref[r + GROUPS * s] = value[SLOT * s : SLOT * s + TILE].astype(BF)


def send_tile(tile_ref, tile_hbm, r, sems):
    if r % PART < PART - 1:
        return []
    copies = []
    for s in range(SLOTS):
        rows = pl.ds(r + 1 - PART + GROUPS * s, PART)
        copies.append(pltpu.make_async_copy(tile_ref.at[rows], tile_hbm.at[rows], sems.at[r // PART * SLOTS + s]))
        copies[-1].start()
    return copies


def normalized(x, axis):
    center = x - jnp.mean(x, axis, keepdims=True)
    scale = lax.rsqrt(jnp.mean(center * center, axis, keepdims=True) + EPS)
    return center * scale, scale


def norm_grad(d, xhat, scale, axis):
    return scale * (d - jnp.mean(d, axis, keepdims=True) - xhat * jnp.mean(d * xhat, axis, keepdims=True))


def message(leading, arrays=1):
    return jax.ShapeDtypeStruct(leading + (PART, arrays * PARTS * LANES), BF)


def part_lanes(p):
    return slice(LANES * p, LANES * (p + 1))


def row_at(r):
    return pl.ds(r // PART * CH * 8 + r % PART, CH, stride=8)


def by_row(scr):
    return scr.reshape(PARTS * CH * 8, LANES)


PADDED = pltpu.VMEM((PARTS, CH, 8, LANES), F32)


def pack(out_ref, scr, array=0, rows=slice(None)):
    for p in range(PARTS):
        out_ref[rows, :, part_lanes(array * PARTS + p)] = scr[p, rows, :PART, :].astype(BF)


def unpack(in_ref, scr, array=0):
    for p in range(PARTS):
        scr[p, :, :PART, :] = in_ref[:, :, part_lanes(array * PARTS + p)].astype(F32)


def read_rows(in_ref, scr, array=0):
    scr[:, :, :, :, GROUPS:, :] = jnp.zeros(BLOCKS + (ROWS - GROUPS, LANES), scr.dtype)
    for p in range(PARTS):
        part = in_ref[:, :, :, :, :, part_lanes(array * PARTS + p)]
        scr[:, :, :, :, PART * p : PART * (p + 1), :] = part.astype(scr.dtype)


def write_rows(out_ref, at, value, scr):
    scr[...] = value.astype(scr.dtype).reshape(NB, ROWS, LANES)
    for p in range(PARTS):
        part = scr[:, PART * p : PART * (p + 1), :].astype(BF)
        if isinstance(at, tuple):
            out_ref[(*at, slice(None), part_lanes(p))] = by_block(part)
        else:
            out_ref[:, at, :, part_lanes(p)] = part


def column_block(k, parity=0):
    return (slice(None), k % 4 + parity, slice(None), k // 4)


def by_block(value):
    return value.reshape(BLOCKS[0], BLOCKS[2], *value.shape[1:])


def column(row):
    return jnp.broadcast_to(row, (8, CH)).T[:, :1]


def fetch(sources, buffers, sems):
    copies = [pltpu.make_async_copy(s, b, sems.at[n]) for n, (s, b) in enumerate(zip(sources, buffers))]
    for copy in copies:
        copy.start()
    return copies


def in_hbm(n):
    return [pl.BlockSpec(memory_space=pltpu.HBM)] * n


def keep_in_hbm(*arrays):
    return [pltpu.with_memory_space_constraint(a, pltpu.HBM) for a in arrays]


def edges_kernel(
    pair_hbm, w_hbm, gain_hbm, bias_hbm, out_hbm,
    pair_ref, w_ref, gain_ref, bias_ref, x_scr, l_scr, r_scr, wt_scr, out_ref, sems, out_sems,
):
    copies = fetch(
        (pair_hbm, w_hbm, gain_hbm, bias_hbm), (pair_ref, w_ref, gain_ref, bias_ref), sems
    )
    x_scr[...] = jnp.zeros(x_scr.shape, F32)
    used = used_lanes((CH, LANES))
    copies[1].wait()
    wt_scr[...] = w_ref[:, : 4 * CH].astype(F32).T.astype(BF)
    copies[2].wait()
    copies[3].wait()
    gain, bias = column(gain_ref[...]), column(bias_ref[...])
    copies[0].wait()
    spread_tile(pair_ref, x_scr)
    for r in range(0, GROUPS, 2):
        xhat, _ = normalized(jnp.concatenate([x_scr[r].T, x_scr[r + 1].T], 1), 0)
        normed = (xhat * gain + bias).astype(BF)
        proj = dot(wt_scr[...], normed, 1, 0)
        left = jax.nn.sigmoid(proj[:CH]) * proj[CH : 2 * CH]
        right = jax.nn.sigmoid(proj[2 * CH : 3 * CH]) * proj[3 * CH :]
        for n in (r, r + 1):
            by_row(l_scr)[row_at(n), :] = jnp.where(used, left[:, part_lanes(n - r)], 0.0)
            by_row(r_scr)[row_at(n), :] = jnp.where(used, right[:, part_lanes(n - r)], 0.0)
    copies = []
    for n in range(CHUNKS):
        rows = slice(CH // CHUNKS * n, CH // CHUNKS * (n + 1))
        pack(out_ref, l_scr, 0, rows)
        pack(out_ref, r_scr, 1, rows)
        copies.append(pltpu.make_async_copy(out_ref.at[rows], out_hbm.at[rows], out_sems.at[n]))
        copies[-1].start()
    for copy in copies:
        copy.wait()


def edges(pair, w_in, gain_in, bias_in):
    return pl.pallas_call(
        edges_kernel,
        out_shape=message((CH,), 2),
        in_specs=in_hbm(4),
        out_specs=pl.BlockSpec(memory_space=pltpu.HBM),
        scratch_shapes=[
            pltpu.VMEM((TILE, TILE, CH), BF),
            pltpu.VMEM((CH, 5 * CH), BF),
            pltpu.VMEM((1, CH), F32),
            pltpu.VMEM((1, CH), F32),
            pltpu.VMEM((GROUPS, LANES, CH), F32),
            PADDED,
            PADDED,
            pltpu.VMEM((4 * CH, CH), BF),
            pltpu.VMEM((CH, PART, 2 * PARTS * LANES), BF),
            pltpu.SemaphoreType.DMA((4,)),
            pltpu.SemaphoreType.DMA((CHUNKS,)),
        ],
        compiler_params=params(),
        cost_estimate=pl.CostEstimate(flops=200_000_000, bytes_accessed=1_200_000, transcendentals=400_000),
        name="edges",
    )(*keep_in_hbm(pair, w_in, gain_in, bias_in))


def side_kernel(
    pair_hbm, cot_hbm, w_hbm, w_out_hbm, gain_hbm, bias_hbm, gain_out_hbm, bias_out_hbm,
    gate_ref, slope_ref, dx_ref, fac_ref, xhat_ref, scale_ref, cols_ref, w_ref, w_out_t_ref,
    pair_ref, cot_ref, w_out_ref, rows_ref, x_scr, c_scr, wt_scr, sems,
):
    copies = fetch(
        (pair_hbm, cot_hbm, w_hbm, w_out_hbm, gain_hbm, bias_hbm, gain_out_hbm, bias_out_hbm),
        (pair_ref, cot_ref, w_ref, w_out_ref) + tuple(rows_ref.at[n] for n in range(4)),
        sems,
    )
    x_scr[...] = jnp.zeros(x_scr.shape, F32)
    c_scr[...] = jnp.zeros(c_scr.shape, F32)
    scale_ref[...] = jnp.zeros(scale_ref.shape, F32)
    cols_ref[...] = jnp.zeros(cols_ref.shape, F32)
    for copy in copies:
        copy.wait()
    wt_scr[...] = w_ref[...].astype(F32).T.astype(BF)
    w_out_t_ref[...] = w_out_ref[...].astype(F32).T.astype(BF)
    gain_in, bias_in, gain_out, bias_out = (column(rows_ref[n]) for n in range(4))
    cols_ref[:, 0:1] = gain_in
    cols_ref[:, 1:2] = gain_out
    cols_ref[:, 2:3] = bias_out
    spread_tile(pair_ref, x_scr)
    spread_tile(cot_ref, c_scr)
    for r in range(GROUPS):
        xhat, scale = normalized(x_scr[r].T, 0)
        normed = (xhat * gain_in + bias_in).astype(BF)
        xhat_ref[r] = xhat
        scale_ref[r : r + 1, :] = scale
        proj = dot(wt_scr[...], normed, 1, 0)
        for h in range(2):
            sig = jax.nn.sigmoid(proj[2 * h * CH : (2 * h + 1) * CH])
            value = proj[(2 * h + 1) * CH : (2 * h + 2) * CH]
            fac_ref[r, 2 * h * CH : (2 * h + 1) * CH, :] = (value * sig * (1.0 - sig)).astype(BF)
            fac_ref[r, (2 * h + 1) * CH : (2 * h + 2) * CH, :] = sig.astype(BF)
        gate = jax.nn.sigmoid(proj[4 * CH :])
        gated = c_scr[r].T * gate
        gate_ref[r] = gate
        slope_ref[r] = gated * (1.0 - gate)
        dx_ref[r] = dot(w_out_ref[...], gated.astype(BF), 1, 0) * gain_out


def side(pair, cotangent, w_in, w_out, gain_in, bias_in, gain_out, bias_out):
    square = jax.ShapeDtypeStruct((GROUPS, CH, LANES), F32)
    return pl.pallas_call(
        side_kernel,
        out_shape=[
            square,
            square,
            square,
            jax.ShapeDtypeStruct((GROUPS, 4 * CH, LANES), BF),
            square,
            jax.ShapeDtypeStruct((ROWS, LANES), F32),
            jax.ShapeDtypeStruct((CH, LANES), F32),
            jax.ShapeDtypeStruct((CH, 5 * CH), BF),
            jax.ShapeDtypeStruct((CH, CH), BF),
        ],
        in_specs=in_hbm(8),
        scratch_shapes=[
            pltpu.VMEM((TILE, TILE, CH), BF),
            pltpu.VMEM((TILE, TILE, CH), BF),
            pltpu.VMEM((CH, CH), BF),
            pltpu.VMEM((4, 1, CH), F32),
            pltpu.VMEM((GROUPS, LANES, CH), F32),
            pltpu.VMEM((GROUPS, LANES, CH), F32),
            pltpu.VMEM((5 * CH, CH), BF),
            pltpu.SemaphoreType.DMA((8,)),
        ],
        compiler_params=params(),
        cost_estimate=pl.CostEstimate(flops=300_000_000, bytes_accessed=6_000_000, transcendentals=600_000),
        name="side",
    )(*keep_in_hbm(pair, cotangent, w_in, w_out, gain_in, bias_in, gain_out, bias_out))


def assemble_left_kernel(in_ref, left_ref, t_scr):
    read_rows(in_ref, t_scr)
    for g in range(KG):
        blocks = [
            t_scr[column_block(SLOTS * g + q)].astype(F32).reshape(CH, LANES) if SLOTS * g + q < KB else None
            for q in range(SLOTS)
        ]
        for s, value in enumerate(swap_slots(blocks)):
            left_ref[CH * s : CH * (s + 1), part_lanes(g)] = value.astype(BF)


def assemble_left(received):
    return pl.pallas_call(
        assemble_left_kernel,
        out_shape=jax.ShapeDtypeStruct((SLOTS * NB * ROWS, KG * LANES), BF),
        scratch_shapes=[pltpu.VMEM(BLOCKS + (ROWS, LANES), BF)],
        compiler_params=params(),
        cost_estimate=pl.CostEstimate(flops=2_000_000, bytes_accessed=1_000_000, transcendentals=0),
        name="assemble_left",
    )(received.reshape(BLOCKS + (PART, 2 * PARTS * LANES)))


def assemble_right_kernel(in_ref, right_ref, t_scr, v_scr, r_scr):
    read_rows(in_ref, t_scr, 1)
    r_scr[...] = jnp.zeros(r_scr.shape, F32)
    for g in range(KG):
        blocks = [
            t_scr[column_block(SLOTS * g + q)].astype(F32).reshape(CH, LANES) if SLOTS * g + q < KB else None
            for q in range(SLOTS)
        ]
        for s, value in enumerate(swap_slots(blocks)):
            v_scr[s] = value
            for b in range(NB):
                to = LANES * (b // SLOTS) + SLOT * (b % SLOTS) + GROUPS * s
                r_scr[to : to + GROUPS, part_lanes(g)] = v_scr[s, ROWS * b : ROWS * b + GROUPS]
    right_ref[...] = r_scr[...].astype(BF)


def assemble_right(received):
    return pl.pallas_call(
        assemble_right_kernel,
        out_shape=jax.ShapeDtypeStruct((JG * LANES, KG * LANES), BF),
        scratch_shapes=[
            pltpu.VMEM(BLOCKS + (ROWS, LANES), BF),
            pltpu.VMEM((SLOTS, CH, LANES), F32),
            pltpu.VMEM((JG * LANES, KG * LANES), F32),
        ],
        compiler_params=params(),
        cost_estimate=pl.CostEstimate(flops=2_000_000, bytes_accessed=1_000_000, transcendentals=0),
        name="assemble_right",
    )(received.reshape(BLOCKS + (PART, 2 * PARTS * LANES)))


def product_messages(left_ref, right_ref, out_ref, place, t_scr):
    prod = dot(left_ref[...], right_ref[...], 1, 1)
    for g in range(JG):
        blocks = [prod[CH * s : CH * (s + 1), part_lanes(g)] for s in range(SLOTS)]
        for q, value in enumerate(swap_slots(blocks)):
            b = SLOTS * g + q
            if b < NB:
                write_rows(out_ref, place(b), value, t_scr)


def products_own_kernel(left_ref, right_ref, out_ref, t_scr):
    product_messages(left_ref, right_ref, out_ref, lambda b: b, t_scr)


def products_own(left, right):
    return pl.pallas_call(
        products_own_kernel,
        out_shape=message((NB, NB)),
        scratch_shapes=[pltpu.VMEM((NB, ROWS, LANES), BF)],
        compiler_params=params(),
        cost_estimate=pl.CostEstimate(flops=230_000_000, bytes_accessed=1_400_000, transcendentals=0),
        name="products_own",
    )(left, right)


def products_kernel(core_ref, left_ref, right_ref, own_ref, out_ref, t_scr):
    core = core_ref[0]
    for b in range(NB):
        out_ref[column_block(2 * b, core)] = by_block(own_ref[:, b])
    product_messages(left_ref, right_ref, out_ref, lambda b: column_block(2 * b, 1 - core), t_scr)


def products(core, left, other, own):
    return pl.pallas_call(
        products_kernel,
        out_shape=message(BLOCKS),
        in_specs=[pl.BlockSpec(memory_space=pltpu.SMEM)] + [pl.BlockSpec(memory_space=pltpu.VMEM)] * 3,
        scratch_shapes=[pltpu.VMEM((NB, ROWS, LANES), BF)],
        compiler_params=params(),
        cost_estimate=pl.CostEstimate(flops=230_000_000, bytes_accessed=1_600_000, transcendentals=0),
        name="products",
    )(core, left, other, own).reshape(CH, PART, PARTS * LANES)


def middle_kernel(
    prod_ref, gate_ref, slope_ref, dx_ref, cols_ref, w_ref,
    update_ref, out_ref, dgate_ref, p_scr, o_scr,
):
    unpack(prod_ref, p_scr)
    used = used_lanes((CH, LANES))
    gain, bias = cols_ref[:, 1:2], cols_ref[:, 2:3]
    for r in range(GROUPS):
        xhat, scale = normalized(by_row(p_scr)[row_at(r), :], 0)
        prodn = (xhat * gain + bias).astype(BF)
        mixed = dot(w_ref[...], prodn, 1, 0)
        gather_tile((gate_ref[r] * mixed).T, update_ref, r)
        dgate_ref[r] = (slope_ref[r] * mixed).astype(BF)
        d_prod = norm_grad(dx_ref[r], xhat, scale, 0)
        by_row(o_scr)[row_at(r), :] = jnp.where(used, d_prod, 0.0)
    pack(out_ref, o_scr)


def middle(prod, gate, slope, dx, cols, w_out_t):
    return pl.pallas_call(
        middle_kernel,
        out_shape=[
            pltpu.VMEM((TILE, TILE, CH), BF),
            message((CH,)),
            jax.ShapeDtypeStruct((GROUPS, CH, LANES), BF),
        ],
        scratch_shapes=[PADDED, PADDED],
        compiler_params=params(),
        cost_estimate=pl.CostEstimate(flops=50_000_000, bytes_accessed=4_000_000, transcendentals=10_000),
        name="middle",
    )(prod, gate, slope, dx, cols, w_out_t)


def regroup_kernel(core_ref, in_ref, keep_ref, send_ref, t_scr):
    core = core_ref[0]
    read_rows(in_ref, t_scr)
    for t, to_ref in enumerate((send_ref, keep_ref)):
        parity = 1 - core if t == 0 else core
        for g in range(JG):
            blocks = [
                t_scr[column_block(2 * (SLOTS * g + q), parity)].astype(F32).reshape(CH, LANES)
                if SLOTS * g + q < NB
                else None
                for q in range(SLOTS)
            ]
            for s, value in enumerate(swap_slots(blocks)):
                to_ref[CH * s : CH * (s + 1), part_lanes(g)] = value.astype(BF)


def regroup(core, received):
    half = jax.ShapeDtypeStruct((SLOTS * NB * ROWS, JG * LANES), BF)
    return pl.pallas_call(
        regroup_kernel,
        out_shape=[half, half],
        in_specs=[pl.BlockSpec(memory_space=pltpu.SMEM), pl.BlockSpec(memory_space=pltpu.VMEM)],
        scratch_shapes=[pltpu.VMEM(BLOCKS + (ROWS, LANES), BF)],
        compiler_params=params(),
        cost_estimate=pl.CostEstimate(flops=2_000_000, bytes_accessed=1_000_000, transcendentals=0),
        name="regroup",
    )(core, received.reshape(BLOCKS + (PART, PARTS * LANES)))


def left_grad_kernel(keep_ref, send_ref, own_ref, other_ref, left_hbm, out_ref, left_ref, t_scr, sems):
    rows = [pl.ds(CH * s, CH) for s in range(SLOTS)]
    copies = fetch([left_hbm.at[at] for at in rows], [left_ref.at[at] for at in rows], sems)
    for g in range(KG):
        lanes = part_lanes(g)
        d_left = dot(keep_ref[...], own_ref[:, lanes], 1, 0) + dot(send_ref[...], other_ref[:, lanes], 1, 0)
        for q, value in enumerate(swap_slots([d_left[CH * s : CH * (s + 1)] for s in range(SLOTS)])):
            if SLOTS * g + q < KB:
                write_rows(out_ref, column_block(SLOTS * g + q), value, t_scr)
    for copy in copies:
        copy.wait()


def left_grad(keep, send, own, other, left_other):
    return pl.pallas_call(
        left_grad_kernel,
        out_shape=[message(BLOCKS), jax.ShapeDtypeStruct((SLOTS * NB * ROWS, KG * LANES), BF)],
        in_specs=[pl.BlockSpec(memory_space=pltpu.VMEM)] * 4 + in_hbm(1),
        scratch_shapes=[pltpu.VMEM((NB, ROWS, LANES), BF), pltpu.SemaphoreType.DMA((SLOTS,))],
        compiler_params=params(),
        cost_estimate=pl.CostEstimate(flops=450_000_000, bytes_accessed=2_200_000, transcendentals=0),
        name="left_grad",
    )(keep, send, own, other, *keep_in_hbm(left_other))


def right_grad_kernel(
    keep_ref, other_ref, left_ref, left_other_ref, d_left_ref, update_ref, out_ref, update_hbm, d_scr, o_scr, sem
):
    copy = pltpu.make_async_copy(update_ref, update_hbm, sem)
    copy.start()
    out_ref[:, :, :, :, :, : PARTS * LANES] = d_left_ref[...]
    d_scr[...] = dot(keep_ref[...], left_ref[...], 0, 0) + dot(other_ref[...], left_other_ref[...], 0, 0)
    for g in range(KG):
        for b in range(NB):
            at = LANES * (b // SLOTS) + SLOT * (b % SLOTS)
            blocks = [d_scr[at + GROUPS * s : at + GROUPS * s + ROWS, part_lanes(g)] for s in range(SLOTS)]
            for q, value in enumerate(swap_slots(blocks)):
                if SLOTS * g + q < KB:
                    k = SLOTS * g + q
                    o_scr[b // 4, k % 4, b % 4, k // 4] = value.astype(o_scr.dtype)
    for p in range(PARTS):
        out_ref[:, :, :, :, :, part_lanes(PARTS + p)] = o_scr[:, :, :, :, PART * p : PART * (p + 1), :].astype(BF)
    copy.wait()


def right_grad(keep, other, left, left_other, d_left, update):
    out, update = pl.pallas_call(
        right_grad_kernel,
        out_shape=[message(BLOCKS, 2), jax.ShapeDtypeStruct((TILE, TILE, CH), BF)],
        out_specs=[pl.BlockSpec(memory_space=pltpu.VMEM), pl.BlockSpec(memory_space=pltpu.HBM)],
        scratch_shapes=[
            pltpu.VMEM((JG * LANES, KG * LANES), F32),
            pltpu.VMEM(BLOCKS + (ROWS, LANES), BF),
            pltpu.SemaphoreType.DMA,
        ],
        compiler_params=params(),
        cost_estimate=pl.CostEstimate(flops=450_000_000, bytes_accessed=2_500_000, transcendentals=0),
        name="right_grad",
    )(keep, other, left, left_other, d_left, pltpu.with_memory_space_constraint(update, pltpu.VMEM))
    return out.reshape(CH, PART, 2 * PARTS * LANES), update


def finish_kernel(
    d_ref, fac_ref, dgate_ref, xhat_ref, scale_ref, cols_ref, w_ref, out_hbm, l_scr, r_scr, out_ref, sems
):
    copies = []
    unpack(d_ref, l_scr, 0)
    unpack(d_ref, r_scr, 1)
    gain = cols_ref[:, 0:1]
    for r in range(GROUPS):
        d_left = by_row(l_scr)[row_at(r), :]
        d_right = by_row(r_scr)[row_at(r), :]
        parts = [
            (d * fac_ref[r, CH * f : CH * (f + 1), :].astype(F32)).astype(BF)
            for f, d in enumerate((d_left, d_left, d_right, d_right))
        ]
        d_proj = jnp.concatenate(parts + [dgate_ref[r]], 0)
        d_normed = dot(w_ref[...], d_proj, 1, 0).astype(BF).astype(F32)
        gather_tile(norm_grad(d_normed * gain, xhat_ref[r], scale_ref[r : r + 1, :], 0).T, out_ref, r)
        copies += send_tile(out_ref, out_hbm, r, sems)
    for copy in copies:
        copy.wait()


def finish(d_edges, fac, dgate, xhat, scale, cols, w_in):
    return pl.pallas_call(
        finish_kernel,
        out_shape=jax.ShapeDtypeStruct((TILE, TILE, CH), BF),
        out_specs=pl.BlockSpec(memory_space=pltpu.HBM),
        scratch_shapes=[
            PADDED,
            PADDED,
            pltpu.VMEM((TILE, TILE, CH), BF),
            pltpu.SemaphoreType.DMA((TILE // PART,)),
        ],
        compiler_params=params(),
        cost_estimate=pl.CostEstimate(flops=250_000_000, bytes_accessed=4_000_000, transcendentals=0),
        name="finish",
    )(d_edges, fac, dgate, xhat, scale, cols, w_in)


def exchange(x):
    return lax.all_to_all(x, WIDE, 0, 0, tiled=True)


def other_core(x):
    return lax.ppermute(x, "core", [(0, 1), (1, 0)])


def shards(pair, cotangent, gain_in, bias_in, w_in, gain_out, bias_out, w_out):
    gain_in, bias_in = gain_in.reshape(1, CH), bias_in.reshape(1, CH)
    gain_out, bias_out = gain_out.reshape(1, CH), bias_out.reshape(1, CH)
    core = lax.axis_index("core").astype(jnp.int32).reshape(1)
    received = exchange(edges(pair, w_in, gain_in, bias_in))
    ready = side(pair, cotangent, w_in, w_out, gain_in, bias_in, gain_out, bias_out)
    received, ready = lax.optimization_barrier((received, ready))
    gate, slope, dx, fac, xhat, scale, cols, w_in, w_out_t = ready
    right = assemble_right(received)
    right_other = other_core(right)
    left = assemble_left(received)
    left_other = other_core(left)
    prod = products(core, left, right_other, products_own(left, right))
    prod, left_other = lax.optimization_barrier((prod, left_other))
    update, d_prod, dgate = middle(exchange(prod), gate, slope, dx, cols, w_out_t)
    keep, send = regroup(core, exchange(d_prod))
    sent = other_core(send)
    d_left, left_other = left_grad(keep, send, right, right_other, left_other)
    d_edges, update = right_grad(keep, sent, left, left_other, d_left, update)
    d_edges = exchange(d_edges)
    grad = finish(d_edges, fac, dgate, xhat, scale, cols, w_in)
    return update, grad


def solution(mesh):
    split = Mesh(mesh.devices.reshape(2, 4, 2, 4, 4), NAMES)
    tile = P(("zh", "x", "core"), ("y", "zl"), None)
    return jax.shard_map(
        shards,
        mesh=split,
        in_specs=(tile, tile, P(), P(), P(), P(), P(), P()),
        out_specs=(tile, tile),
        check_vma=False,
    )
```
